32 devices in a mesh: dp: 4 (over y, x), seq: 4 (over z), tensor: 2 (over core).
Axes of the slice: x: 2, y: 2, z: 4, core: 2. Of those that a mesh axis runs over, the one named last changes fastest.
Arguments:
- hidden_in: bfloat16 [4, 2048, 1536], P('dp', 'seq'), may hold values from -6 to 6
- lengths: int32 [4, 4], P('dp'), may hold values from 64 to 1536, as said below
- attn_gain: float32 [1536], replicated, may hold values from 0.1 to 1.9
- w_query: bfloat16 [1536, 1536], P(None, 'tensor'), may hold values from -0.21875 to 0.21875
- w_key: bfloat16 [1536, 768], P(None, 'tensor'), may hold values from -0.21875 to 0.21875
- w_value: bfloat16 [1536, 768], P(None, 'tensor'), may hold values from -0.15625 to 0.15625
- w_out: bfloat16 [1536, 1536], P('tensor'), may hold values from -1.25 to 1.25
- mlp_gain: float32 [1536], replicated, may hold values from 0.1 to 1.9
- w_gate: bfloat16 [1536, 4096], P(None, 'tensor'), may hold values from -0.15625 to 0.15625
- w_up: bfloat16 [1536, 4096], P(None, 'tensor'), may hold values from -0.15625 to 0.15625
- w_down: bfloat16 [4096, 1536], P('tensor'), may hold values from -0.09375 to 0.09375
- out_grad: bfloat16 [4, 2048, 1536], P('dp', 'seq'), may hold values from -6 to 6
Outputs:
- output: bfloat16 [4, 2048, 1536], P('dp', 'seq')
- grad_input: bfloat16 [4, 2048, 1536], P('dp', 'seq')
- grad_attn_gain: float32 [1536], P(('dp', 'seq'))
- grad_w_query: float32 [1536, 1536], P(('dp', 'seq'), 'tensor')
- grad_w_key: float32 [1536, 768], P(('dp', 'seq'), 'tensor')
- grad_w_value: float32 [1536, 768], P(('dp', 'seq'), 'tensor')
- grad_w_out: float32 [1536, 1536], P('tensor', ('dp', 'seq'))
- grad_mlp_gain: float32 [1536], P(('dp', 'seq'))
- grad_w_gate: float32 [1536, 4096], P(('dp', 'seq'), 'tensor')
- grad_w_up: float32 [1536, 4096], P(('dp', 'seq'), 'tensor')
- grad_w_down: float32 [4096, 1536], P('tensor', ('dp', 'seq'))
The draws below stay inside these ranges and needn't reach their ends.
Inputs may be any that keep to these rules, and one draw needn't show every extreme that they name: Each row holds the lengths of the 4 documents packed into one sequence, in order; their sum is less than 2048, and the positions after the last document are padding.
All inputs are finite; a program needn't handle non-finite values.
Results may differ from the reference program's by a relative error of at most 0.019.
Values may be sent and summed in bfloat16 or wider, within the bound.
A program may use at most 256 MiB of HBM per device.

```python
import jax
import jax.numpy as jnp
from jax import lax

D = 1536
HQ = 16
KV = 8
HD = 96
FF = 4096
SEQ_LEN = 2048
TOK_DEV = 512
SEQS = 4


def draw_lengths(key, part):
    key = jax.random.fold_in(key, 17)
    split_keys = jax.random.split(key, 4)
    leading = jax.random.randint(split_keys[0], (SEQS,), TOK_DEV // 4, TOK_DEV // 2)
    reach = jax.random.randint(split_keys[1], (SEQS,), 1, TOK_DEV // 4)
    spanning = SEQ_LEN - TOK_DEV - leading + reach
    rest = TOK_DEV - reach
    third_doc = jax.random.randint(split_keys[2], (SEQS,), TOK_DEV // 4, TOK_DEV // 2)
    fourth_doc = jax.random.randint(split_keys[3], (SEQS,), TOK_DEV // 8, rest - third_doc)
    return jnp.stack([leading, spanning, third_doc, fourth_doc], axis=-1).astype(jnp.int32)


def levels(rng, shape, cuts, least, high):
    level = 1.0
    for dim, shards_of in cuts:
        steps = jax.random.uniform(jax.random.fold_in(jax.random.fold_in(rng, 6), dim), (shards_of,), jnp.float32, least / len(cuts), high / len(cuts))
        level = level * jnp.repeat(jnp.exp(steps), shape[dim] // shards_of).reshape((-1,) + (1,) * (len(shape) - 1 - dim))
    return level


def scatter_about(own_key, dims, spread, limit, pieces=(), held_as=jnp.bfloat16):
    values = spread * jax.random.normal(own_key, dims, jnp.float32)
    if pieces:
        values = values * levels(own_key, dims, pieces, -0.22, 0.18)
    return jnp.clip(values, -limit, limit).astype(held_as)


def setup_inputs(seed: int = 0) -> dict:
    key_of = jax.random.split(jax.random.key(seed), 13)
    hidden_in = scatter_about(key_of[0], (SEQS, SEQ_LEN, D), 1.0, 6.0, ((0, 4), (1, 4)))
    lengths = draw_lengths(jax.random.fold_in(key_of[12], 71), 0)
    attn_gain = jnp.clip(1.0 + 0.18 * jax.random.normal(key_of[2], (D,), jnp.float32), 0.1, 1.9)
    w_query = scatter_about(key_of[3], (D, HQ * HD), (D // 2) ** -0.5, 0.21875, ((1, 2),))
    w_key = scatter_about(key_of[4], (D, KV * HD), (D // 2) ** -0.5, 0.21875, ((1, 2),))
    w_value = scatter_about(key_of[5], (D, KV * HD), D ** -0.5, 0.15625, ((1, 2),))
    w_out = scatter_about(key_of[6], (HQ * HD, D), (HQ * HD // 64) ** -0.5, 1.25, ((0, 2),))
    mlp_gain = jnp.clip(1.0 + 0.18 * jax.random.normal(key_of[7], (D,), jnp.float32), 0.1, 1.9)
    w_gate = scatter_about(key_of[8], (D, FF), D ** -0.5, 0.15625, ((1, 2),))
    w_up = scatter_about(key_of[9], (D, FF), D ** -0.5, 0.15625, ((1, 2),))
    w_down = scatter_about(key_of[10], (FF, D), FF ** -0.5, 0.09375, ((0, 2),))
    out_grad = scatter_about(key_of[11], (SEQS, SEQ_LEN, D), 1.0, 6.0, ((0, 4), (1, 4)))
    return {"hidden_in": hidden_in, "lengths": lengths, "attn_gain": attn_gain, "w_query": w_query, "w_key": w_key, "w_value": w_value, "w_out": w_out, "mlp_gain": mlp_gain, "w_gate": w_gate, "w_up": w_up, "w_down": w_down, "out_grad": out_grad}


@jax.custom_vjp
def low(v):
    return lax.optimization_barrier(v.astype(jnp.bfloat16)).astype(jnp.float32)

@jax.custom_vjp
def low_back(v):
    return v

def low_keep(v):
    return (low(v), None)

def low_pass(kept, grad):
    return (grad,)

def back_keep(v):
    return (v, None)

def back_low(kept, grad):
    return (low(grad),)
low.defvjp(low_keep, low_pass)
low_back.defvjp(back_keep, back_low)
epsilon = 1e-05
rope_theta = 100000.0
masked_score = -1e+30

def doc_layout(length_row, row_count):
    positions = jnp.arange(row_count, dtype=jnp.int32)
    doc_ends = jnp.cumsum(length_row).astype(jnp.int32)
    passed = (positions[:, None] >= doc_ends[None, :]).astype(jnp.int32)
    segment = lax.optimization_barrier(jnp.sum(passed, axis=1)).astype(jnp.int32)
    doc_start = lax.optimization_barrier(jnp.sum(passed * length_row[None, :], axis=1)).astype(jnp.int32)
    return (positions, segment, positions - doc_start)

def rope_tables(offsets):
    half_size = HD // 2
    inverse = rope_theta ** (-2.0 * jnp.arange(half_size, dtype=jnp.float32) / HD)
    angles = offsets.astype(jnp.float32)[:, None] * inverse[None, :]
    return (jnp.cos(angles)[:, None, :], jnp.sin(angles)[:, None, :])

def rotate(values, cosine, sine_table):
    half_size = values.shape[-1] // 2
    first_half = values[..., :half_size]
    second_half = values[..., half_size:]
    return jnp.concatenate([first_half * cosine - second_half * sine_table, second_half * cosine + first_half * sine_table], axis=-1)

def normalize(values, gain):
    return values * lax.rsqrt(lax.optimization_barrier(jnp.mean(values * values, axis=-1, keepdims=True)) + epsilon) * gain

def matmul(left, right):
    return jnp.dot(left, right, precision=lax.Precision.HIGHEST)

def attend_block(query_block, first_row, keys, values, positions, segment, valid_flag):
    row_count = query_block.shape[0]
    query_rows = first_row + jnp.arange(row_count, dtype=jnp.int32)
    query_seg = lax.dynamic_slice_in_dim(segment, first_row, row_count, 0)
    same_doc = (query_seg[:, None] == segment[None, :]) & (positions[None, :] <= query_rows[:, None]) & valid_flag[None, :]
    allowed_mask = same_doc | (positions[None, :] == query_rows[:, None])
    raw_scores = jnp.einsum('qkgd,jkd->kgqj', query_block, keys, precision=lax.Precision.HIGHEST) * HD ** (-0.5)
    scores = jnp.where(allowed_mask[None, None], low_back(raw_scores), masked_score)
    row_max = lax.optimization_barrier(jnp.max(scores, axis=-1, keepdims=True))
    row_sum = lax.optimization_barrier(jnp.sum(jnp.exp(scores - row_max), axis=-1, keepdims=True))
    probs = low(jnp.exp(scores - (row_max + jnp.log(row_sum))))
    heads_out = jnp.einsum('kgqj,jkd->qkgd', probs, values, precision=lax.Precision.HIGHEST)
    return heads_out.reshape(row_count, HQ * HD)

def layer(inputs, weight_list, length_row):
    attn_gain, w_query, w_key, w_value, w_out, mlp_gain, w_gate, w_up, w_down = weight_list
    seq_total = inputs.shape[0]
    positions, segment, offsets = doc_layout(length_row, seq_total)
    valid_flag = segment < length_row.shape[0]
    valid_rows = valid_flag.astype(jnp.float32)[:, None]
    cosine, sine_table = rope_tables(offsets)
    attn_input = low(normalize(inputs, attn_gain))
    query_raw = low_back(matmul(attn_input, w_query)).reshape(seq_total, HQ, HD)
    key_raw = low_back(matmul(attn_input, w_key)).reshape(seq_total, KV, HD)
    values = low_back(low(matmul(attn_input, w_value))).reshape(seq_total, KV, HD)
    queries = low(rotate(query_raw, cosine, sine_table)).reshape(seq_total, KV, HQ // KV, HD)
    keys = low(rotate(key_raw, cosine, sine_table))
    block_rows = min(512, seq_total)
    attend = jax.checkpoint(attend_block)

    def one_block(block_index):
        first_row = block_index * block_rows
        query_block = lax.dynamic_slice_in_dim(queries, first_row, block_rows, 0)
        return attend(query_block, first_row, keys, values, positions, segment, valid_flag)
    blocks_out = lax.map(one_block, jnp.arange(seq_total // block_rows, dtype=jnp.int32))
    attn_heads = blocks_out.reshape(seq_total, HQ * HD)
    attn_heads = low_back(low(attn_heads * valid_rows))
    middle = inputs + low_back(matmul(attn_heads, w_out))
    mlp_input = low(normalize(middle, mlp_gain))
    gate = low_back(matmul(mlp_input, w_gate))
    upward = low_back(matmul(mlp_input, w_up))
    hidden = low(jax.nn.silu(gate) * upward)
    return middle + matmul(hidden, w_down)

def reference(hidden_in, lengths, attn_gain, w_query, w_key, w_value, w_out, mlp_gain, w_gate, w_up, w_down, out_grad):
    weights = tuple((weight.astype(jnp.float32) for weight in (attn_gain, w_query, w_key, w_value, w_out, mlp_gain, w_gate, w_up, w_down)))

    def one_sequence(totals, sequence):
        inputs_row, length_row, grad_row = sequence

        def forward(inputs_f, *weight_list):
            return layer(inputs_f, weight_list, length_row)
        result, pullback = jax.vjp(forward, inputs_row.astype(jnp.float32), *weights)
        gradients = pullback(grad_row.astype(jnp.float32))
        totals = tuple((summed + grad_one for summed, grad_one in zip(totals, gradients[1:])))
        return (totals, (result.astype(jnp.bfloat16), gradients[0].astype(jnp.bfloat16)))
    starting = tuple((jnp.zeros_like(weight) for weight in weights))
    totals, (outputs, grad_inputs) = lax.scan(one_sequence, starting, (hidden_in, lengths, out_grad))
    return (outputs, grad_inputs, totals[0], totals[1], totals[2], totals[3], totals[4], totals[5], totals[6], totals[7], totals[8])
```

```python
import jax
import jax.numpy as jnp
from jax import lax
from jax.experimental import pallas as pl
from jax.experimental.pallas import tpu as pltpu
from jax.sharding import PartitionSpec as P

HQ = 16
KV = 8
HD = 96


epsilon = 1e-05
rope_theta = 100000.0
masked_score = -1e30


def doc_layout(length_row, first_row, row_count):
    positions = first_row + jnp.arange(row_count, dtype=jnp.int32)
    doc_ends = jnp.cumsum(length_row)
    passed = (positions[:, None] >= doc_ends[None, :]).astype(jnp.int32)
    segment = jnp.sum(passed, axis=1)
    doc_start = jnp.sum(passed * length_row[None, :], axis=1)
    return (positions, segment, positions - doc_start, segment < length_row.shape[0])


def rope_tables(offsets):
    half_size = HD // 2
    inverse = rope_theta ** (-2.0 * jnp.arange(half_size, dtype=jnp.float32) / HD)
    angles = offsets.astype(jnp.float32)[:, None] * inverse[None, :]
    return (jnp.cos(angles)[:, None, :], jnp.sin(angles)[:, None, :])


def rotate(values, cosine, sine_table):
    half_size = values.shape[-1] // 2
    first_half = values[..., :half_size]
    second_half = values[..., half_size:]
    return jnp.concatenate(
        [
            first_half * cosine - second_half * sine_table,
            second_half * cosine + first_half * sine_table,
        ],
        axis=-1,
    )


def rotate_back(gradient, cosine, sine_table):
    half_size = gradient.shape[-1] // 2
    first_half = gradient[..., :half_size]
    second_half = gradient[..., half_size:]
    return jnp.concatenate(
        [
            first_half * cosine + second_half * sine_table,
            second_half * cosine - first_half * sine_table,
        ],
        axis=-1,
    )


def outer_sum(left, right):
    return lax.dot_general(
        left, right, (((0,), (0,)), ((), ())), preferred_element_type=jnp.float32
    )


def times_transpose(left, right):
    return lax.dot_general(
        left, right, (((1,), (1,)), ((), ())), preferred_element_type=jnp.float32
    )


def allowed_pairs(query_rows, query_seg, key_rows, key_seg, key_valid):
    same_doc = (
        (query_seg[:, None] == key_seg[None, :])
        & (key_rows[None, :] <= query_rows[:, None])
        & key_valid[None, :]
    )
    return same_doc | (key_rows[None, :] == query_rows[:, None])


def score_block(queries, key_part, allowed_mask):
    raw_scores = jnp.einsum("qkgd,jkd->kgqj", queries, key_part, preferred_element_type=jnp.float32)
    return jnp.where(allowed_mask[None, None], raw_scores * HD ** (-0.5), masked_score)


def backward_terms(queries, grad_heads, log_total, delta, key_part, value_part, allowed_mask):
    probs = jnp.exp(score_block(queries, key_part, allowed_mask) - log_total[..., None])
    grad_probs = jnp.einsum(
        "qkgd,jkd->kgqj", grad_heads, value_part, preferred_element_type=jnp.float32
    )
    grad_scores = (probs * (grad_probs - delta[..., None])).astype(jnp.bfloat16)
    return (probs.astype(jnp.bfloat16), grad_scores)


def block_loader(keys_all, values_all, query_info, key_info, block_rows):
    query_rows, query_seg = query_info

    def load_block(block_index):
        first_key = block_index * block_rows
        key_part = lax.dynamic_slice_in_dim(keys_all, first_key, block_rows, 0)
        value_part = lax.dynamic_slice_in_dim(values_all, first_key, block_rows, 0)
        key_rows, key_seg, key_valid = tuple(
            (lax.dynamic_slice_in_dim(member, first_key, block_rows, 0) for member in key_info)
        )
        return (
            key_part,
            value_part,
            allowed_pairs(query_rows, query_seg, key_rows, key_seg, key_valid),
        )

    return load_block


def attend_forward(queries, keys_all, values_all, query_info, key_info, block_rows):
    last_row = query_info[0][-1]
    block_count = keys_all.shape[0] // block_rows
    stat_shape = (queries.shape[1], queries.shape[2], queries.shape[0])
    load_block = block_loader(keys_all, values_all, query_info, key_info, block_rows)

    def stats_step(block_index, running):

        def stats_compute(state_in):
            row_max, row_sum = state_in
            key_part, value_part, allowed_mask = load_block(block_index)
            scores = score_block(queries, key_part, allowed_mask)
            new_max = jnp.maximum(row_max, jnp.max(scores, axis=-1))
            new_sum = row_sum * jnp.exp(row_max - new_max) + jnp.sum(
                jnp.exp(scores - new_max[..., None]), axis=-1
            )
            return (new_max, new_sum)

        return lax.cond(
            block_index * block_rows <= last_row, stats_compute, lambda state_in: state_in, running
        )

    start_stats = (
        jnp.full(stat_shape, masked_score, jnp.float32),
        jnp.zeros(stat_shape, jnp.float32),
    )
    row_max, row_sum = lax.fori_loop(0, block_count, stats_step, start_stats)
    log_total = row_max + jnp.log(row_sum)

    def output_step(block_index, running):

        def output_compute(state_in):
            kept_sum, rest_sum = state_in
            key_part, value_part, allowed_mask = load_block(block_index)
            probs = jnp.exp(score_block(queries, key_part, allowed_mask) - log_total[..., None])
            probs_low = probs.astype(jnp.bfloat16)
            rest_low = (probs - probs_low.astype(jnp.float32)).astype(jnp.bfloat16)
            kept_sum = kept_sum + jnp.einsum(
                "kgqj,jkd->qkgd", probs_low, value_part, preferred_element_type=jnp.float32
            )
            rest_sum = rest_sum + jnp.einsum(
                "kgqj,jkd->qkgd", rest_low, value_part, preferred_element_type=jnp.float32
            )
            return (kept_sum, rest_sum)

        return lax.cond(
            block_index * block_rows <= last_row, output_compute, lambda state_in: state_in, running
        )

    zero_out = jnp.zeros(queries.shape, jnp.float32)
    kept_sum, rest_sum = lax.fori_loop(0, block_count, output_step, (zero_out, zero_out))
    return (log_total, kept_sum, kept_sum + rest_sum)


def attend_backward(
    queries, grad_heads, log_total, delta, keys_all, values_all, query_info, key_info, block_rows
):
    last_row = query_info[0][-1]
    block_count = keys_all.shape[0] // block_rows
    key_width = keys_all.shape[1] * keys_all.shape[2]
    load_block = block_loader(keys_all, values_all, query_info, key_info, block_rows)

    def grad_step(running, block_index):

        def grad_compute(state_in):
            key_part, value_part, allowed_mask = load_block(block_index)
            probs_low, grad_scores = backward_terms(
                queries, grad_heads, log_total, delta, key_part, value_part, allowed_mask
            )
            grad_query = state_in + jnp.einsum(
                "kgqj,jkd->qkgd", grad_scores, key_part, preferred_element_type=jnp.float32
            )
            key_terms = ()
            grad_key = jnp.einsum(
                "kgqj,qkgd->jkd", grad_scores, queries, preferred_element_type=jnp.float32
            )
            grad_value = jnp.einsum(
                "kgqj,qkgd->jkd", probs_low, grad_heads, preferred_element_type=jnp.float32
            )
            key_terms = (
                grad_key.reshape(block_rows, key_width),
                grad_value.reshape(block_rows, key_width),
            )
            return (grad_query, key_terms)

        def skipped(state_in):
            key_terms = ()
            zero_block = jnp.zeros((block_rows, key_width), jnp.float32)
            key_terms = (zero_block, zero_block)
            return (state_in, key_terms)

        return lax.cond(block_index * block_rows <= last_row, grad_compute, skipped, running)

    grad_query, key_terms = lax.scan(
        grad_step, jnp.zeros(queries.shape, jnp.float32), jnp.arange(block_count, dtype=jnp.int32)
    )
    key_terms = tuple((member.reshape(block_count * block_rows, key_width) for member in key_terms))
    return (grad_query, key_terms)


def local(
    hidden_in,
    lengths,
    attn_gain,
    w_query,
    w_key,
    w_value,
    w_out,
    mlp_gain,
    w_gate,
    w_up,
    w_down,
    out_grad,
):
    seq_count = hidden_in.shape[0]
    tok_rows = hidden_in.shape[1]
    width = hidden_in.shape[2]
    row_total = seq_count * tok_rows
    seq_total = tok_rows * lax.axis_size("seq")
    first_row = lax.axis_index("seq") * tok_rows
    half_rows = row_total // lax.axis_size("tensor")
    half_start = lax.axis_index("tensor") * half_rows
    block_rows = min(512, seq_total)
    kv_local = w_key.shape[1] // HD
    group_size = HQ // KV
    heads_local = kv_local * group_size

    def own_half(array_in):
        return lax.dynamic_slice_in_dim(array_in, half_start, half_rows, 0)

    inputs = hidden_in.reshape(row_total, width).astype(jnp.float32)
    query_rows, query_seg, query_offsets, query_valid = jax.vmap(
        lambda length_row: doc_layout(length_row, first_row, tok_rows)
    )(lengths)
    key_layout = jax.vmap(lambda length_row: doc_layout(length_row, 0, seq_total))(lengths)
    cosine, sine_table = rope_tables(query_offsets.reshape(row_total))
    valid_rows = query_valid.reshape(row_total).astype(jnp.float32)[:, None]
    inverse_one = lax.rsqrt(jnp.mean(inputs * inputs, axis=-1, keepdims=True) + epsilon)
    normed_one = inputs * inverse_one
    attn_input = (normed_one * attn_gain).astype(jnp.bfloat16)
    query_raw = jnp.dot(attn_input, w_query, preferred_element_type=jnp.float32).reshape(
        row_total, heads_local, HD
    )
    key_raw = jnp.dot(attn_input, w_key, preferred_element_type=jnp.float32).reshape(
        row_total, kv_local, HD
    )
    values_own = (
        jnp.dot(attn_input, w_value, preferred_element_type=jnp.float32)
        .astype(jnp.bfloat16)
        .reshape(seq_count, tok_rows, kv_local * HD)
    )
    queries = (
        rotate(query_raw, cosine, sine_table)
        .astype(jnp.bfloat16)
        .reshape(seq_count, tok_rows, kv_local, group_size, HD)
    )
    keys_own = (
        rotate(key_raw, cosine, sine_table)
        .astype(jnp.bfloat16)
        .reshape(seq_count, tok_rows, kv_local * HD)
    )
    keys_all, values_all = (
        lax.all_gather(keys_own, "seq", axis=1, tiled=True),
        lax.all_gather(values_own, "seq", axis=1, tiled=True),
    )
    key_shape = (seq_count, seq_total, kv_local, HD)

    def forward_one(items):
        query_s, key_s, value_s, rows_s, seg_s, key_rows, key_seg, key_valid = items
        return attend_forward(
            query_s, key_s, value_s, (rows_s, seg_s), (key_rows, key_seg, key_valid), block_rows
        )

    log_total, kept_sum, exact_sum = lax.map(
        forward_one,
        (
            queries,
            keys_all.reshape(key_shape),
            values_all.reshape(key_shape),
            query_rows,
            query_seg,
            key_layout[0],
            key_layout[1],
            key_layout[3],
        ),
    )
    attn_heads = (kept_sum.reshape(row_total, heads_local * HD) * valid_rows).astype(jnp.bfloat16)
    attn_part = jnp.dot(attn_heads, w_out, preferred_element_type=jnp.float32)
    middle = own_half(inputs) + lax.psum_scatter(
        attn_part, "tensor", scatter_dimension=0, tiled=True
    )
    inverse_two = lax.rsqrt(jnp.mean(middle * middle, axis=-1, keepdims=True) + epsilon)
    normed_two = middle * inverse_two
    mlp_half = (normed_two * mlp_gain).astype(jnp.bfloat16)
    mlp_input = lax.all_gather(mlp_half, "tensor", axis=0, tiled=True)
    gate = jnp.dot(mlp_input, w_gate, preferred_element_type=jnp.float32)
    upward = jnp.dot(mlp_input, w_up, preferred_element_type=jnp.float32)
    hidden = (jax.nn.silu(gate) * upward).astype(jnp.bfloat16)
    mlp_part = jnp.dot(hidden, w_down, preferred_element_type=jnp.float32)
    result = middle + lax.psum_scatter(
        mlp_part.astype(jnp.bfloat16), "tensor", scatter_dimension=0, tiled=True
    ).astype(jnp.float32)
    cotangent = out_grad.reshape(row_total, width)
    grad_hidden = times_transpose(cotangent, w_down)
    sigmoid_gate = jax.nn.sigmoid(gate)
    grad_gate = (grad_hidden * upward * sigmoid_gate * (1.0 + gate * (1.0 - sigmoid_gate))).astype(
        jnp.bfloat16
    )
    grad_upward = (grad_hidden * gate * sigmoid_gate).astype(jnp.bfloat16)
    grad_w_down = outer_sum(hidden, cotangent)
    grad_w_gate = outer_sum(mlp_input, grad_gate)
    grad_w_up = outer_sum(mlp_input, grad_upward)
    grad_mlp_in = lax.psum_scatter(
        times_transpose(grad_gate, w_gate) + times_transpose(grad_upward, w_up),
        "tensor",
        scatter_dimension=0,
        tiled=True,
    )
    mlp_gain_part = jnp.sum(grad_mlp_in * normed_two, axis=0)
    scaled_two = grad_mlp_in * mlp_gain
    grad_middle = own_half(cotangent).astype(jnp.float32) + inverse_two * (
        scaled_two - normed_two * jnp.mean(scaled_two * normed_two, axis=-1, keepdims=True)
    )
    grad_middle_low = lax.all_gather(grad_middle.astype(jnp.bfloat16), "tensor", axis=0, tiled=True)
    grad_w_out = outer_sum(attn_heads, grad_middle_low)
    grad_heads = (
        times_transpose(grad_middle_low, w_out).astype(jnp.bfloat16)
        * valid_rows.astype(jnp.bfloat16)
    ).reshape(seq_count, tok_rows, kv_local, group_size, HD)
    delta = jnp.einsum(
        "sqkgd,sqkgd->skgq", grad_heads, exact_sum, preferred_element_type=jnp.float32
    )
    keys_back, values_back = (
        lax.all_gather(keys_own, "seq", axis=1, tiled=True),
        lax.all_gather(values_own, "seq", axis=1, tiled=True),
    )
    keys_back = keys_back.reshape(key_shape)
    values_back = values_back.reshape(key_shape)

    def backward_one():

        def run(items):
            (
                query_s,
                grad_s,
                log_s,
                delta_s,
                key_s,
                value_s,
                rows_s,
                seg_s,
                key_rows,
                key_seg,
                key_valid,
            ) = items
            return attend_backward(
                query_s,
                grad_s,
                log_s,
                delta_s,
                key_s,
                value_s,
                (rows_s, seg_s),
                (key_rows, key_seg, key_valid),
                block_rows,
            )

        return run

    backward_items = (
        queries,
        grad_heads,
        log_total,
        delta,
        keys_back,
        values_back,
        query_rows,
        query_seg,
        key_layout[0],
        key_layout[1],
        key_layout[3],
    )
    grad_query, key_terms = lax.map(backward_one(), backward_items)
    grad_key_sum, grad_value_sum = (
        lax.psum_scatter(
            key_terms[0].astype(jnp.bfloat16), "seq", scatter_dimension=1, tiled=True
        ).astype(jnp.float32),
        lax.psum_scatter(
            key_terms[1].astype(jnp.bfloat16), "seq", scatter_dimension=1, tiled=True
        ).astype(jnp.float32),
    )
    grad_key_rot = grad_key_sum.reshape(row_total, kv_local, HD) * HD ** (-0.5)
    grad_key_low = (
        rotate_back(grad_key_rot, cosine, sine_table)
        .astype(jnp.bfloat16)
        .reshape(row_total, kv_local * HD)
    )
    grad_value_low = grad_value_sum.reshape(row_total, kv_local * HD).astype(jnp.bfloat16)
    grad_query_rot = (grad_query * HD ** (-0.5)).reshape(row_total, heads_local, HD)
    grad_query_low = (
        rotate_back(grad_query_rot, cosine, sine_table)
        .astype(jnp.bfloat16)
        .reshape(row_total, heads_local * HD)
    )
    grad_w_query = outer_sum(attn_input, grad_query_low)
    grad_w_key = outer_sum(attn_input, grad_key_low)
    grad_w_value = outer_sum(attn_input, grad_value_low)
    attn_back_part = (
        times_transpose(grad_query_low, w_query)
        + times_transpose(grad_key_low, w_key)
        + times_transpose(grad_value_low, w_value)
    )
    grad_attn_in = lax.psum_scatter(
        attn_back_part.astype(jnp.bfloat16), "tensor", scatter_dimension=0, tiled=True
    ).astype(jnp.float32)
    normed_half = own_half(normed_one)
    attn_gain_part = jnp.sum(grad_attn_in * normed_half, axis=0)
    scaled_one = grad_attn_in * attn_gain
    grad_inputs = grad_middle + own_half(inverse_one) * (
        scaled_one - normed_half * jnp.mean(scaled_one * normed_half, axis=-1, keepdims=True)
    )
    grad_attn_gain, grad_mlp_gain = lax.psum((attn_gain_part, mlp_gain_part), "tensor")
    reduced = tuple(
        (
            lax.psum_scatter(grad_attn_gain, ("dp", "seq"), scatter_dimension=0, tiled=True),
            lax.psum_scatter(grad_w_query, ("dp", "seq"), scatter_dimension=0, tiled=True),
            lax.psum_scatter(grad_w_key, ("dp", "seq"), scatter_dimension=0, tiled=True),
            lax.psum_scatter(grad_w_value, ("dp", "seq"), scatter_dimension=0, tiled=True),
            lax.psum_scatter(grad_w_out, ("dp", "seq"), scatter_dimension=1, tiled=True),
            lax.psum_scatter(grad_mlp_gain, ("dp", "seq"), scatter_dimension=0, tiled=True),
            lax.psum_scatter(grad_w_gate, ("dp", "seq"), scatter_dimension=0, tiled=True),
            lax.psum_scatter(grad_w_up, ("dp", "seq"), scatter_dimension=0, tiled=True),
            lax.psum_scatter(grad_w_down, ("dp", "seq"), scatter_dimension=1, tiled=True),
        )
    )
    result_all, grad_all = (
        lax.all_gather(result.astype(jnp.bfloat16), "tensor", axis=0, tiled=True),
        lax.all_gather(grad_inputs.astype(jnp.bfloat16), "tensor", axis=0, tiled=True),
    )
    out_shape = (seq_count, tok_rows, width)
    return (
        result_all.reshape(out_shape),
        grad_all.reshape(out_shape),
        reduced[0],
        reduced[1],
        reduced[2],
        reduced[3],
        reduced[4],
        reduced[5],
        reduced[6],
        reduced[7],
        reduced[8],
    )


LOG2E = 1.4426950408889634
QUERY_TILE = 256
KEY_TILE = 512
PAD = 128
MEBI = 1024 * 1024


def doc_start(ends, rows):
    start = jnp.zeros_like(rows)
    previous = 0
    for end in ends:
        start = jnp.where(rows >= end, end, start)
    return jnp.where(rows >= ends[-1], rows, start)


def attention_forward_kernel(
    info, part_0, part_1, part_2, part_3, heads, keys, values, out_0, out_1, out_2, out_3, exact, lse, low
):
    parts, outs = (part_0, part_1, part_2, part_3), (out_0, out_1, out_2, out_3)
    rows_each = part_0.shape[0]
    total = rows_each * len(parts)
    ends = [info[index] for index in range(4)]
    place = info[4]
    heads[...] = jnp.zeros_like(heads)
    keys[...] = jnp.zeros_like(keys)
    values[...] = jnp.zeros_like(values)
    for step, part in enumerate(parts):
        rows = pl.ds(pl.multiple_of((place ^ step) * rows_each, rows_each), rows_each)
        heads[0, rows, :HD] = part[:, :HD]
        heads[1, rows, :HD] = part[:, HD : 2 * HD]
        keys[rows, :HD] = part[:, 2 * HD : 3 * HD]
        values[rows, :HD] = part[:, 3 * HD :]
    scale = HD ** (-0.5) * LOG2E

    def query_step(index, nothing):
        first = pl.multiple_of(index * QUERY_TILE, QUERY_TILE)
        tile = pl.ds(first, QUERY_TILE)
        queries = jnp.concatenate([heads[0, tile, :], heads[1, tile, :]], axis=0)
        row_ids = lax.broadcasted_iota(jnp.int32, (2 * QUERY_TILE, 1), 0) % QUERY_TILE + first
        starts = doc_start(ends, row_ids)
        low_tile = doc_start(ends, first) // KEY_TILE
        high_tile = (first + QUERY_TILE - 1) // KEY_TILE + 1

        def key_step(key_index, state):
            row_max, row_sum, summed = state
            first_key = pl.multiple_of(key_index * KEY_TILE, KEY_TILE)
            key_rows = pl.ds(first_key, KEY_TILE)
            scores = scale * lax.dot_general(
                queries, keys[key_rows, :], (((1,), (1,)), ((), ())), preferred_element_type=jnp.float32
            )
            columns = lax.broadcasted_iota(jnp.int32, (1, KEY_TILE), 1) + first_key
            scores = jnp.where((columns >= starts) & (columns <= row_ids), scores, masked_score)
            new_max = jnp.maximum(row_max, jnp.max(scores, axis=1, keepdims=True))
            probs = jnp.exp2(scores - new_max)
            shrink = jnp.exp2(row_max - new_max)
            row_sum = row_sum * shrink + jnp.sum(probs, axis=1, keepdims=True)
            summed = summed * shrink + jnp.dot(
                probs.astype(jnp.bfloat16), values[key_rows, :], preferred_element_type=jnp.float32
            )
            return (new_max, row_sum, summed)

        row_max, row_sum, summed = lax.fori_loop(
            low_tile,
            high_tile,
            key_step,
            (
                jnp.full((2 * QUERY_TILE, 1), masked_score, jnp.float32),
                jnp.zeros((2 * QUERY_TILE, 1), jnp.float32),
                jnp.zeros((2 * QUERY_TILE, PAD), jnp.float32),
            ),
        )
        result = jnp.where(row_ids < ends[-1], summed / row_sum, 0.0)
        total_log = row_max + jnp.log(row_sum) * LOG2E
        total_row = jnp.transpose(jnp.broadcast_to(total_log, (2 * QUERY_TILE, PAD)))[:1, :]
        for head in range(2):
            mine = result[head * QUERY_TILE : (head + 1) * QUERY_TILE]
            exact[head, tile, :] = mine
            low[tile, head * HD : (head + 1) * HD] = mine[:, :HD].astype(jnp.bfloat16)
            lse[head : head + 1, tile] = total_row[:, head * QUERY_TILE : (head + 1) * QUERY_TILE]
        return nothing

    lax.fori_loop(0, total // QUERY_TILE, query_step, 0)
    for step, out in enumerate(outs):
        rows = pl.ds(pl.multiple_of((place ^ step) * rows_each, rows_each), rows_each)
        out[...] = low[rows, :]


def attention_forward(info, parts):
    rows_each = parts[0].shape[0]
    total = rows_each * len(parts)
    wide = jax.ShapeDtypeStruct((total, PAD), jnp.bfloat16)
    return pl.pallas_call(
        attention_forward_kernel,
        out_shape=(
            jax.ShapeDtypeStruct((2, total, PAD), jnp.bfloat16),
            wide,
            wide,
            *(jax.ShapeDtypeStruct((rows_each, 2 * HD), jnp.bfloat16) for _ in parts),
            jax.ShapeDtypeStruct((2, total, PAD), jnp.float32),
            jax.ShapeDtypeStruct((2, total), jnp.float32),
        ),
        in_specs=[pl.BlockSpec(memory_space=pltpu.SMEM)]
        + [pl.BlockSpec(memory_space=pltpu.VMEM)] * len(parts),
        out_specs=(pl.BlockSpec(memory_space=pltpu.VMEM),) * 9,
        scratch_shapes=[pltpu.VMEM((total, 2 * HD), jnp.bfloat16)],
        compiler_params=pltpu.CompilerParams(vmem_limit_bytes=48 * MEBI),
        cost_estimate=pl.CostEstimate(
            flops=4 * 2 * total * total * PAD // 2, bytes_accessed=8 * MEBI, transcendentals=total * total
        ),
        name="attention_forward",
    )(info, *parts)


def attention_backward_kernel(
    info,
    grad_0,
    grad_1,
    grad_2,
    grad_3,
    heads,
    keys,
    values,
    exact,
    lse,
    back_0,
    back_1,
    back_2,
    back_3,
    grad_heads,
    grad_query,
    grad_key,
    grad_value,
):
    grads, backs = (grad_0, grad_1, grad_2, grad_3), (back_0, back_1, back_2, back_3)
    rows_each = grad_0.shape[0]
    total = rows_each * len(grads)
    ends = [info[index] for index in range(4)]
    place = info[4]
    grad_heads[...] = jnp.zeros_like(grad_heads)
    grad_key[...] = jnp.zeros_like(grad_key)
    grad_value[...] = jnp.zeros_like(grad_value)
    for step, grad in enumerate(grads):
        rows = pl.ds(pl.multiple_of((place ^ step) * rows_each, rows_each), rows_each)
        grad_heads[0, rows, :HD] = grad[:, :HD]
        grad_heads[1, rows, :HD] = grad[:, HD:]
    scale = HD ** (-0.5) * LOG2E

    def query_step(index, nothing):
        first = pl.multiple_of(index * QUERY_TILE, QUERY_TILE)
        tile = pl.ds(first, QUERY_TILE)
        queries = jnp.concatenate([heads[0, tile, :], heads[1, tile, :]], axis=0)
        grad_rows = jnp.concatenate([grad_heads[0, tile, :], grad_heads[1, tile, :]], axis=0)
        exact_rows = jnp.concatenate([exact[0, tile, :], exact[1, tile, :]], axis=0)
        delta = jnp.sum(
            jnp.transpose(grad_rows.astype(jnp.float32) * exact_rows), axis=0, keepdims=True
        )
        log_row = jnp.concatenate([lse[0:1, tile], lse[1:2, tile]], axis=1)
        row_ids = lax.broadcasted_iota(jnp.int32, (1, 2 * QUERY_TILE), 1) % QUERY_TILE + first
        starts = doc_start(ends, row_ids)
        low_tile = doc_start(ends, first) // KEY_TILE
        high_tile = (first + QUERY_TILE - 1) // KEY_TILE + 1

        def key_step(key_index, summed):
            first_key = pl.multiple_of(key_index * KEY_TILE, KEY_TILE)
            key_rows = pl.ds(first_key, KEY_TILE)
            key_part, value_part = keys[key_rows, :], values[key_rows, :]
            scores = scale * times_transpose(key_part, queries)
            columns = lax.broadcasted_iota(jnp.int32, (KEY_TILE, 1), 0) + first_key
            probs = jnp.where(
                (columns >= starts) & (columns <= row_ids), jnp.exp2(scores - log_row), 0.0
            )
            grad_scores = (probs * (times_transpose(value_part, grad_rows) - delta)).astype(
                jnp.bfloat16
            )
            grad_value[key_rows, :] += jnp.dot(
                probs.astype(jnp.bfloat16), grad_rows, preferred_element_type=jnp.float32
            )
            grad_key[key_rows, :] += jnp.dot(
                grad_scores, queries, preferred_element_type=jnp.float32
            )
            return summed + outer_sum(grad_scores, key_part)

        summed = lax.fori_loop(
            low_tile, high_tile, key_step, jnp.zeros((2 * QUERY_TILE, PAD), jnp.float32)
        )
        grad_query[0, tile, :] = summed[:QUERY_TILE]
        grad_query[1, tile, :] = summed[QUERY_TILE:]
        return nothing

    lax.fori_loop(0, total // QUERY_TILE, query_step, 0)
    for step, back in enumerate(backs):
        rows = pl.ds(pl.multiple_of((place ^ step) * rows_each, rows_each), rows_each)
        back[:, :HD] = (grad_query[0, rows, :HD] * HD ** (-0.5)).astype(jnp.bfloat16)
        back[:, HD : 2 * HD] = (grad_query[1, rows, :HD] * HD ** (-0.5)).astype(jnp.bfloat16)
        back[:, 2 * HD : 3 * HD] = (grad_key[rows, :HD] * HD ** (-0.5)).astype(jnp.bfloat16)
        back[:, 3 * HD :] = grad_value[rows, :HD].astype(jnp.bfloat16)


def attention_backward(info, grads, kept):
    rows_each = grads[0].shape[0]
    total = rows_each * len(grads)
    return pl.pallas_call(
        attention_backward_kernel,
        out_shape=tuple(jax.ShapeDtypeStruct((rows_each, 4 * HD), jnp.bfloat16) for _ in grads),
        in_specs=[pl.BlockSpec(memory_space=pltpu.SMEM)]
        + [pl.BlockSpec(memory_space=pltpu.VMEM)] * (len(grads) + len(kept)),
        out_specs=(pl.BlockSpec(memory_space=pltpu.VMEM),) * len(grads),
        scratch_shapes=[
            pltpu.VMEM((2, total, PAD), jnp.bfloat16),
            pltpu.VMEM((2, total, PAD), jnp.float32),
            pltpu.VMEM((total, PAD), jnp.float32),
            pltpu.VMEM((total, PAD), jnp.float32),
        ],
        compiler_params=pltpu.CompilerParams(vmem_limit_bytes=48 * MEBI),
        cost_estimate=pl.CostEstimate(
            flops=10 * 2 * total * total * PAD // 2, bytes_accessed=8 * MEBI, transcendentals=total * total
        ),
        name="attention_backward",
    )(info, *grads, *kept)


STEPS = {"y": ("dp", 2), "x": ("dp", 1), "far": ("seq", 2), "near": ("seq", 1)}
ORDER = ("y", "x", "far", "near")


def swap(array, axis, bit):
    return lax.ppermute(array, axis, [(i, i ^ bit) for i in range(lax.axis_size(axis))])


def side(step):
    axis, bit = STEPS[step]
    return (lax.axis_index(axis) // bit) % 2


def grad_rows_reduced(left, right, steps):
    width, columns = left.shape[1], right.shape[1]
    left_open = list(ORDER)
    blocks = left.reshape(left.shape[0], 2, 2, 2, 2, width // 16)
    here = side(steps[0])
    place = left_open.index(steps[0])

    def piece(which):
        chosen = lax.dynamic_index_in_dim(blocks, which, place + 1, keepdims=False)
        return (
            outer_sum(chosen.reshape(left.shape[0], width // 2), right)
            .astype(jnp.bfloat16)
            .reshape(2, 2, 2, width // 16, columns)
        )

    arrived = swap(piece(1 - here), *STEPS[steps[0]])
    kept = piece(here).astype(jnp.float32) + arrived.astype(jnp.float32)
    left_open.remove(steps[0])
    for step in steps[1:]:
        place, here = left_open.index(step), side(step)
        kept = kept.astype(jnp.bfloat16)
        arrived = swap(
            lax.dynamic_index_in_dim(kept, 1 - here, place, keepdims=False), *STEPS[step]
        )
        kept = lax.dynamic_index_in_dim(kept, here, place, keepdims=False).astype(
            jnp.float32
        ) + arrived.astype(jnp.float32)
        left_open.remove(step)
    return kept


def local_paired(
    hidden_in,
    lengths,
    attn_gain,
    w_query,
    w_key,
    w_value,
    w_out,
    mlp_gain,
    w_gate,
    w_up,
    w_down,
    out_grad,
):
    rows, width = hidden_in.shape[1], hidden_in.shape[2]
    half_rows = rows // 2
    half_start = lax.axis_index("tensor") * half_rows
    place = lax.axis_index("seq")
    kv_local = w_key.shape[1] // HD
    group_size = HQ // KV

    def own_half(array_in):
        return lax.dynamic_slice_in_dim(array_in, half_start, half_rows, 0)

    def own_sum(part):
        return lax.psum_scatter(part, "tensor", scatter_dimension=0, tiled=True)

    def both_halves(part):
        return lax.all_gather(part, "tensor", axis=0, tiled=True)

    def dealt(stacked):
        own = [lax.dynamic_index_in_dim(stacked, place ^ d, 0, keepdims=False) for d in range(4)]
        return [own[0]] + [swap(own[d], "seq", d) for d in range(1, 4)]

    def returned(parts):
        arrived = jnp.stack([parts[0]] + [swap(parts[d], "seq", d) for d in range(1, 4)])
        return jnp.stack(
            [lax.dynamic_index_in_dim(arrived, place ^ d, 0, keepdims=False) for d in range(4)],
            axis=1,
        )

    inputs = hidden_in[0].astype(jnp.float32)
    _, _, offsets, valid = doc_layout(lengths[0], place * rows, rows)
    info = jnp.concatenate([jnp.cumsum(lengths[0]), place[None]]).astype(jnp.int32)
    cosine, sine_table = rope_tables(offsets)
    valid_rows = valid.astype(jnp.float32)[:, None]
    inverse_one = lax.rsqrt(jnp.mean(inputs * inputs, axis=-1, keepdims=True) + epsilon)
    normed_one = inputs * inverse_one
    attn_input = (normed_one * attn_gain).astype(jnp.bfloat16)

    def project(weight):
        return jnp.dot(attn_input, weight, preferred_element_type=jnp.float32)

    queries = rotate(project(w_query).reshape(rows, -1, HD), cosine, sine_table)
    keys = rotate(project(w_key).reshape(rows, -1, HD), cosine, sine_table)
    values = project(w_value)
    dealt_heads = jnp.concatenate(
        [
            queries.astype(jnp.bfloat16).reshape(rows, kv_local, group_size * HD),
            keys.astype(jnp.bfloat16),
            values.astype(jnp.bfloat16).reshape(rows, kv_local, HD),
        ],
        axis=-1,
    )
    forward = attention_forward(info, dealt(jnp.moveaxis(dealt_heads, 1, 0)))
    kept = forward[:3] + forward[7:]
    attn_heads = returned(forward[3:7]).reshape(rows, -1)
    middle = own_half(inputs) + own_sum(
        jnp.dot(attn_heads, w_out, preferred_element_type=jnp.float32)
    )
    inverse_two = lax.rsqrt(jnp.mean(middle * middle, axis=-1, keepdims=True) + epsilon)
    normed_two = middle * inverse_two
    mlp_input = both_halves((normed_two * mlp_gain).astype(jnp.bfloat16))
    gate = jnp.dot(mlp_input, w_gate, preferred_element_type=jnp.float32)
    upward = jnp.dot(mlp_input, w_up, preferred_element_type=jnp.float32)
    cotangent = out_grad[0]
    grad_hidden = times_transpose(cotangent, w_down)
    sigmoid_gate = jax.nn.sigmoid(gate)
    hidden = (gate * sigmoid_gate * upward).astype(jnp.bfloat16)
    grad_gate = (grad_hidden * upward * sigmoid_gate * (1.0 + gate * (1.0 - sigmoid_gate))).astype(
        jnp.bfloat16
    )
    grad_upward = (grad_hidden * gate * sigmoid_gate).astype(jnp.bfloat16)
    grad_mlp_in = own_sum(
        times_transpose(grad_gate, w_gate) + times_transpose(grad_upward, w_up)
    )
    grad_w_down = grad_rows_reduced(cotangent, hidden, ("x", "y", "near", "far"))
    grad_w_gate = grad_rows_reduced(mlp_input, grad_gate, ("y", "x", "near", "far"))
    grad_w_up = grad_rows_reduced(mlp_input, grad_upward, ("x", "y", "near", "far"))
    mlp_part = jnp.dot(hidden, w_down, preferred_element_type=jnp.float32)
    result = middle + own_sum(mlp_part.astype(jnp.bfloat16)).astype(jnp.float32)
    mlp_gain_part = jnp.sum(grad_mlp_in * normed_two, axis=0)
    scaled_two = grad_mlp_in * mlp_gain
    grad_middle = own_half(cotangent).astype(jnp.float32) + inverse_two * (
        scaled_two - normed_two * jnp.mean(scaled_two * normed_two, axis=-1, keepdims=True)
    )
    grad_middle_low = both_halves(grad_middle.astype(jnp.bfloat16))
    grad_heads = times_transpose(grad_middle_low, w_out).astype(jnp.bfloat16) * valid_rows.astype(
        jnp.bfloat16
    )
    grad_parts = dealt(jnp.moveaxis(grad_heads.reshape(rows, kv_local, group_size * HD), 1, 0))
    grad_w_out = grad_rows_reduced(grad_middle_low, attn_heads, ("y", "x", "near", "far"))
    grad_dealt = returned(attention_backward(info, grad_parts, kept))
    split_at = group_size * HD
    grad_query = rotate_back(
        grad_dealt[:, :, :split_at].reshape(rows, -1, HD).astype(jnp.float32), cosine, sine_table
    )
    grad_key = rotate_back(
        grad_dealt[:, :, split_at : split_at + HD].astype(jnp.float32), cosine, sine_table
    )
    grad_query_low = grad_query.astype(jnp.bfloat16).reshape(rows, -1)
    grad_key_low = grad_key.astype(jnp.bfloat16).reshape(rows, -1)
    grad_value_low = grad_dealt[:, :, split_at + HD :].reshape(rows, -1)
    grad_w_qkv = grad_rows_reduced(
        attn_input,
        jnp.concatenate([grad_query_low, grad_key_low, grad_value_low], axis=1),
        ("x", "y", "near", "far"),
    )
    grad_attn_in = own_sum(
        (
            times_transpose(grad_query_low, w_query)
            + times_transpose(grad_key_low, w_key)
            + times_transpose(grad_value_low, w_value)
        ).astype(jnp.bfloat16)
    ).astype(jnp.float32)
    normed_half = own_half(normed_one)
    attn_gain_part = jnp.sum(grad_attn_in * normed_half, axis=0)
    scaled_one = grad_attn_in * attn_gain
    grad_inputs = grad_middle + own_half(inverse_one) * (
        scaled_one - normed_half * jnp.mean(scaled_one * normed_half, axis=-1, keepdims=True)
    )
    gains = jnp.stack([attn_gain_part, mlp_gain_part]).reshape(2, 16, 1, width // 16)
    gains = jnp.broadcast_to(gains, (2, 16, 2, width // 16)).reshape(2, 32, width // 16)
    gains = jnp.sum(
        lax.all_to_all(jnp.moveaxis(gains, 1, 0), ("dp", "seq", "tensor"), 0, 0, tiled=True), axis=0
    )
    query_width, key_width = w_query.shape[1], w_key.shape[1]
    return (
        both_halves(result.astype(jnp.bfloat16))[None],
        both_halves(grad_inputs.astype(jnp.bfloat16))[None],
        gains[0],
        grad_w_qkv[:, :query_width],
        grad_w_qkv[:, query_width : query_width + key_width],
        grad_w_qkv[:, query_width + key_width :],
        grad_w_out.T,
        gains[1],
        grad_w_gate,
        grad_w_up,
        grad_w_down.T,
    )


def solution(mesh):
    in_specs = (
        P("dp", "seq", None),
        P("dp", None),
        P(),
        P(None, "tensor"),
        P(None, "tensor"),
        P(None, "tensor"),
        P("tensor", None),
        P(),
        P(None, "tensor"),
        P(None, "tensor"),
        P("tensor", None),
        P("dp", "seq", None),
    )
    out_specs = (
        P("dp", "seq", None),
        P("dp", "seq", None),
        P(("dp", "seq")),
        P(("dp", "seq"), "tensor"),
        P(("dp", "seq"), "tensor"),
        P(("dp", "seq"), "tensor"),
        P("tensor", ("dp", "seq")),
        P(("dp", "seq")),
        P(("dp", "seq"), "tensor"),
        P(("dp", "seq"), "tensor"),
        P("tensor", ("dp", "seq")),
    )
    body = local_paired if tuple(mesh.shape[name] for name in ("dp", "seq", "tensor")) == (4, 4, 2) else local
    return jax.shard_map(body, mesh=mesh, in_specs=in_specs, out_specs=out_specs, check_vma=False)
```

```python
import jax
import jax.numpy as jnp
from jax import lax
from jax.experimental import pallas as pl
from jax.experimental.pallas import tpu as pltpu
from jax.sharding import PartitionSpec as P

HQ = 16
KV = 8
HD = 96


epsilon = 1e-05
rope_theta = 100000.0
masked_score = -1e30


def doc_layout(length_row, first_row, row_count):
    positions = first_row + jnp.arange(row_count, dtype=jnp.int32)
    doc_ends = jnp.cumsum(length_row)
    passed = (positions[:, None] >= doc_ends[None, :]).astype(jnp.int32)
    segment = jnp.sum(passed, axis=1)
    doc_start = jnp.sum(passed * length_row[None, :], axis=1)
    return (positions, segment, positions - doc_start, segment < length_row.shape[0])


def rope_tables(offsets):
    half_size = HD // 2
    inverse = rope_theta ** (-2.0 * jnp.arange(half_size, dtype=jnp.float32) / HD)
    angles = offsets.astype(jnp.float32)[:, None] * inverse[None, :]
    return (jnp.cos(angles)[:, None, :], jnp.sin(angles)[:, None, :])


def rotate(values, cosine, sine_table):
    half_size = values.shape[-1] // 2
    first_half = values[..., :half_size]
    second_half = values[..., half_size:]
    return jnp.concatenate(
        [
            first_half * cosine - second_half * sine_table,
            second_half * cosine + first_half * sine_table,
        ],
        axis=-1,
    )


def rotate_back(gradient, cosine, sine_table):
    half_size = gradient.shape[-1] // 2
    first_half = gradient[..., :half_size]
    second_half = gradient[..., half_size:]
    return jnp.concatenate(
        [
            first_half * cosine + second_half * sine_table,
            second_half * cosine - first_half * sine_table,
        ],
        axis=-1,
    )


def outer_sum(left, right):
    return lax.dot_general(
        left, right, (((0,), (0,)), ((), ())), preferred_element_type=jnp.float32
    )


def times_transpose(left, right):
    return lax.dot_general(
        left, right, (((1,), (1,)), ((), ())), preferred_element_type=jnp.float32
    )


def allowed_pairs(query_rows, query_seg, key_rows, key_seg, key_valid):
    same_doc = (
        (query_seg[:, None] == key_seg[None, :])
        & (key_rows[None, :] <= query_rows[:, None])
        & key_valid[None, :]
    )
    return same_doc | (key_rows[None, :] == query_rows[:, None])


def score_block(queries, key_part, allowed_mask):
    raw_scores = jnp.einsum("qkgd,jkd->kgqj", queries, key_part, preferred_element_type=jnp.float32)
    return jnp.where(allowed_mask[None, None], raw_scores * HD ** (-0.5), masked_score)


def backward_terms(queries, grad_heads, log_total, delta, key_part, value_part, allowed_mask):
    probs = jnp.exp(score_block(queries, key_part, allowed_mask) - log_total[..., None])
    grad_probs = jnp.einsum(
        "qkgd,jkd->kgqj", grad_heads, value_part, preferred_element_type=jnp.float32
    )
    grad_scores = (probs * (grad_probs - delta[..., None])).astype(jnp.bfloat16)
    return (probs.astype(jnp.bfloat16), grad_scores)


def block_loader(keys_all, values_all, query_info, key_info, block_rows):
    query_rows, query_seg = query_info

    def load_block(block_index):
        first_key = block_index * block_rows
        key_part = lax.dynamic_slice_in_dim(keys_all, first_key, block_rows, 0)
        value_part = lax.dynamic_slice_in_dim(values_all, first_key, block_rows, 0)
        key_rows, key_seg, key_valid = tuple(
            (lax.dynamic_slice_in_dim(member, first_key, block_rows, 0) for member in key_info)
        )
        return (
            key_part,
            value_part,
            allowed_pairs(query_rows, query_seg, key_rows, key_seg, key_valid),
        )

    return load_block


def attend_forward(queries, keys_all, values_all, query_info, key_info, block_rows):
    last_row = query_info[0][-1]
    block_count = keys_all.shape[0] // block_rows
    stat_shape = (queries.shape[1], queries.shape[2], queries.shape[0])
    load_block = block_loader(keys_all, values_all, query_info, key_info, block_rows)

    def stats_step(block_index, running):

        def stats_compute(state_in):
            row_max, row_sum = state_in
            key_part, value_part, allowed_mask = load_block(block_index)
            scores = score_block(queries, key_part, allowed_mask)
            new_max = jnp.maximum(row_max, jnp.max(scores, axis=-1))
            new_sum = row_sum * jnp.exp(row_max - new_max) + jnp.sum(
                jnp.exp(scores - new_max[..., None]), axis=-1
            )
            return (new_max, new_sum)

        return lax.cond(
            block_index * block_rows <= last_row, stats_compute, lambda state_in: state_in, running
        )

    start_stats = (
        jnp.full(stat_shape, masked_score, jnp.float32),
        jnp.zeros(stat_shape, jnp.float32),
    )
    row_max, row_sum = lax.fori_loop(0, block_count, stats_step, start_stats)
    log_total = row_max + jnp.log(row_sum)

    def output_step(block_index, running):

        def output_compute(state_in):
            kept_sum, rest_sum = state_in
            key_part, value_part, allowed_mask = load_block(block_index)
            probs = jnp.exp(score_block(queries, key_part, allowed_mask) - log_total[..., None])
            probs_low = probs.astype(jnp.bfloat16)
            rest_low = (probs - probs_low.astype(jnp.float32)).astype(jnp.bfloat16)
            kept_sum = kept_sum + jnp.einsum(
                "kgqj,jkd->qkgd", probs_low, value_part, preferred_element_type=jnp.float32
            )
            rest_sum = rest_sum + jnp.einsum(
                "kgqj,jkd->qkgd", rest_low, value_part, preferred_element_type=jnp.float32
            )
            return (kept_sum, rest_sum)

        return lax.cond(
            block_index * block_rows <= last_row, output_compute, lambda state_in: state_in, running
        )

    zero_out = jnp.zeros(queries.shape, jnp.float32)
    kept_sum, rest_sum = lax.fori_loop(0, block_count, output_step, (zero_out, zero_out))
    return (log_total, kept_sum, kept_sum + rest_sum)


def attend_backward(
    queries, grad_heads, log_total, delta, keys_all, values_all, query_info, key_info, block_rows
):
    last_row = query_info[0][-1]
    block_count = keys_all.shape[0] // block_rows
    key_width = keys_all.shape[1] * keys_all.shape[2]
    load_block = block_loader(keys_all, values_all, query_info, key_info, block_rows)

    def grad_step(running, block_index):

        def grad_compute(state_in):
            key_part, value_part, allowed_mask = load_block(block_index)
            probs_low, grad_scores = backward_terms(
                queries, grad_heads, log_total, delta, key_part, value_part, allowed_mask
            )
            grad_query = state_in + jnp.einsum(
                "kgqj,jkd->qkgd", grad_scores, key_part, preferred_element_type=jnp.float32
            )
            key_terms = ()
            grad_key = jnp.einsum(
                "kgqj,qkgd->jkd", grad_scores, queries, preferred_element_type=jnp.float32
            )
            grad_value = jnp.einsum(
                "kgqj,qkgd->jkd", probs_low, grad_heads, preferred_element_type=jnp.float32
            )
            key_terms = (
                grad_key.reshape(block_rows, key_width),
                grad_value.reshape(block_rows, key_width),
            )
            return (grad_query, key_terms)

        def skipped(state_in):
            key_terms = ()
            zero_block = jnp.zeros((block_rows, key_width), jnp.float32)
            key_terms = (zero_block, zero_block)
            return (state_in, key_terms)

        return lax.cond(block_index * block_rows <= last_row, grad_compute, skipped, running)

    grad_query, key_terms = lax.scan(
        grad_step, jnp.zeros(queries.shape, jnp.float32), jnp.arange(block_count, dtype=jnp.int32)
    )
    key_terms = tuple((member.reshape(block_count * block_rows, key_width) for member in key_terms))
    return (grad_query, key_terms)


def local(
    hidden_in,
    lengths,
    attn_gain,
    w_query,
    w_key,
    w_value,
    w_out,
    mlp_gain,
    w_gate,
    w_up,
    w_down,
    out_grad,
):
    seq_count = hidden_in.shape[0]
    tok_rows = hidden_in.shape[1]
    width = hidden_in.shape[2]
    row_total = seq_count * tok_rows
    seq_total = tok_rows * lax.axis_size("seq")
    first_row = lax.axis_index("seq") * tok_rows
    half_rows = row_total // lax.axis_size("tensor")
    half_start = lax.axis_index("tensor") * half_rows
    block_rows = min(512, seq_total)
    kv_local = w_key.shape[1] // HD
    group_size = HQ // KV
    heads_local = kv_local * group_size

    def own_half(array_in):
        return lax.dynamic_slice_in_dim(array_in, half_start, half_rows, 0)

    inputs = hidden_in.reshape(row_total, width).astype(jnp.float32)
    query_rows, query_seg, query_offsets, query_valid = jax.vmap(
        lambda length_row: doc_layout(length_row, first_row, tok_rows)
    )(lengths)
    key_layout = jax.vmap(lambda length_row: doc_layout(length_row, 0, seq_total))(lengths)
    cosine, sine_table = rope_tables(query_offsets.reshape(row_total))
    valid_rows = query_valid.reshape(row_total).astype(jnp.float32)[:, None]
    inverse_one = lax.rsqrt(jnp.mean(inputs * inputs, axis=-1, keepdims=True) + epsilon)
    normed_one = inputs * inverse_one
    attn_input = (normed_one * attn_gain).astype(jnp.bfloat16)
    query_raw = jnp.dot(attn_input, w_query, preferred_element_type=jnp.float32).reshape(
        row_total, heads_local, HD
    )
    key_raw = jnp.dot(attn_input, w_key, preferred_element_type=jnp.float32).reshape(
        row_total, kv_local, HD
    )
    values_own = (
        jnp.dot(attn_input, w_value, preferred_element_type=jnp.float32)
        .astype(jnp.bfloat16)
        .reshape(seq_count, tok_rows, kv_local * HD)
    )
    queries = (
        rotate(query_raw, cosine, sine_table)
        .astype(jnp.bfloat16)
        .reshape(seq_count, tok_rows, kv_local, group_size, HD)
    )
    keys_own = (
        rotate(key_raw, cosine, sine_table)
        .astype(jnp.bfloat16)
        .reshape(seq_count, tok_rows, kv_local * HD)
    )
    keys_all, values_all = (
        lax.all_gather(keys_own, "seq", axis=1, tiled=True),
        lax.all_gather(values_own, "seq", axis=1, tiled=True),
    )
    key_shape = (seq_count, seq_total, kv_local, HD)

    def forward_one(items):
        query_s, key_s, value_s, rows_s, seg_s, key_rows, key_seg, key_valid = items
        return attend_forward(
            query_s, key_s, value_s, (rows_s, seg_s), (key_rows, key_seg, key_valid), block_rows
        )

    log_total, kept_sum, exact_sum = lax.map(
        forward_one,
        (
            queries,
            keys_all.reshape(key_shape),
            values_all.reshape(key_shape),
            query_rows,
            query_seg,
            key_layout[0],
            key_layout[1],
            key_layout[3],
        ),
    )
    attn_heads = (kept_sum.reshape(row_total, heads_local * HD) * valid_rows).astype(jnp.bfloat16)
    attn_part = jnp.dot(attn_heads, w_out, preferred_element_type=jnp.float32)
    middle = own_half(inputs) + lax.psum_scatter(
        attn_part, "tensor", scatter_dimension=0, tiled=True
    )
    inverse_two = lax.rsqrt(jnp.mean(middle * middle, axis=-1, keepdims=True) + epsilon)
    normed_two = middle * inverse_two
    mlp_half = (normed_two * mlp_gain).astype(jnp.bfloat16)
    mlp_input = lax.all_gather(mlp_half, "tensor", axis=0, tiled=True)
    gate = jnp.dot(mlp_input, w_gate, preferred_element_type=jnp.float32)
    upward = jnp.dot(mlp_input, w_up, preferred_element_type=jnp.float32)
    hidden = (jax.nn.silu(gate) * upward).astype(jnp.bfloat16)
    mlp_part = jnp.dot(hidden, w_down, preferred_element_type=jnp.float32)
    result = middle + lax.psum_scatter(
        mlp_part.astype(jnp.bfloat16), "tensor", scatter_dimension=0, tiled=True
    ).astype(jnp.float32)
    cotangent = out_grad.reshape(row_total, width)
    grad_hidden = times_transpose(cotangent, w_down)
    sigmoid_gate = jax.nn.sigmoid(gate)
    grad_gate = (grad_hidden * upward * sigmoid_gate * (1.0 + gate * (1.0 - sigmoid_gate))).astype(
        jnp.bfloat16
    )
    grad_upward = (grad_hidden * gate * sigmoid_gate).astype(jnp.bfloat16)
    grad_w_down = outer_sum(hidden, cotangent)
    grad_w_gate = outer_sum(mlp_input, grad_gate)
    grad_w_up = outer_sum(mlp_input, grad_upward)
    grad_mlp_in = lax.psum_scatter(
        times_transpose(grad_gate, w_gate) + times_transpose(grad_upward, w_up),
        "tensor",
        scatter_dimension=0,
        tiled=True,
    )
    mlp_gain_part = jnp.sum(grad_mlp_in * normed_two, axis=0)
    scaled_two = grad_mlp_in * mlp_gain
    grad_middle = own_half(cotangent).astype(jnp.float32) + inverse_two * (
        scaled_two - normed_two * jnp.mean(scaled_two * normed_two, axis=-1, keepdims=True)
    )
    grad_middle_low = lax.all_gather(grad_middle.astype(jnp.bfloat16), "tensor", axis=0, tiled=True)
    grad_w_out = outer_sum(attn_heads, grad_middle_low)
    grad_heads = (
        times_transpose(grad_middle_low, w_out).astype(jnp.bfloat16)
        * valid_rows.astype(jnp.bfloat16)
    ).reshape(seq_count, tok_rows, kv_local, group_size, HD)
    delta = jnp.einsum(
        "sqkgd,sqkgd->skgq", grad_heads, exact_sum, preferred_element_type=jnp.float32
    )
    keys_back, values_back = (
        lax.all_gather(keys_own, "seq", axis=1, tiled=True),
        lax.all_gather(values_own, "seq", axis=1, tiled=True),
    )
    keys_back = keys_back.reshape(key_shape)
    values_back = values_back.reshape(key_shape)

    def backward_one():

        def run(items):
            (
                query_s,
                grad_s,
                log_s,
                delta_s,
                key_s,
                value_s,
                rows_s,
                seg_s,
                key_rows,
                key_seg,
                key_valid,
            ) = items
            return attend_backward(
                query_s,
                grad_s,
                log_s,
                delta_s,
                key_s,
                value_s,
                (rows_s, seg_s),
                (key_rows, key_seg, key_valid),
                block_rows,
            )

        return run

    backward_items = (
        queries,
        grad_heads,
        log_total,
        delta,
        keys_back,
        values_back,
        query_rows,
        query_seg,
        key_layout[0],
        key_layout[1],
        key_layout[3],
    )
    grad_query, key_terms = lax.map(backward_one(), backward_items)
    grad_key_sum, grad_value_sum = (
        lax.psum_scatter(
            key_terms[0].astype(jnp.bfloat16), "seq", scatter_dimension=1, tiled=True
        ).astype(jnp.float32),
        lax.psum_scatter(
            key_terms[1].astype(jnp.bfloat16), "seq", scatter_dimension=1, tiled=True
        ).astype(jnp.float32),
    )
    grad_key_rot = grad_key_sum.reshape(row_total, kv_local, HD) * HD ** (-0.5)
    grad_key_low = (
        rotate_back(grad_key_rot, cosine, sine_table)
        .astype(jnp.bfloat16)
        .reshape(row_total, kv_local * HD)
    )
    grad_value_low = grad_value_sum.reshape(row_total, kv_local * HD).astype(jnp.bfloat16)
    grad_query_rot = (grad_query * HD ** (-0.5)).reshape(row_total, heads_local, HD)
    grad_query_low = (
        rotate_back(grad_query_rot, cosine, sine_table)
        .astype(jnp.bfloat16)
        .reshape(row_total, heads_local * HD)
    )
    grad_w_query = outer_sum(attn_input, grad_query_low)
    grad_w_key = outer_sum(attn_input, grad_key_low)
    grad_w_value = outer_sum(attn_input, grad_value_low)
    attn_back_part = (
        times_transpose(grad_query_low, w_query)
        + times_transpose(grad_key_low, w_key)
        + times_transpose(grad_value_low, w_value)
    )
    grad_attn_in = lax.psum_scatter(
        attn_back_part.astype(jnp.bfloat16), "tensor", scatter_dimension=0, tiled=True
    ).astype(jnp.float32)
    normed_half = own_half(normed_one)
    attn_gain_part = jnp.sum(grad_attn_in * normed_half, axis=0)
    scaled_one = grad_attn_in * attn_gain
    grad_inputs = grad_middle + own_half(inverse_one) * (
        scaled_one - normed_half * jnp.mean(scaled_one * normed_half, axis=-1, keepdims=True)
    )
    grad_attn_gain, grad_mlp_gain = lax.psum((attn_gain_part, mlp_gain_part), "tensor")
    reduced = tuple(
        (
            lax.psum_scatter(grad_attn_gain, ("dp", "seq"), scatter_dimension=0, tiled=True),
            lax.psum_scatter(grad_w_query, ("dp", "seq"), scatter_dimension=0, tiled=True),
            lax.psum_scatter(grad_w_key, ("dp", "seq"), scatter_dimension=0, tiled=True),
            lax.psum_scatter(grad_w_value, ("dp", "seq"), scatter_dimension=0, tiled=True),
            lax.psum_scatter(grad_w_out, ("dp", "seq"), scatter_dimension=1, tiled=True),
            lax.psum_scatter(grad_mlp_gain, ("dp", "seq"), scatter_dimension=0, tiled=True),
            lax.psum_scatter(grad_w_gate, ("dp", "seq"), scatter_dimension=0, tiled=True),
            lax.psum_scatter(grad_w_up, ("dp", "seq"), scatter_dimension=0, tiled=True),
            lax.psum_scatter(grad_w_down, ("dp", "seq"), scatter_dimension=1, tiled=True),
        )
    )
    result_all, grad_all = (
        lax.all_gather(result.astype(jnp.bfloat16), "tensor", axis=0, tiled=True),
        lax.all_gather(grad_inputs.astype(jnp.bfloat16), "tensor", axis=0, tiled=True),
    )
    out_shape = (seq_count, tok_rows, width)
    return (
        result_all.reshape(out_shape),
        grad_all.reshape(out_shape),
        reduced[0],
        reduced[1],
        reduced[2],
        reduced[3],
        reduced[4],
        reduced[5],
        reduced[6],
        reduced[7],
        reduced[8],
    )


LOG2E = 1.4426950408889634
QUERY_TILE = 256
KEY_TILE = 512
PAD = 128
ROW_TILE = 256
MEBI = 1024 * 1024
VMEM_LIMIT = 56 * MEBI
IN_VMEM = pl.BlockSpec(memory_space=pltpu.VMEM)
IN_ANY = pl.BlockSpec(memory_space=pl.ANY)


def doc_start(ends, rows):
    start = jnp.zeros_like(rows)
    for end in ends:
        start = jnp.where(rows >= end, end, start)
    return jnp.where(rows >= ends[-1], rows, start)


def dot_plain(left, right):
    return jnp.dot(left, right, preferred_element_type=jnp.float32)


def local_call(kernel, name, info, operands, in_specs, out_shape, out_specs, grid, scratch=(), flops=0):
    sizes = [a.size * a.dtype.itemsize for a in (*operands, *out_shape)]
    return pl.pallas_call(
        kernel,
        out_shape=out_shape,
        grid_spec=pltpu.PrefetchScalarGridSpec(
            num_scalar_prefetch=1,
            grid=grid,
            in_specs=in_specs,
            out_specs=out_specs,
            scratch_shapes=scratch,
        ),
        compiler_params=pltpu.CompilerParams(vmem_limit_bytes=VMEM_LIMIT),
        cost_estimate=pl.CostEstimate(flops=flops, bytes_accessed=sum(sizes), transcendentals=0),
        name=name,
    )(info, *operands)


def shape_of(*dims, dtype=jnp.bfloat16):
    return jax.ShapeDtypeStruct(dims, dtype)


def row_block(array):
    return pl.BlockSpec((ROW_TILE, array.shape[1]), lambda i, info: (i, 0))


def whole(array):
    return pl.BlockSpec(array.shape, lambda i, info: (0,) * len(array.shape))


def norm_scale(values):
    return lax.rsqrt(jnp.mean(values * values, axis=-1, keepdims=True) + epsilon)


def partner(position, step):
    if step == 1:
        return position + 1 - 2 * (position % 2)
    if step == 2:
        return position + 2 - 4 * (position // 2)
    return 3 - position


def greet(places):
    barrier = pltpu.get_barrier_semaphore()
    for device in places:
        pl.semaphore_signal(barrier, inc=1, device_id=device, device_id_type=pl.DeviceIdType.MESH)
    pl.semaphore_wait(barrier, len(places))


def remote_copy(source, target, send_sem, recv_sem, device):
    return pltpu.make_async_remote_copy(
        src_ref=source,
        dst_ref=target,
        send_sem=send_sem,
        recv_sem=recv_sem,
        device_id=device,
        device_id_type=pl.DeviceIdType.MESH,
    )


def project_kernel(
    x,
    gain,
    w_query,
    w_key,
    w_value,
    cosine,
    sine,
    cotangent,
    normed,
    part_0,
    part_1,
    part_2,
    part_3,
    cotangent_x,
    heads,
    send_sem,
    recv_sem,
):
    dp_index, place, core = (lax.axis_index(name) for name in ("dp", "seq", "tensor"))
    rows = x.shape[0]
    half = pl.ds(pl.multiple_of(core * (rows // 2), rows // 2), rows // 2)
    peers = [{"seq": partner(place, d)} for d in (1, 2, 3)]
    beside, across = {"dp": partner(dp_index, 1)}, {"tensor": 1 - core}
    greet([*peers, beside, across])
    beside_copy = remote_copy(
        cotangent.at[half], cotangent_x.at[half], send_sem.at[0], recv_sem.at[0], beside
    )
    across_copy = remote_copy(
        cotangent_x.at[half], cotangent_x.at[half], send_sem.at[1], recv_sem.at[1], across
    )
    beside_copy.start()
    copies = []
    for block in range(rows // ROW_TILE):
        tile = pl.ds(block * ROW_TILE, ROW_TILE)
        inputs = x[tile, :].astype(jnp.float32)
        low = (inputs * norm_scale(inputs) * gain[...]).astype(jnp.bfloat16)
        normed[tile, :] = low
        table = pl.ds(pl.multiple_of(place * rows + block * ROW_TILE, ROW_TILE), ROW_TILE)
        cos_part, sin_part = cosine[table, :HD], sine[table, :HD]

        def turned(part, cos_part=cos_part, sin_part=sin_part):
            swapped = jnp.concatenate([part[:, HD // 2 :], part[:, : HD // 2]], axis=1)
            return (part * cos_part + swapped * sin_part).astype(jnp.bfloat16)

        value = dot_plain(low, w_value[...])
        for head in range(4):
            heads[head, tile, 3 * HD :] = value[:, head * HD : (head + 1) * HD].astype(jnp.bfloat16)
        key = dot_plain(low, w_key[...])
        for head in range(4):
            heads[head, tile, 2 * HD : 3 * HD] = turned(key[:, head * HD : (head + 1) * HD])
        query = dot_plain(low, w_query[...])
        for head in range(4):
            first = 2 * head * HD
            heads[head, tile, :HD] = turned(query[:, first : first + HD])
            heads[head, tile, HD : 2 * HD] = turned(query[:, first + HD : first + 2 * HD])
        for d, out in ((1, part_1), (2, part_2), (3, part_3)):
            index = 2 + 3 * block + d - 1
            copy = remote_copy(
                heads.at[partner(place, d), tile],
                out.at[tile],
                send_sem.at[index],
                recv_sem.at[index],
                peers[d - 1],
            )
            copy.start()
            copies.append(copy)
    part_0[...] = heads[place]
    beside_copy.wait()
    across_copy.start()
    across_copy.wait()
    for copy in copies:
        copy.wait()


def project(x, gain, w_query, w_key, w_value, cosine, sine, cotangent):
    rows, width = x.shape
    count = 2 + 3 * (rows // ROW_TILE)
    flops = 2 * rows * width * (w_query.shape[1] + 2 * w_key.shape[1])
    return pl.pallas_call(
        project_kernel,
        out_shape=(shape_of(rows, width),) + (shape_of(rows, 4 * HD),) * 4 + (shape_of(rows, width),),
        in_specs=[IN_VMEM] * 7 + [pl.BlockSpec(memory_space=pl.ANY)],
        out_specs=(IN_VMEM,) * 5 + (pl.BlockSpec(memory_space=pl.ANY),),
        scratch_shapes=[
            pltpu.VMEM((4, rows, 4 * HD), jnp.bfloat16),
            pltpu.SemaphoreType.DMA((count,)),
            pltpu.SemaphoreType.DMA((count,)),
        ],
        compiler_params=pltpu.CompilerParams(
            collective_id=0, has_side_effects=True, vmem_limit_bytes=VMEM_LIMIT
        ),
        cost_estimate=pl.CostEstimate(flops=flops, bytes_accessed=16 * MEBI, transcendentals=0),
        name="project",
    )(x, gain, w_query, w_key, w_value, cosine, sine, cotangent)


def middle_kernel(
    ends,
    head_0,
    head_1,
    head_2,
    head_3,
    x,
    gain,
    cotangent,
    normed_one,
    w_out_far,
    w_gate_far,
    w_up_far,
    w_down_far,
    merged,
    normed,
    hidden,
    grad_gate,
    grad_up,
    hidden_x,
    gate_x,
    gate_y,
    up_y,
    normed_x,
    normed_y,
    shards,
    grad_low,
    grad_middle,
    gain_sum,
    back_0,
    back_1,
    back_2,
    back_3,
    result,
    w_out,
    w_gate,
    w_up,
    w_down,
    arrived,
    heads,
    part,
    other,
    grad_part,
    grad_other,
    down_part,
    down_other,
    load_sem,
    send_sem,
    recv_sem,
):
    dp_index, place, core = (lax.axis_index(name) for name in ("dp", "seq", "tensor"))
    along_x, along_y = dp_index % 2, dp_index // 2
    rows, width = x.shape
    units = w_gate.shape[1]
    half_rows = rows // 2
    half = pl.ds(pl.multiple_of(core * half_rows, half_rows), half_rows)
    peers = [{"seq": partner(place, d)} for d in (1, 2, 3)]
    over_x, over_y = {"dp": partner(dp_index, 1)}, {"dp": partner(dp_index, 2)}
    across = {"tensor": 1 - core}
    greet([*peers, over_x, over_y, across])

    used = []

    def send(source, target, device):
        index = len(used)
        copy = remote_copy(source, target, send_sem.at[index], recv_sem.at[index], device)
        copy.start()
        used.append(copy)
        return copy

    loads = [
        pltpu.make_async_copy(source, target, load_sem.at[index])
        for index, (source, target) in enumerate(
            ((w_out_far, w_out), (w_gate_far, w_gate), (w_up_far, w_up), (w_down_far, w_down))
        )
    ]
    head_copies = [
        send(source, arrived.at[d], peers[d])
        for d, source in enumerate((head_1, head_2, head_3))
    ]
    for load in loads:
        load.start()
    heads[place] = head_0[...]
    for load in loads:
        load.wait()
    for d, copy in enumerate(head_copies):
        copy.wait()
        heads[partner(place, d + 1)] = arrived[d]

    shard_near = send(normed_one.at[half], shards.at[0, half], peers[0])
    shard_far = send(normed_one.at[half], shards.at[1, half], peers[1])

    for head in range(4):
        merged[:, 2 * head * HD : 2 * (head + 1) * HD] = heads[head]
    tiles = [pl.ds(block * ROW_TILE, ROW_TILE) for block in range(rows // ROW_TILE)]
    part_copies = []
    for tile in tiles:
        part[tile, :] = dot_plain(merged[tile, :], w_out[...]).astype(jnp.bfloat16)
        part_copies.append(send(part.at[tile], other.at[tile], across))

    def middle_rows(tile):
        return x[tile, :].astype(jnp.float32) + (
            part[tile, :].astype(jnp.float32) + other[tile, :].astype(jnp.float32)
        )

    for tile, copy in zip(tiles, part_copies, strict=True):
        copy.wait()
        middle = middle_rows(tile)
        normed[tile, :] = (middle * norm_scale(middle) * gain[...]).astype(jnp.bfloat16)
    normed_copies = [
        send(normed.at[half], normed_x.at[half], over_x),
        send(normed.at[half], normed_y.at[half], over_y),
    ]

    unit_tile = units // 4

    def unit_step(index, nothing):
        columns = pl.ds(pl.multiple_of(index * unit_tile, unit_tile), unit_tile)
        inner = pl.ds(pl.multiple_of((index % 2) * unit_tile, unit_tile), unit_tile)
        low = normed[...]
        gate, up = dot_plain(low, w_gate[:, columns]), dot_plain(low, w_up[:, columns])
        back = times_transpose(cotangent[...], w_down[columns, :])
        sigma = jax.nn.sigmoid(gate)
        swish = gate * sigma
        hidden[index // 2, :, inner] = (swish * up).astype(jnp.bfloat16)
        grad_gate[index] = (back * up * sigma * (1.0 + gate * (1.0 - sigma))).astype(jnp.bfloat16)
        grad_up[index // 2, :, inner] = (back * swish).astype(jnp.bfloat16)
        return nothing

    lax.fori_loop(0, 4, unit_step, 0)
    late = [
        send(hidden.at[1 - along_x], hidden_x, over_x),
        send(grad_up.at[1 - along_y], up_y, over_y),
        send(grad_gate.at[1 - along_x], gate_x, over_x),
        send(grad_gate.at[3 - along_y], gate_y, over_y),
    ]
    shard_near.wait()
    late.append(send(shards.at[0, half], shards.at[0, half], across))

    width_tile = width // 3
    grad_copies = []
    for index in range(3):
        columns = pl.ds(index * width_tile, width_tile)
        total = None
        for quarter in range(4):
            inner = pl.ds(quarter * unit_tile, unit_tile)
            term = times_transpose(grad_gate[quarter], w_gate[columns, inner])
            total = term if total is None else total + term
        for side in range(2):
            inner = pl.ds(side * 2 * unit_tile, 2 * unit_tile)
            total = total + times_transpose(grad_up[side], w_up[columns, inner])
        grad_part[:, columns] = total.astype(jnp.bfloat16)
        grad_copies.append(send(grad_part.at[:, columns], grad_other.at[:, columns], across))
    for copy, landed in zip(normed_copies, (normed_x, normed_y), strict=True):
        copy.wait()
        late.append(send(landed.at[half], landed.at[half], across))
    for copy in grad_copies:
        copy.wait()

    for block, tile in enumerate(tiles):
        middle = middle_rows(tile)
        inverse = norm_scale(middle)
        unit_rows = middle * inverse
        grad_normed = grad_part[tile, :].astype(jnp.float32) + grad_other[tile, :].astype(
            jnp.float32
        )
        gain_term = jnp.sum(grad_normed * unit_rows, axis=0, keepdims=True)
        gain_sum[...] = gain_term if block == 0 else gain_sum[...] + gain_term
        scaled = grad_normed * gain[...]
        total = cotangent[tile, :].astype(jnp.float32) + inverse * (
            scaled - unit_rows * jnp.mean(scaled * unit_rows, axis=-1, keepdims=True)
        )
        grad_middle[tile, :] = total
        low = total.astype(jnp.bfloat16)
        grad_low[tile, :] = low
        row_ids = lax.broadcasted_iota(jnp.int32, (ROW_TILE, 1), 0) + (
            place * rows + block * ROW_TILE
        )
        back = jnp.where(row_ids < ends[3], times_transpose(low, w_out[...]), 0.0)
        for head in range(4):
            heads[head, tile, :] = back[:, 2 * head * HD : 2 * (head + 1) * HD].astype(jnp.bfloat16)
    for d, out in enumerate((back_1, back_2, back_3)):
        late.append(send(heads.at[partner(place, d + 1)], out, peers[d]))
    back_0[...] = heads[place]
    shard_far.wait()
    late.append(send(shards.at[1, half], shards.at[1, half], across))
    shard_both = send(shards.at[1, half], shards.at[2, half], peers[0])

    down_copies = []
    for index in range(3):
        columns = pl.ds(index * width_tile, width_tile)
        total = dot_plain(hidden[0], w_down[: units // 2, columns]) + dot_plain(
            hidden[1], w_down[units // 2 :, columns]
        )
        down_part[:, columns] = total.astype(jnp.bfloat16)
        down_copies.append(send(down_part.at[:, columns], down_other.at[:, columns], across))
    for copy in down_copies:
        copy.wait()
    for tile in tiles:
        result[tile, :] = (
            middle_rows(tile)
            + (down_part[tile, :].astype(jnp.float32) + down_other[tile, :].astype(jnp.float32))
        ).astype(jnp.bfloat16)
    shard_both.wait()
    late.append(send(shards.at[2, half], shards.at[2, half], across))
    for copy in late:
        copy.wait()


def middle(ends, head_parts, x, gain, cotangent, normed_one, w_out, w_gate, w_up, w_down):
    rows, width = x.shape
    units = w_gate.shape[1]
    wide, message = shape_of(rows, width), shape_of(rows, 2 * HD)
    outs = (
        (shape_of(rows, w_out.shape[0]), IN_VMEM),
        (wide, IN_VMEM),
        (shape_of(2, rows, units // 2), IN_VMEM),
        (shape_of(4, rows, units // 4), IN_VMEM),
        (shape_of(2, rows, units // 2), IN_VMEM),
        (shape_of(rows, units // 2), IN_ANY),
        (shape_of(rows, units // 4), IN_ANY),
        (shape_of(rows, units // 4), IN_ANY),
        (shape_of(rows, units // 2), IN_ANY),
        (wide, IN_ANY),
        (wide, IN_ANY),
        (shape_of(3, rows, width), IN_ANY),
        (wide, IN_VMEM),
        (shape_of(rows, width, dtype=jnp.float32), IN_VMEM),
        (shape_of(1, width, dtype=jnp.float32), IN_VMEM),
        (message, IN_VMEM),
        (message, IN_ANY),
        (message, IN_ANY),
        (message, IN_ANY),
        (wide, IN_VMEM),
    )
    low = [pltpu.VMEM((rows, width), jnp.bfloat16)]
    count = 30
    return pl.pallas_call(
        middle_kernel,
        out_shape=tuple(a for a, _ in outs),
        in_specs=[pl.BlockSpec(memory_space=pltpu.SMEM)]
        + [IN_VMEM]
        + [IN_ANY] * 3
        + [IN_VMEM] * 3
        + [IN_ANY] * 5,
        out_specs=tuple(b for _, b in outs),
        scratch_shapes=[
            pltpu.VMEM(w_out.shape, jnp.bfloat16),
            pltpu.VMEM(w_gate.shape, jnp.bfloat16),
            pltpu.VMEM(w_up.shape, jnp.bfloat16),
            pltpu.VMEM(w_down.shape, jnp.bfloat16),
            pltpu.VMEM((3, rows, 2 * HD), jnp.bfloat16),
            pltpu.VMEM((4, rows, 2 * HD), jnp.bfloat16),
            *low * 6,
            pltpu.SemaphoreType.DMA((4,)),
            pltpu.SemaphoreType.DMA((count,)),
            pltpu.SemaphoreType.DMA((count,)),
        ],
        compiler_params=pltpu.CompilerParams(
            collective_id=1, has_side_effects=True, vmem_limit_bytes=62 * MEBI
        ),
        cost_estimate=pl.CostEstimate(
            flops=12 * rows * width * units, bytes_accessed=48 * MEBI, transcendentals=0
        ),
        name="middle",
    )(ends, *head_parts, x, gain, cotangent, normed_one, w_out, w_gate, w_up, w_down)


def input_back_kernel(
    info, part_0, part_1, part_2, part_3, w_query, w_key, w_value, result, heads, query, key, value
):
    for step, part in enumerate((part_0, part_1, part_2, part_3)):
        heads[info[4] ^ step] = part[...]
    for head in range(4):
        query[:, 2 * head * HD : 2 * (head + 1) * HD] = heads[head, :, : 2 * HD]
        key[:, head * HD : (head + 1) * HD] = heads[head, :, 2 * HD : 3 * HD]
        value[:, head * HD : (head + 1) * HD] = heads[head, :, 3 * HD :]
    result[...] = (
        times_transpose(query[...], w_query[...])
        + times_transpose(key[...], w_key[...])
        + times_transpose(value[...], w_value[...])
    ).astype(jnp.bfloat16)


def input_back(info, parts, w_query, w_key, w_value):
    rows, width = parts[0].shape[0], w_query.shape[0]
    out = shape_of(rows, width)
    weights = (w_query, w_key, w_value)
    return local_call(
        input_back_kernel,
        "input_back",
        info,
        (*parts, *weights),
        [row_block(a) for a in parts] + [whole(a) for a in weights],
        (out,),
        [row_block(out)],
        (rows // ROW_TILE,),
        [pltpu.VMEM((4, ROW_TILE, 4 * HD), jnp.bfloat16)]
        + [pltpu.VMEM((ROW_TILE, a.shape[1]), jnp.bfloat16) for a in weights],
        2 * rows * sum(a.size for a in weights),
    )[0]


def finish_kernel(info, x, grad_part, grad_other, grad_middle, gain, result, gain_sum):
    step = pl.program_id(0)
    inputs = x[...].astype(jnp.float32)
    inverse = norm_scale(inputs)
    normed = inputs * inverse
    grad_normed = grad_part[...].astype(jnp.float32) + grad_other[...].astype(jnp.float32)
    gain_term = jnp.sum(grad_normed * normed, axis=0, keepdims=True)

    @pl.when(step == 0)
    def _():
        gain_sum[...] = gain_term

    @pl.when(step > 0)
    def _():
        gain_sum[...] += gain_term

    scaled = grad_normed * gain[...]
    result[...] = (
        grad_middle[...]
        + inverse * (scaled - normed * jnp.mean(scaled * normed, axis=-1, keepdims=True))
    ).astype(jnp.bfloat16)


def finish(info, x, grad_part, grad_other, grad_middle, gain):
    rows, width = x.shape
    operands = (x, grad_part, grad_other, grad_middle, gain)
    outs = (shape_of(rows, width), shape_of(1, width, dtype=jnp.float32))
    return local_call(
        finish_kernel,
        "finish",
        info,
        operands,
        [row_block(a) for a in operands[:4]] + [whole(gain)],
        outs,
        [row_block(outs[0]), whole(outs[1])],
        (rows // ROW_TILE,),
    )


def outer_blocks(info, name, lefts, rights, chosen):
    width = lefts[0].shape[1]
    block_rows = width // 4
    columns = rights[0][1][-1]
    count = len(lefts)

    def kernel(info, *refs):
        total = None
        for left, right in zip(refs[:count], refs[count : 2 * count], strict=True):
            right_value = right[0] if len(right.shape) == 3 else right[...]
            term = outer_sum(left[...], right_value)
            total = term if total is None else total + term
        refs[-1][0] = total.astype(jnp.bfloat16)

    out = shape_of(2, block_rows, columns)
    return local_call(
        kernel,
        name,
        info,
        (*lefts, *(a for a, _, _ in rights)),
        [
            pl.BlockSpec((a.shape[0], block_rows), lambda k, info: (0, chosen(k, info)))
            for a in lefts
        ]
        + [
            pl.BlockSpec(block, lambda k, info, index=index: index(info))
            for _, block, index in rights
        ],
        (out,),
        [pl.BlockSpec((1, block_rows, columns), lambda k, info: (k, 0, 0))],
        (2,),
        (),
        4 * sum(a.shape[0] for a in lefts) * block_rows * columns,
    )[0]


def attention_forward_kernel(
    info, part_0, part_1, part_2, part_3, heads, keys, values, out_0, out_1, out_2, out_3, exact, lse, low
):
    parts, outs = (part_0, part_1, part_2, part_3), (out_0, out_1, out_2, out_3)
    rows_each = part_0.shape[0]
    total = rows_each * len(parts)
    ends = [info[index] for index in range(4)]
    place = info[4]
    heads[...] = jnp.zeros_like(heads)
    keys[...] = jnp.zeros_like(keys)
    values[...] = jnp.zeros_like(values)
    for step, part in enumerate(parts):
        rows = pl.ds(pl.multiple_of((place ^ step) * rows_each, rows_each), rows_each)
        heads[0, rows, :HD] = part[:, :HD]
        heads[1, rows, :HD] = part[:, HD : 2 * HD]
        keys[rows, :HD] = part[:, 2 * HD : 3 * HD]
        values[rows, :HD] = part[:, 3 * HD :]
    scale = HD ** (-0.5) * LOG2E

    def query_step(index, nothing):
        first = pl.multiple_of(index * QUERY_TILE, QUERY_TILE)
        tile = pl.ds(first, QUERY_TILE)
        queries = jnp.concatenate([heads[0, tile, :], heads[1, tile, :]], axis=0)
        row_ids = lax.broadcasted_iota(jnp.int32, (2 * QUERY_TILE, 1), 0) % QUERY_TILE + first
        starts = doc_start(ends, row_ids)
        low_tile = doc_start(ends, first) // KEY_TILE
        high_tile = (first + QUERY_TILE - 1) // KEY_TILE + 1

        def key_step(key_index, state):
            row_max, row_sum, summed = state
            first_key = pl.multiple_of(key_index * KEY_TILE, KEY_TILE)
            key_rows = pl.ds(first_key, KEY_TILE)
            scores = scale * lax.dot_general(
                queries, keys[key_rows, :], (((1,), (1,)), ((), ())), preferred_element_type=jnp.float32
            )
            columns = lax.broadcasted_iota(jnp.int32, (1, KEY_TILE), 1) + first_key
            scores = jnp.where((columns >= starts) & (columns <= row_ids), scores, masked_score)
            new_max = jnp.maximum(row_max, jnp.max(scores, axis=1, keepdims=True))
            probs = jnp.exp2(scores - new_max)
            shrink = jnp.exp2(row_max - new_max)
            row_sum = row_sum * shrink + jnp.sum(probs, axis=1, keepdims=True)
            summed = summed * shrink + jnp.dot(
                probs.astype(jnp.bfloat16), values[key_rows, :], preferred_element_type=jnp.float32
            )
            return (new_max, row_sum, summed)

        row_max, row_sum, summed = lax.fori_loop(
            low_tile,
            high_tile,
            key_step,
            (
                jnp.full((2 * QUERY_TILE, 1), masked_score, jnp.float32),
                jnp.zeros((2 * QUERY_TILE, 1), jnp.float32),
                jnp.zeros((2 * QUERY_TILE, PAD), jnp.float32),
            ),
        )
        result = jnp.where(row_ids < ends[-1], summed / row_sum, 0.0)
        total_log = row_max + jnp.log(row_sum) * LOG2E
        total_row = jnp.transpose(jnp.broadcast_to(total_log, (2 * QUERY_TILE, PAD)))[:1, :]
        for head in range(2):
            mine = result[head * QUERY_TILE : (head + 1) * QUERY_TILE]
            exact[head, tile, :] = mine
            low[tile, head * HD : (head + 1) * HD] = mine[:, :HD].astype(jnp.bfloat16)
            lse[head : head + 1, tile] = total_row[:, head * QUERY_TILE : (head + 1) * QUERY_TILE]
        return nothing

    lax.fori_loop(0, total // QUERY_TILE, query_step, 0)
    for step, out in enumerate(outs):
        rows = pl.ds(pl.multiple_of((place ^ step) * rows_each, rows_each), rows_each)
        out[...] = low[rows, :]


def attention_forward(info, parts):
    rows_each = parts[0].shape[0]
    total = rows_each * len(parts)
    wide = jax.ShapeDtypeStruct((total, PAD), jnp.bfloat16)
    return pl.pallas_call(
        attention_forward_kernel,
        out_shape=(
            jax.ShapeDtypeStruct((2, total, PAD), jnp.bfloat16),
            wide,
            wide,
            *(jax.ShapeDtypeStruct((rows_each, 2 * HD), jnp.bfloat16) for _ in parts),
            jax.ShapeDtypeStruct((2, total, PAD), jnp.float32),
            jax.ShapeDtypeStruct((2, total), jnp.float32),
        ),
        in_specs=[pl.BlockSpec(memory_space=pltpu.SMEM)]
        + [pl.BlockSpec(memory_space=pltpu.VMEM)] * len(parts),
        out_specs=(pl.BlockSpec(memory_space=pltpu.VMEM),) * 9,
        scratch_shapes=[pltpu.VMEM((total, 2 * HD), jnp.bfloat16)],
        compiler_params=pltpu.CompilerParams(vmem_limit_bytes=48 * MEBI),
        cost_estimate=pl.CostEstimate(
            flops=4 * 2 * total * total * PAD // 2, bytes_accessed=8 * MEBI, transcendentals=total * total
        ),
        name="attention_forward",
    )(info, *parts)


def attention_backward_kernel(
    info,
    grad_0,
    grad_1,
    grad_2,
    grad_3,
    heads,
    keys,
    values,
    exact,
    lse,
    cosine,
    sine,
    back_0,
    back_1,
    back_2,
    back_3,
    grad_heads,
    grad_query,
    grad_key,
    grad_value,
):
    grads, backs = (grad_0, grad_1, grad_2, grad_3), (back_0, back_1, back_2, back_3)
    rows_each = grad_0.shape[0]
    total = rows_each * len(grads)
    ends = [info[index] for index in range(4)]
    place = info[4]
    grad_heads[...] = jnp.zeros_like(grad_heads)
    grad_key[...] = jnp.zeros_like(grad_key)
    grad_value[...] = jnp.zeros_like(grad_value)
    for step, grad in enumerate(grads):
        rows = pl.ds(pl.multiple_of((place ^ step) * rows_each, rows_each), rows_each)
        grad_heads[0, rows, :HD] = grad[:, :HD]
        grad_heads[1, rows, :HD] = grad[:, HD:]
    scale = HD ** (-0.5) * LOG2E

    def query_step(index, nothing):
        first = pl.multiple_of(index * QUERY_TILE, QUERY_TILE)
        tile = pl.ds(first, QUERY_TILE)
        queries = jnp.concatenate([heads[0, tile, :], heads[1, tile, :]], axis=0)
        grad_rows = jnp.concatenate([grad_heads[0, tile, :], grad_heads[1, tile, :]], axis=0)
        exact_rows = jnp.concatenate([exact[0, tile, :], exact[1, tile, :]], axis=0)
        delta = jnp.sum(
            jnp.transpose(grad_rows.astype(jnp.float32) * exact_rows), axis=0, keepdims=True
        )
        log_row = jnp.concatenate([lse[0:1, tile], lse[1:2, tile]], axis=1)
        row_ids = lax.broadcasted_iota(jnp.int32, (1, 2 * QUERY_TILE), 1) % QUERY_TILE + first
        starts = doc_start(ends, row_ids)
        low_tile = doc_start(ends, first) // KEY_TILE
        high_tile = (first + QUERY_TILE - 1) // KEY_TILE + 1

        def key_step(key_index, summed):
            first_key = pl.multiple_of(key_index * KEY_TILE, KEY_TILE)
            key_rows = pl.ds(first_key, KEY_TILE)
            key_part, value_part = keys[key_rows, :], values[key_rows, :]
            scores = scale * times_transpose(key_part, queries)
            columns = lax.broadcasted_iota(jnp.int32, (KEY_TILE, 1), 0) + first_key
            probs = jnp.where(
                (columns >= starts) & (columns <= row_ids), jnp.exp2(scores - log_row), 0.0
            )
            grad_scores = (probs * (times_transpose(value_part, grad_rows) - delta)).astype(
                jnp.bfloat16
            )
            grad_value[key_rows, :] += jnp.dot(
                probs.astype(jnp.bfloat16), grad_rows, preferred_element_type=jnp.float32
            )
            grad_key[key_rows, :] += jnp.dot(
                grad_scores, queries, preferred_element_type=jnp.float32
            )
            return summed + outer_sum(grad_scores, key_part)

        summed = lax.fori_loop(
            low_tile, high_tile, key_step, jnp.zeros((2 * QUERY_TILE, PAD), jnp.float32)
        )
        grad_query[0, tile, :] = summed[:QUERY_TILE]
        grad_query[1, tile, :] = summed[QUERY_TILE:]
        return nothing

    lax.fori_loop(0, total // QUERY_TILE, query_step, 0)
    for step, back in enumerate(backs):
        rows = pl.ds(pl.multiple_of((place ^ step) * rows_each, rows_each), rows_each)
        cos_part, sin_part = cosine[rows, :], sine[rows, :]

        def turned_back(part):
            lanes = lax.broadcasted_iota(jnp.int32, part.shape, 1)
            swapped = jnp.where(
                lanes < HD // 2, pltpu.roll(part, PAD - HD // 2, 1), pltpu.roll(part, HD // 2, 1)
            )
            turned = (part * cos_part - swapped * sin_part) * HD ** (-0.5)
            return turned[:, :HD].astype(jnp.bfloat16)

        back[:, :HD] = turned_back(grad_query[0, rows, :])
        back[:, HD : 2 * HD] = turned_back(grad_query[1, rows, :])
        back[:, 2 * HD : 3 * HD] = turned_back(grad_key[rows, :])
        back[:, 3 * HD :] = grad_value[rows, :HD].astype(jnp.bfloat16)


def attention_backward(info, grads, kept):
    rows_each = grads[0].shape[0]
    total = rows_each * len(grads)
    return pl.pallas_call(
        attention_backward_kernel,
        out_shape=tuple(jax.ShapeDtypeStruct((rows_each, 4 * HD), jnp.bfloat16) for _ in grads),
        in_specs=[pl.BlockSpec(memory_space=pltpu.SMEM)]
        + [pl.BlockSpec(memory_space=pltpu.VMEM)] * (len(grads) + len(kept)),
        out_specs=(pl.BlockSpec(memory_space=pltpu.VMEM),) * len(grads),
        scratch_shapes=[
            pltpu.VMEM((2, total, PAD), jnp.bfloat16),
            pltpu.VMEM((2, total, PAD), jnp.float32),
            pltpu.VMEM((total, PAD), jnp.float32),
            pltpu.VMEM((total, PAD), jnp.float32),
        ],
        compiler_params=pltpu.CompilerParams(vmem_limit_bytes=48 * MEBI),
        cost_estimate=pl.CostEstimate(
            flops=10 * 2 * total * total * PAD // 2, bytes_accessed=8 * MEBI, transcendentals=total * total
        ),
        name="attention_backward",
    )(info, *grads, *kept)


def swap(array, axis, bit):
    return lax.ppermute(array, axis, [(i, i ^ bit) for i in range(lax.axis_size(axis))])


def pick(array, index, dim):
    return lax.dynamic_index_in_dim(array, index, dim, keepdims=False)


def summed(kept, arrived):
    return kept.astype(jnp.float32) + arrived.astype(jnp.float32)


def local_paired(
    hidden_in,
    lengths,
    attn_gain,
    w_query,
    w_key,
    w_value,
    w_out,
    mlp_gain,
    w_gate,
    w_up,
    w_down,
    out_grad,
):
    rows, width = hidden_in.shape[1], hidden_in.shape[2]
    dp_index, place, core = (lax.axis_index(name) for name in ("dp", "seq", "tensor"))
    along_x, along_y = dp_index % 2, dp_index // 2
    total_rows = 4 * rows
    x, cotangent = hidden_in[0], out_grad[0]
    gain_one, gain_two = attn_gain[None], mlp_gain[None]
    info = jnp.concatenate(
        [jnp.cumsum(lengths[0]), jnp.stack([place, along_x, along_y, core])]
    ).astype(jnp.int32)

    def other_core(array):
        return swap(array, "tensor", 1)

    def over_x(array):
        return swap(array, "dp", 1)

    def over_y(array):
        return swap(array, "dp", 2)

    def dealt(parts):
        return [parts[0]] + [swap(parts[d], "seq", d) for d in range(1, 4)]

    _, _, offsets, _ = doc_layout(lengths[0], 0, total_rows)
    cosine, sine = rope_tables(offsets)
    cosine, sine = cosine[:, 0], sine[:, 0]
    spare = PAD - HD
    cosine = jnp.pad(jnp.concatenate([cosine, cosine], axis=1), ((0, 0), (0, spare)))
    sine = jnp.pad(jnp.concatenate([-sine, sine], axis=1), ((0, 0), (0, spare)))

    attn_input, *sent, cotangent_x = project(
        x, gain_one, w_query, w_key, w_value, cosine, sine, cotangent
    )
    forward = attention_forward(info, sent)
    kept = forward[:3] + forward[7:]
    (
        attn_heads,
        mlp_input,
        hidden,
        grad_gate,
        grad_up,
        hidden_x,
        gate_x,
        gate_y,
        up_y,
        mlp_x,
        mlp_y,
        input_shards,
        grad_low,
        grad_middle,
        mlp_gain_part,
        grad_0,
        grad_1,
        grad_2,
        grad_3,
        result,
    ) = middle(
        info, forward[3:7], x, gain_two, cotangent, attn_input, w_out, w_gate, w_up, w_down
    )
    grad_dealt = (grad_0, grad_1, grad_2, grad_3)

    def y_blocks(flip):
        return lambda k, info: 2 * (info[6] ^ flip) + k

    def x_blocks(flip):
        return lambda k, info: 2 * k + (info[5] ^ flip)

    def halved(kept_rows, arrived, steps):
        total = summed(kept_rows, arrived)
        for step in steps:
            axis, bit, here, dim = step
            total = total.astype(jnp.bfloat16)
            total = summed(pick(total, here, dim), swap(pick(total, 1 - here, dim), axis, bit))
        return total

    near_step = ("seq", 1, place % 2, 2)
    far_step = ("seq", 2, place // 2, 1)

    def all_tokens(array):
        return (array, array.shape, lambda info: (0, 0))

    def unit_gradient(name, lefts, mine, index, arrived, blocks, reduce_over, share_with, here):
        columns = mine.shape[2]
        rights = (
            (mine, (1, rows, columns), lambda info: (index(info), 0, 0)),
            all_tokens(arrived),
        )
        away = outer_blocks(info, name + "_away", lefts, rights, blocks(1))
        stay = outer_blocks(info, name + "_stay", lefts, rights, blocks(0))
        shape = (2, 2, 2, width // 16, columns)
        total = halved(
            stay.reshape(shape), reduce_over(away).reshape(shape), (near_step, far_step)
        ).astype(jnp.bfloat16)
        own = pick(total, here, 0)
        received = share_with(pick(total, 1 - here, 0))
        return jnp.where(
            here == 0,
            jnp.concatenate([own, received], axis=1),
            jnp.concatenate([received, own], axis=1),
        ).astype(jnp.float32)

    def x_index(info):
        return info[5]

    def y_index(info):
        return info[6]

    def low_y_index(info):
        return 2 + info[6]

    grad_w_down = unit_gradient(
        "down", (cotangent, cotangent_x), hidden, x_index, hidden_x, y_blocks, over_y, over_x, along_x
    )
    grad_w_up = unit_gradient(
        "up", (mlp_input, mlp_y), grad_up, y_index, up_y, x_blocks, over_x, over_y, along_y
    )
    grad_w_gate = jnp.concatenate(
        [
            unit_gradient(
                "gate_x", (mlp_input, mlp_x), grad_gate, x_index, gate_x, y_blocks, over_y, over_x, along_x
            ),
            unit_gradient(
                "gate_y", (mlp_input, mlp_y), grad_gate, low_y_index, gate_y, x_blocks, over_x, over_y, along_y
            ),
        ],
        axis=1,
    )

    out_right = (all_tokens(attn_heads),)
    shape = (2, 2, 2, width // 16, attn_heads.shape[1])
    out_away = outer_blocks(info, "out_away", (grad_low,), out_right, x_blocks(1))
    out_stay = outer_blocks(info, "out_stay", (grad_low,), out_right, x_blocks(0))
    grad_w_out = halved(
        out_stay.reshape(shape),
        over_x(out_away).reshape(shape),
        (("dp", 2, along_y, 0), ("seq", 1, place % 2, 1), ("seq", 2, place // 2, 0)),
    )

    backs = attention_backward(info, grad_dealt, kept + (cosine, sine))
    returned = dealt(backs)
    lefts = [attn_input] + [input_shards[d] for d in range(3)]
    rights = [all_tokens(back) for back in backs]
    head_away = outer_blocks(info, "head_away", lefts, rights, x_blocks(1))
    head_stay = outer_blocks(info, "head_stay", lefts, rights, x_blocks(0))
    head_rows = halved(head_stay, over_x(head_away), (("dp", 2, along_y, 0),))
    head_rows = head_rows.astype(jnp.bfloat16).reshape(4, width // 16, 4 * HD)
    arrived = jnp.stack(dealt([pick(head_rows, place ^ d, 0) for d in range(4)]))
    heads = jnp.stack([pick(arrived, place ^ d, 0) for d in range(4)], axis=1).astype(jnp.float32)
    grad_w_query = heads[:, :, : 2 * HD].reshape(width // 16, -1)
    grad_w_key = heads[:, :, 2 * HD : 3 * HD].reshape(width // 16, -1)
    grad_w_value = heads[:, :, 3 * HD :].reshape(width // 16, -1)

    back_part = input_back(info, returned, w_query, w_key, w_value)
    grad_inputs, attn_gain_part = finish(
        info, x, back_part, other_core(back_part), grad_middle, gain_one
    )
    gains = jnp.stack([attn_gain_part, mlp_gain_part]).reshape(2, 16, width // 16)
    gains = jnp.sum(
        lax.all_to_all(jnp.moveaxis(gains, 1, 0), ("dp", "seq"), 0, 0, tiled=True), axis=0
    )
    return (
        result[None],
        grad_inputs[None],
        gains[0],
        grad_w_query,
        grad_w_key,
        grad_w_value,
        grad_w_out.T,
        gains[1],
        grad_w_gate,
        grad_w_up,
        grad_w_down.T,
    )


def solution(mesh):
    in_specs = (
        P("dp", "seq", None),
        P("dp", None),
        P(),
        P(None, "tensor"),
        P(None, "tensor"),
        P(None, "tensor"),
        P("tensor", None),
        P(),
        P(None, "tensor"),
        P(None, "tensor"),
        P("tensor", None),
        P("dp", "seq", None),
    )
    out_specs = (
        P("dp", "seq", None),
        P("dp", "seq", None),
        P(("dp", "seq")),
        P(("dp", "seq"), "tensor"),
        P(("dp", "seq"), "tensor"),
        P(("dp", "seq"), "tensor"),
        P("tensor", ("dp", "seq")),
        P(("dp", "seq")),
        P(("dp", "seq"), "tensor"),
        P(("dp", "seq"), "tensor"),
        P("tensor", ("dp", "seq")),
    )
    body = local_paired if tuple(mesh.shape[name] for name in ("dp", "seq", "tensor")) == (4, 4, 2) else local
    return jax.shard_map(body, mesh=mesh, in_specs=in_specs, out_specs=out_specs, check_vma=False)
```

```python
import jax
import jax.numpy as jnp
from jax import lax
from jax.experimental import pallas as pl
from jax.experimental.pallas import tpu as pltpu
from jax.sharding import PartitionSpec as P

HQ = 16
KV = 8
HD = 96


epsilon = 1e-05
rope_theta = 100000.0
masked_score = -1e30


def doc_layout(length_row, first_row, row_count):
    positions = first_row + jnp.arange(row_count, dtype=jnp.int32)
    doc_ends = jnp.cumsum(length_row)
    passed = (positions[:, None] >= doc_ends[None, :]).astype(jnp.int32)
    segment = jnp.sum(passed, axis=1)
    doc_start = jnp.sum(passed * length_row[None, :], axis=1)
    return (positions, segment, positions - doc_start, segment < length_row.shape[0])


def rope_tables(offsets):
    half_size = HD // 2
    inverse = rope_theta ** (-2.0 * jnp.arange(half_size, dtype=jnp.float32) / HD)
    angles = offsets.astype(jnp.float32)[:, None] * inverse[None, :]
    return (jnp.cos(angles)[:, None, :], jnp.sin(angles)[:, None, :])


def rotate(values, cosine, sine_table):
    half_size = values.shape[-1] // 2
    first_half = values[..., :half_size]
    second_half = values[..., half_size:]
    return jnp.concatenate(
        [
            first_half * cosine - second_half * sine_table,
            second_half * cosine + first_half * sine_table,
        ],
        axis=-1,
    )


def rotate_back(gradient, cosine, sine_table):
    half_size = gradient.shape[-1] // 2
    first_half = gradient[..., :half_size]
    second_half = gradient[..., half_size:]
    return jnp.concatenate(
        [
            first_half * cosine + second_half * sine_table,
            second_half * cosine - first_half * sine_table,
        ],
        axis=-1,
    )


def outer_sum(left, right):
    return lax.dot_general(
        left, right, (((0,), (0,)), ((), ())), preferred_element_type=jnp.float32
    )


def times_transpose(left, right):
    return lax.dot_general(
        left, right, (((1,), (1,)), ((), ())), preferred_element_type=jnp.float32
    )


def allowed_pairs(query_rows, query_seg, key_rows, key_seg, key_valid):
    same_doc = (
        (query_seg[:, None] == key_seg[None, :])
        & (key_rows[None, :] <= query_rows[:, None])
        & key_valid[None, :]
    )
    return same_doc | (key_rows[None, :] == query_rows[:, None])


def score_block(queries, key_part, allowed_mask):
    raw_scores = jnp.einsum("qkgd,jkd->kgqj", queries, key_part, preferred_element_type=jnp.float32)
    return jnp.where(allowed_mask[None, None], raw_scores * HD ** (-0.5), masked_score)


def backward_terms(queries, grad_heads, log_total, delta, key_part, value_part, allowed_mask):
    probs = jnp.exp(score_block(queries, key_part, allowed_mask) - log_total[..., None])
    grad_probs = jnp.einsum(
        "qkgd,jkd->kgqj", grad_heads, value_part, preferred_element_type=jnp.float32
    )
    grad_scores = (probs * (grad_probs - delta[..., None])).astype(jnp.bfloat16)
    return (probs.astype(jnp.bfloat16), grad_scores)


def block_loader(keys_all, values_all, query_info, key_info, block_rows):
    query_rows, query_seg = query_info

    def load_block(block_index):
        first_key = block_index * block_rows
        key_part = lax.dynamic_slice_in_dim(keys_all, first_key, block_rows, 0)
        value_part = lax.dynamic_slice_in_dim(values_all, first_key, block_rows, 0)
        key_rows, key_seg, key_valid = tuple(
            (lax.dynamic_slice_in_dim(member, first_key, block_rows, 0) for member in key_info)
        )
        return (
            key_part,
            value_part,
            allowed_pairs(query_rows, query_seg, key_rows, key_seg, key_valid),
        )

    return load_block


def attend_forward(queries, keys_all, values_all, query_info, key_info, block_rows):
    last_row = query_info[0][-1]
    block_count = keys_all.shape[0] // block_rows
    stat_shape = (queries.shape[1], queries.shape[2], queries.shape[0])
    load_block = block_loader(keys_all, values_all, query_info, key_info, block_rows)

    def stats_step(block_index, running):

        def stats_compute(state_in):
            row_max, row_sum = state_in
            key_part, value_part, allowed_mask = load_block(block_index)
            scores = score_block(queries, key_part, allowed_mask)
            new_max = jnp.maximum(row_max, jnp.max(scores, axis=-1))
            new_sum = row_sum * jnp.exp(row_max - new_max) + jnp.sum(
                jnp.exp(scores - new_max[..., None]), axis=-1
            )
            return (new_max, new_sum)

        return lax.cond(
            block_index * block_rows <= last_row, stats_compute, lambda state_in: state_in, running
        )

    start_stats = (
        jnp.full(stat_shape, masked_score, jnp.float32),
        jnp.zeros(stat_shape, jnp.float32),
    )
    row_max, row_sum = lax.fori_loop(0, block_count, stats_step, start_stats)
    log_total = row_max + jnp.log(row_sum)

    def output_step(block_index, running):

        def output_compute(state_in):
            kept_sum, rest_sum = state_in
            key_part, value_part, allowed_mask = load_block(block_index)
            probs = jnp.exp(score_block(queries, key_part, allowed_mask) - log_total[..., None])
            probs_low = probs.astype(jnp.bfloat16)
            rest_low = (probs - probs_low.astype(jnp.float32)).astype(jnp.bfloat16)
            kept_sum = kept_sum + jnp.einsum(
                "kgqj,jkd->qkgd", probs_low, value_part, preferred_element_type=jnp.float32
            )
            rest_sum = rest_sum + jnp.einsum(
                "kgqj,jkd->qkgd", rest_low, value_part, preferred_element_type=jnp.float32
            )
            return (kept_sum, rest_sum)

        return lax.cond(
            block_index * block_rows <= last_row, output_compute, lambda state_in: state_in, running
        )

    zero_out = jnp.zeros(queries.shape, jnp.float32)
    kept_sum, rest_sum = lax.fori_loop(0, block_count, output_step, (zero_out, zero_out))
    return (log_total, kept_sum, kept_sum + rest_sum)


def attend_backward(
    queries, grad_heads, log_total, delta, keys_all, values_all, query_info, key_info, block_rows
):
    last_row = query_info[0][-1]
    block_count = keys_all.shape[0] // block_rows
    key_width = keys_all.shape[1] * keys_all.shape[2]
    load_block = block_loader(keys_all, values_all, query_info, key_info, block_rows)

    def grad_step(running, block_index):

        def grad_compute(state_in):
            key_part, value_part, allowed_mask = load_block(block_index)
            probs_low, grad_scores = backward_terms(
                queries, grad_heads, log_total, delta, key_part, value_part, allowed_mask
            )
            grad_query = state_in + jnp.einsum(
                "kgqj,jkd->qkgd", grad_scores, key_part, preferred_element_type=jnp.float32
            )
            key_terms = ()
            grad_key = jnp.einsum(
                "kgqj,qkgd->jkd", grad_scores, queries, preferred_element_type=jnp.float32
            )
            grad_value = jnp.einsum(
                "kgqj,qkgd->jkd", probs_low, grad_heads, preferred_element_type=jnp.float32
            )
            key_terms = (
                grad_key.reshape(block_rows, key_width),
                grad_value.reshape(block_rows, key_width),
            )
            return (grad_query, key_terms)

        def skipped(state_in):
            key_terms = ()
            zero_block = jnp.zeros((block_rows, key_width), jnp.float32)
            key_terms = (zero_block, zero_block)
            return (state_in, key_terms)

        return lax.cond(block_index * block_rows <= last_row, grad_compute, skipped, running)

    grad_query, key_terms = lax.scan(
        grad_step, jnp.zeros(queries.shape, jnp.float32), jnp.arange(block_count, dtype=jnp.int32)
    )
    key_terms = tuple((member.reshape(block_count * block_rows, key_width) for member in key_terms))
    return (grad_query, key_terms)


def local(
    hidden_in,
    lengths,
    attn_gain,
    w_query,
    w_key,
    w_value,
    w_out,
    mlp_gain,
    w_gate,
    w_up,
    w_down,
    out_grad,
):
    seq_count = hidden_in.shape[0]
    tok_rows = hidden_in.shape[1]
    width = hidden_in.shape[2]
    row_total = seq_count * tok_rows
    seq_total = tok_rows * lax.axis_size("seq")
    first_row = lax.axis_index("seq") * tok_rows
    half_rows = row_total // lax.axis_size("tensor")
    half_start = lax.axis_index("tensor") * half_rows
    block_rows = min(512, seq_total)
    kv_local = w_key.shape[1] // HD
    group_size = HQ // KV
    heads_local = kv_local * group_size

    def own_half(array_in):
        return lax.dynamic_slice_in_dim(array_in, half_start, half_rows, 0)

    inputs = hidden_in.reshape(row_total, width).astype(jnp.float32)
    query_rows, query_seg, query_offsets, query_valid = jax.vmap(
        lambda length_row: doc_layout(length_row, first_row, tok_rows)
    )(lengths)
    key_layout = jax.vmap(lambda length_row: doc_layout(length_row, 0, seq_total))(lengths)
    cosine, sine_table = rope_tables(query_offsets.reshape(row_total))
    valid_rows = query_valid.reshape(row_total).astype(jnp.float32)[:, None]
    inverse_one = lax.rsqrt(jnp.mean(inputs * inputs, axis=-1, keepdims=True) + epsilon)
    normed_one = inputs * inverse_one
    attn_input = (normed_one * attn_gain).astype(jnp.bfloat16)
    query_raw = jnp.dot(attn_input, w_query, preferred_element_type=jnp.float32).reshape(
        row_total, heads_local, HD
    )
    key_raw = jnp.dot(attn_input, w_key, preferred_element_type=jnp.float32).reshape(
        row_total, kv_local, HD
    )
    values_own = (
        jnp.dot(attn_input, w_value, preferred_element_type=jnp.float32)
        .astype(jnp.bfloat16)
        .reshape(seq_count, tok_rows, kv_local * HD)
    )
    queries = (
        rotate(query_raw, cosine, sine_table)
        .astype(jnp.bfloat16)
        .reshape(seq_count, tok_rows, kv_local, group_size, HD)
    )
    keys_own = (
        rotate(key_raw, cosine, sine_table)
        .astype(jnp.bfloat16)
        .reshape(seq_count, tok_rows, kv_local * HD)
    )
    keys_all, values_all = (
        lax.all_gather(keys_own, "seq", axis=1, tiled=True),
        lax.all_gather(values_own, "seq", axis=1, tiled=True),
    )
    key_shape = (seq_count, seq_total, kv_local, HD)

    def forward_one(items):
        query_s, key_s, value_s, rows_s, seg_s, key_rows, key_seg, key_valid = items
        return attend_forward(
            query_s, key_s, value_s, (rows_s, seg_s), (key_rows, key_seg, key_valid), block_rows
        )

    log_total, kept_sum, exact_sum = lax.map(
        forward_one,
        (
            queries,
            keys_all.reshape(key_shape),
            values_all.reshape(key_shape),
            query_rows,
            query_seg,
            key_layout[0],
            key_layout[1],
            key_layout[3],
        ),
    )
    attn_heads = (kept_sum.reshape(row_total, heads_local * HD) * valid_rows).astype(jnp.bfloat16)
    attn_part = jnp.dot(attn_heads, w_out, preferred_element_type=jnp.float32)
    middle = own_half(inputs) + lax.psum_scatter(
        attn_part, "tensor", scatter_dimension=0, tiled=True
    )
    inverse_two = lax.rsqrt(jnp.mean(middle * middle, axis=-1, keepdims=True) + epsilon)
    normed_two = middle * inverse_two
    mlp_half = (normed_two * mlp_gain).astype(jnp.bfloat16)
    mlp_input = lax.all_gather(mlp_half, "tensor", axis=0, tiled=True)
    gate = jnp.dot(mlp_input, w_gate, preferred_element_type=jnp.float32)
    upward = jnp.dot(mlp_input, w_up, preferred_element_type=jnp.float32)
    hidden = (jax.nn.silu(gate) * upward).astype(jnp.bfloat16)
    mlp_part = jnp.dot(hidden, w_down, preferred_element_type=jnp.float32)
    result = middle + lax.psum_scatter(
        mlp_part.astype(jnp.bfloat16), "tensor", scatter_dimension=0, tiled=True
    ).astype(jnp.float32)
    cotangent = out_grad.reshape(row_total, width)
    grad_hidden = times_transpose(cotangent, w_down)
    sigmoid_gate = jax.nn.sigmoid(gate)
    grad_gate = (grad_hidden * upward * sigmoid_gate * (1.0 + gate * (1.0 - sigmoid_gate))).astype(
        jnp.bfloat16
    )
    grad_upward = (grad_hidden * gate * sigmoid_gate).astype(jnp.bfloat16)
    grad_w_down = outer_sum(hidden, cotangent)
    grad_w_gate = outer_sum(mlp_input, grad_gate)
    grad_w_up = outer_sum(mlp_input, grad_upward)
    grad_mlp_in = lax.psum_scatter(
        times_transpose(grad_gate, w_gate) + times_transpose(grad_upward, w_up),
        "tensor",
        scatter_dimension=0,
        tiled=True,
    )
    mlp_gain_part = jnp.sum(grad_mlp_in * normed_two, axis=0)
    scaled_two = grad_mlp_in * mlp_gain
    grad_middle = own_half(cotangent).astype(jnp.float32) + inverse_two * (
        scaled_two - normed_two * jnp.mean(scaled_two * normed_two, axis=-1, keepdims=True)
    )
    grad_middle_low = lax.all_gather(grad_middle.astype(jnp.bfloat16), "tensor", axis=0, tiled=True)
    grad_w_out = outer_sum(attn_heads, grad_middle_low)
    grad_heads = (
        times_transpose(grad_middle_low, w_out).astype(jnp.bfloat16)
        * valid_rows.astype(jnp.bfloat16)
    ).reshape(seq_count, tok_rows, kv_local, group_size, HD)
    delta = jnp.einsum(
        "sqkgd,sqkgd->skgq", grad_heads, exact_sum, preferred_element_type=jnp.float32
    )
    keys_back, values_back = (
        lax.all_gather(keys_own, "seq", axis=1, tiled=True),
        lax.all_gather(values_own, "seq", axis=1, tiled=True),
    )
    keys_back = keys_back.reshape(key_shape)
    values_back = values_back.reshape(key_shape)

    def backward_one():

        def run(items):
            (
                query_s,
                grad_s,
                log_s,
                delta_s,
                key_s,
                value_s,
                rows_s,
                seg_s,
                key_rows,
                key_seg,
                key_valid,
            ) = items
            return attend_backward(
                query_s,
                grad_s,
                log_s,
                delta_s,
                key_s,
                value_s,
                (rows_s, seg_s),
                (key_rows, key_seg, key_valid),
                block_rows,
            )

        return run

    backward_items = (
        queries,
        grad_heads,
        log_total,
        delta,
        keys_back,
        values_back,
        query_rows,
        query_seg,
        key_layout[0],
        key_layout[1],
        key_layout[3],
    )
    grad_query, key_terms = lax.map(backward_one(), backward_items)
    grad_key_sum, grad_value_sum = (
        lax.psum_scatter(
            key_terms[0].astype(jnp.bfloat16), "seq", scatter_dimension=1, tiled=True
        ).astype(jnp.float32),
        lax.psum_scatter(
            key_terms[1].astype(jnp.bfloat16), "seq", scatter_dimension=1, tiled=True
        ).astype(jnp.float32),
    )
    grad_key_rot = grad_key_sum.reshape(row_total, kv_local, HD) * HD ** (-0.5)
    grad_key_low = (
        rotate_back(grad_key_rot, cosine, sine_table)
        .astype(jnp.bfloat16)
        .reshape(row_total, kv_local * HD)
    )
    grad_value_low = grad_value_sum.reshape(row_total, kv_local * HD).astype(jnp.bfloat16)
    grad_query_rot = (grad_query * HD ** (-0.5)).reshape(row_total, heads_local, HD)
    grad_query_low = (
        rotate_back(grad_query_rot, cosine, sine_table)
        .astype(jnp.bfloat16)
        .reshape(row_total, heads_local * HD)
    )
    grad_w_query = outer_sum(attn_input, grad_query_low)
    grad_w_key = outer_sum(attn_input, grad_key_low)
    grad_w_value = outer_sum(attn_input, grad_value_low)
    attn_back_part = (
        times_transpose(grad_query_low, w_query)
        + times_transpose(grad_key_low, w_key)
        + times_transpose(grad_value_low, w_value)
    )
    grad_attn_in = lax.psum_scatter(
        attn_back_part.astype(jnp.bfloat16), "tensor", scatter_dimension=0, tiled=True
    ).astype(jnp.float32)
    normed_half = own_half(normed_one)
    attn_gain_part = jnp.sum(grad_attn_in * normed_half, axis=0)
    scaled_one = grad_attn_in * attn_gain
    grad_inputs = grad_middle + own_half(inverse_one) * (
        scaled_one - normed_half * jnp.mean(scaled_one * normed_half, axis=-1, keepdims=True)
    )
    grad_attn_gain, grad_mlp_gain = lax.psum((attn_gain_part, mlp_gain_part), "tensor")
    reduced = tuple(
        (
            lax.psum_scatter(grad_attn_gain, ("dp", "seq"), scatter_dimension=0, tiled=True),
            lax.psum_scatter(grad_w_query, ("dp", "seq"), scatter_dimension=0, tiled=True),
            lax.psum_scatter(grad_w_key, ("dp", "seq"), scatter_dimension=0, tiled=True),
            lax.psum_scatter(grad_w_value, ("dp", "seq"), scatter_dimension=0, tiled=True),
            lax.psum_scatter(grad_w_out, ("dp", "seq"), scatter_dimension=1, tiled=True),
            lax.psum_scatter(grad_mlp_gain, ("dp", "seq"), scatter_dimension=0, tiled=True),
            lax.psum_scatter(grad_w_gate, ("dp", "seq"), scatter_dimension=0, tiled=True),
            lax.psum_scatter(grad_w_up, ("dp", "seq"), scatter_dimension=0, tiled=True),
            lax.psum_scatter(grad_w_down, ("dp", "seq"), scatter_dimension=1, tiled=True),
        )
    )
    result_all, grad_all = (
        lax.all_gather(result.astype(jnp.bfloat16), "tensor", axis=0, tiled=True),
        lax.all_gather(grad_inputs.astype(jnp.bfloat16), "tensor", axis=0, tiled=True),
    )
    out_shape = (seq_count, tok_rows, width)
    return (
        result_all.reshape(out_shape),
        grad_all.reshape(out_shape),
        reduced[0],
        reduced[1],
        reduced[2],
        reduced[3],
        reduced[4],
        reduced[5],
        reduced[6],
        reduced[7],
        reduced[8],
    )


LOG2E = 1.4426950408889634
QUERY_TILE = 256
KEY_TILE = 512
PAD = 128
ROW_TILE = 256
MEBI = 1024 * 1024
VMEM_LIMIT = 56 * MEBI
IN_VMEM = pl.BlockSpec(memory_space=pltpu.VMEM)
IN_ANY = pl.BlockSpec(memory_space=pl.ANY)


def doc_start(ends, rows):
    start = jnp.zeros_like(rows)
    for end in ends:
        start = jnp.where(rows >= end, end, start)
    return jnp.where(rows >= ends[-1], rows, start)


def dot_plain(left, right):
    return jnp.dot(left, right, preferred_element_type=jnp.float32)


def shape_of(*dims, dtype=jnp.bfloat16):
    return jax.ShapeDtypeStruct(dims, dtype)


def norm_scale(values):
    return lax.rsqrt(jnp.mean(values * values, axis=-1, keepdims=True) + epsilon)


def partner(position, step):
    if step == 0:
        return position
    if step == 1:
        return position + 1 - 2 * (position % 2)
    if step == 2:
        return position + 2 - 4 * (position // 2)
    return 3 - position


def greet(places):
    barrier = pltpu.get_barrier_semaphore()
    for device in places:
        pl.semaphore_signal(barrier, inc=1, device_id=device, device_id_type=pl.DeviceIdType.MESH)
    pl.semaphore_wait(barrier, len(places))


class Copies:
    def __init__(self, load_sem, send_sem, recv_sem):
        self.sems = (load_sem, send_sem, recv_sem)
        self.loads, self.sends = 0, 0

    def load(self, source, target):
        copy = pltpu.make_async_copy(source, target, self.sems[0].at[self.loads])
        copy.start()
        self.loads += 1
        return copy

    def send(self, source, target, device):
        copy = pltpu.make_async_remote_copy(
            src_ref=source,
            dst_ref=target,
            send_sem=self.sems[1].at[self.sends],
            recv_sem=self.sems[2].at[self.sends],
            device_id=device,
            device_id_type=pl.DeviceIdType.MESH,
        )
        copy.start()
        self.sends += 1
        return copy


def wait_all(copies):
    for copy in copies:
        copy.wait()


def forward_kernel(
    ends_ref,
    x_far,
    gain_one,
    gain_two,
    cotangent_far,
    cosine_far,
    sine_far,
    w_query,
    w_key,
    w_value,
    w_out_far,
    w_gate_far,
    w_up_far,
    w_down_far,
    lse,
    gain_sum,
    heads_out,
    keys_out,
    values_out,
    exact_out,
    cotangent_x,
    normed_one_out,
    shards,
    normed_out,
    normed_x,
    normed_y,
    hidden_out,
    grad_gate_out,
    grad_up_out,
    hidden_x,
    up_y,
    merged_out,
    grad_low_out,
    grad_middle_out,
    down_away,
    up_away,
    back_0,
    back_1,
    back_2,
    back_3,
    result,
    w_out,
    w_gate,
    w_up,
    w_down,
    x,
    cotangent,
    cosine,
    sine,
    normed_one,
    packed,
    packed_in,
    heads,
    keys,
    values,
    exact,
    low,
    low_in,
    merged,
    part,
    other,
    normed,
    hidden,
    grad_gate,
    grad_up,
    grad_part,
    grad_other,
    grad_middle,
    free_sem,
    load_sem,
    send_sem,
    recv_sem,
):
    dp_index, place, core = (lax.axis_index(name) for name in ("dp", "seq", "tensor"))
    along_x, along_y = dp_index % 2, dp_index // 2
    rows, width = x.shape
    units = w_up.shape[1]
    half_rows, quarter_rows = rows // 2, rows // 4
    half = pl.ds(pl.multiple_of(core * half_rows, half_rows), half_rows)
    first_quarter = pl.ds(pl.multiple_of(core * half_rows, quarter_rows), quarter_rows)
    second_quarter = pl.ds(
        pl.multiple_of(core * half_rows + quarter_rows, quarter_rows), quarter_rows
    )
    peers = [{"seq": partner(place, d)} for d in (1, 2, 3)]
    over_x, over_y = {"dp": partner(dp_index, 1)}, {"dp": partner(dp_index, 2)}
    across = {"tensor": 1 - core}
    tiles = [pl.ds(block * ROW_TILE, ROW_TILE) for block in range(rows // ROW_TILE)]
    copies = Copies(load_sem, send_sem, recv_sem)
    send, load = copies.send, copies.load
    late = []

    columns = [w.shape[1] for w in (w_query, w_key, w_value)]
    starts = [0, columns[0], columns[0] + columns[1]]
    weight_parts = [
        w_gate.at[:, pl.ds(start, size)] for start, size in zip(starts, columns, strict=True)
    ]
    own_rows = pl.ds(pl.multiple_of(place * rows, rows), rows)
    x_load = load(x_far, x)
    table_loads = [load(cosine_far.at[own_rows], cosine), load(sine_far.at[own_rows], sine)]
    head_loads = [
        load(w, target)
        for w, target in zip((w_value, w_key, w_query), reversed(weight_parts), strict=True)
    ]
    greet([*peers, over_x, over_y, across])
    beside_copy = send(cotangent_far.at[half], cotangent_x.at[half], over_x)
    other_loads = [load(w_out_far, w_out), load(w_up_far, w_up), load(w_down_far, w_down)]
    cotangent_load = load(cotangent_far, cotangent)

    heads[...] = jnp.zeros_like(heads)
    keys[...] = jnp.zeros_like(keys)
    values[...] = jnp.zeros_like(values)
    x_load.wait()
    packed_copies = []
    for block, tile in enumerate(tiles):
        inputs = x[tile, :].astype(jnp.float32)
        rows_low = (inputs * norm_scale(inputs) * gain_one[...]).astype(jnp.bfloat16)
        normed_one[tile, :] = rows_low
        if block == 0:
            wait_all(head_loads)
            wait_all(table_loads)
        cos_part, sin_part = cosine[tile, :HD], sine[tile, :HD]

        def turned(value, cos_part=cos_part, sin_part=sin_part):
            swapped = jnp.concatenate([value[:, HD // 2 :], value[:, : HD // 2]], axis=1)
            return (value * cos_part + swapped * sin_part).astype(jnp.bfloat16)

        value = dot_plain(rows_low, weight_parts[2][...])
        for head in range(4):
            packed[head, tile, 3 * HD :] = value[:, head * HD : (head + 1) * HD].astype(jnp.bfloat16)
        key = dot_plain(rows_low, weight_parts[1][...])
        for head in range(4):
            packed[head, tile, 2 * HD : 3 * HD] = turned(key[:, head * HD : (head + 1) * HD])
        query = dot_plain(rows_low, weight_parts[0][...])
        for head in range(4):
            first = 2 * head * HD
            packed[head, tile, :HD] = turned(query[:, first : first + HD])
            packed[head, tile, HD : 2 * HD] = turned(query[:, first + HD : first + 2 * HD])
        for d in (1, 2, 3):
            packed_copies.append(
                (
                    d,
                    tile,
                    send(packed.at[partner(place, d), tile], packed_in.at[d - 1, tile], peers[d - 1]),
                )
            )
    gate_load = load(w_gate_far, w_gate)
    outs = [load(normed_one, normed_one_out)]

    def unpack(source, block):
        here = pl.ds(pl.multiple_of(block * rows, rows), rows)
        heads[0, here, :HD] = source[:, :HD]
        heads[1, here, :HD] = source[:, HD : 2 * HD]
        keys[here, :HD] = source[:, 2 * HD : 3 * HD]
        values[here, :HD] = source[:, 3 * HD :]

    unpack(packed.at[place], place)
    beside_copy.wait()
    cotangent_copy = send(cotangent_x.at[half], cotangent_x.at[half], across)
    for d, tile, copy in packed_copies:
        copy.wait()
    for d in (1, 2, 3):
        unpack(packed_in.at[d - 1], partner(place, d))
    outs += [load(heads, heads_out), load(keys, keys_out), load(values, values_out)]

    shard_near = send(normed_one.at[half], shards.at[0, half], peers[0])
    shard_far = [send(normed_one.at[first_quarter], shards.at[1, first_quarter], peers[1])]

    ends = [ends_ref[index] for index in range(4)]
    scale = HD ** (-0.5) * LOG2E

    def attend(first, key_tiles):
        tile = pl.ds(first, QUERY_TILE)
        queries = jnp.concatenate([heads[0, tile, :], heads[1, tile, :]], axis=0)
        row_ids = lax.broadcasted_iota(jnp.int32, (2 * QUERY_TILE, 1), 0) % QUERY_TILE + first
        doc_starts = doc_start(ends, row_ids)

        def key_step(key_index, state):
            row_max, row_sum, summed = state
            first_key = pl.multiple_of(key_index * KEY_TILE, KEY_TILE)
            key_rows = pl.ds(first_key, KEY_TILE)
            scores = scale * times_transpose(queries, keys[key_rows, :])
            key_ids = lax.broadcasted_iota(jnp.int32, (1, KEY_TILE), 1) + first_key
            scores = jnp.where((key_ids >= doc_starts) & (key_ids <= row_ids), scores, masked_score)
            new_max = jnp.maximum(row_max, jnp.max(scores, axis=1, keepdims=True))
            probs = jnp.exp2(scores - new_max)
            shrink = jnp.exp2(row_max - new_max)
            row_sum = row_sum * shrink + jnp.sum(probs, axis=1, keepdims=True)
            summed = summed * shrink + dot_plain(probs.astype(jnp.bfloat16), values[key_rows, :])
            return (new_max, row_sum, summed)

        row_max, row_sum, summed = lax.fori_loop(
            0,
            key_tiles,
            key_step,
            (
                jnp.full((2 * QUERY_TILE, 1), masked_score, jnp.float32),
                jnp.zeros((2 * QUERY_TILE, 1), jnp.float32),
                jnp.zeros((2 * QUERY_TILE, PAD), jnp.float32),
            ),
        )
        attended = jnp.where(row_ids < ends[-1], summed / row_sum, 0.0)
        total_log = row_max + jnp.log(row_sum) * LOG2E
        total_row = jnp.transpose(jnp.broadcast_to(total_log, (2 * QUERY_TILE, PAD)))[:1, :]
        return attended, total_row

    def attend_block(step, nothing):
        distance = 3 - step
        one, two = distance % 2, distance // 2
        flipped = place + one * (1 - 2 * (place % 2))
        block = flipped + two * (2 - 4 * (flipped // 2))

        slot = step % 2

        def attend_tile(index, nothing):
            first = pl.multiple_of(block * rows + index * QUERY_TILE, QUERY_TILE)
            attended, total_row = attend(first, block + 1)
            tile = pl.ds(first, QUERY_TILE)
            inner = pl.ds(pl.multiple_of(index * QUERY_TILE, QUERY_TILE), QUERY_TILE)
            for head in range(2):
                mine = attended[head * QUERY_TILE : (head + 1) * QUERY_TILE]
                exact[slot, head, inner, :] = mine
                low[distance, inner, head * HD : (head + 1) * HD] = mine[:, :HD].astype(
                    jnp.bfloat16
                )
                lse[head : head + 1, tile] = total_row[
                    :, head * QUERY_TILE : (head + 1) * QUERY_TILE
                ]
            return nothing

        lax.fori_loop(0, rows // QUERY_TILE, attend_tile, nothing)
        return block

    low_copies, exact_copies = {}, []
    for step in range(4):
        if step > 1:
            exact_copies[step - 2].wait()
        block = attend_block(step, 0)
        exact_rows = pl.ds(pl.multiple_of(block * rows, rows), rows)
        exact_copies.append(load(exact.at[step % 2], exact_out.at[:, exact_rows]))
        distance = 3 - step
        if distance:
            low_copies[distance] = send(
                low.at[distance], low_in.at[place], peers[distance - 1]
            )
    outs += exact_copies[2:]
    low_in[place] = low[0]
    for distance in (3, 2, 1):
        low_copies[distance].wait()
    shard_far.append(send(normed_one.at[second_quarter], shards.at[1, second_quarter], peers[1]))
    shard_far[0].wait()
    shard_both = [send(shards.at[1, first_quarter], shards.at[2, first_quarter], peers[0])]
    shard_near.wait()
    late.append(send(shards.at[0, half], shards.at[0, half], across))

    for head in range(4):
        merged[:, 2 * head * HD : 2 * (head + 1) * HD] = low_in[head]
    wait_all(other_loads)
    part_copies = []
    for tile in tiles:
        part[tile, :] = dot_plain(merged[tile, :], w_out[...]).astype(jnp.bfloat16)
        part_copies.append(send(part.at[tile], other.at[tile], across))

    def middle_rows(tile):
        return x[tile, :].astype(jnp.float32) + (
            part[tile, :].astype(jnp.float32) + other[tile, :].astype(jnp.float32)
        )

    for tile, copy in zip(tiles, part_copies, strict=True):
        copy.wait()
        middle = middle_rows(tile)
        normed[tile, :] = (middle * norm_scale(middle) * gain_two[...]).astype(jnp.bfloat16)
    normed_copies = [
        send(normed.at[half], normed_x.at[half], over_x),
        send(normed.at[half], normed_y.at[half], over_y),
    ]
    outs += [load(normed, normed_out), load(merged, merged_out)]
    cotangent_load.wait()
    gate_load.wait()

    unit_tile = units // 4

    def unit_step(index, nothing):
        columns = pl.ds(pl.multiple_of(index * unit_tile, unit_tile), unit_tile)
        inner = pl.ds(pl.multiple_of((index % 2) * unit_tile, unit_tile), unit_tile)
        rows_low = normed[...]
        gate, up = dot_plain(rows_low, w_gate[:, columns]), dot_plain(rows_low, w_up[:, columns])
        back = times_transpose(cotangent[...], w_down[columns, :])
        sigma = jax.nn.sigmoid(gate)
        swish = gate * sigma
        hidden[index // 2, :, inner] = (swish * up).astype(jnp.bfloat16)
        grad_gate[index] = (back * up * sigma * (1.0 + gate * (1.0 - sigma))).astype(jnp.bfloat16)
        grad_up[index // 2, :, inner] = (back * swish).astype(jnp.bfloat16)
        return nothing

    lax.fori_loop(0, 4, unit_step, 0)
    unit_copies = [
        send(hidden.at[1 - along_x], hidden_x, over_x),
        send(grad_up.at[1 - along_y], up_y, over_y),
    ]
    outs += [load(hidden, hidden_out), load(grad_gate, grad_gate_out), load(grad_up, grad_up_out)]

    width_tile = width // 3
    grad_copies = []
    for index in range(3):
        columns = pl.ds(index * width_tile, width_tile)
        total = None
        for quarter in range(4):
            inner = pl.ds(quarter * unit_tile, unit_tile)
            term = times_transpose(grad_gate[quarter], w_gate[columns, inner])
            total = term if total is None else total + term
        for side in range(2):
            inner = pl.ds(side * 2 * unit_tile, 2 * unit_tile)
            total = total + times_transpose(grad_up[side], w_up[columns, inner])
        grad_part[:, columns] = total.astype(jnp.bfloat16)
        grad_copies.append(send(grad_part.at[:, columns], grad_other.at[:, columns], across))
    shard_far[1].wait()
    late.append(send(shards.at[1, half], shards.at[1, half], across))
    shard_both.append(send(shards.at[1, second_quarter], shards.at[2, second_quarter], peers[0]))
    wait_all(grad_copies)

    for block, tile in enumerate(tiles):
        middle = middle_rows(tile)
        inverse = norm_scale(middle)
        unit_rows = middle * inverse
        grad_normed = grad_part[tile, :].astype(jnp.float32) + grad_other[tile, :].astype(
            jnp.float32
        )
        gain_term = jnp.sum(grad_normed * unit_rows, axis=0, keepdims=True)
        gain_sum[...] = gain_term if block == 0 else gain_sum[...] + gain_term
        scaled = grad_normed * gain_two[...]
        total = cotangent[tile, :].astype(jnp.float32) + inverse * (
            scaled - unit_rows * jnp.mean(scaled * unit_rows, axis=-1, keepdims=True)
        )
        if block:
            outs.pop().wait()
        grad_middle[...] = total
        outs.append(load(grad_middle, grad_middle_out.at[tile]))
        rows_low = total.astype(jnp.bfloat16)
        grad_part[tile, :] = rows_low
        row_ids = lax.broadcasted_iota(jnp.int32, (ROW_TILE, 1), 0) + (
            place * rows + block * ROW_TILE
        )
        back = jnp.where(row_ids < ends[3], times_transpose(rows_low, w_out[...]), 0.0)
        for head in range(4):
            low[head, tile, :] = back[:, 2 * head * HD : 2 * (head + 1) * HD].astype(jnp.bfloat16)
    pl.semaphore_signal(free_sem, inc=1, device_id=across, device_id_type=pl.DeviceIdType.MESH)
    back_copies = [
        send(low.at[partner(place, d)], out, peers[d - 1])
        for d, out in ((1, back_1), (2, back_2), (3, back_3))
    ]
    outs += [
        load(low.at[place], back_0),
        load(grad_part, grad_low_out),
    ]

    outs[0].wait()
    down_copies = []
    for index in range(3):
        columns = pl.ds(index * width_tile, width_tile)
        total = dot_plain(hidden[0], w_down[: units // 2, columns]) + dot_plain(
            hidden[1], w_down[units // 2 :, columns]
        )
        normed_one[:, columns] = total.astype(jnp.bfloat16)
        if index == 0:
            pl.semaphore_wait(free_sem, 1)
        down_copies.append(send(normed_one.at[:, columns], grad_other.at[:, columns], across))

    wait_all(normed_copies)
    late.append(send(normed_x.at[half], normed_x.at[half], across))
    normed_copy = send(normed_y.at[half], normed_y.at[half], across)
    wait_all(unit_copies)
    cotangent_copy.wait()
    normed_copy.wait()
    cotangent_slot, normed_slot = w_gate.at[pl.ds(0, rows), pl.ds(0, width)], w_gate.at[
        pl.ds(rows, rows), pl.ds(0, width)
    ]
    hidden_slot, up_slot = w_up.at[pl.ds(0, rows), pl.ds(0, units // 2)], w_up.at[
        pl.ds(rows, rows), pl.ds(0, units // 2)
    ]
    slot_loads = [
        load(cotangent_x, cotangent_slot),
        load(hidden_x, hidden_slot),
        load(normed_y, normed_slot),
        load(up_y, up_slot),
    ]
    wait_all(down_copies)
    for tile in tiles:
        x[tile, :] = (
            middle_rows(tile)
            + (normed_one[tile, :].astype(jnp.float32) + grad_other[tile, :].astype(jnp.float32))
        ).astype(jnp.bfloat16)
    outs.append(load(x, result))
    wait_all(shard_both)
    late.append(send(shards.at[2, half], shards.at[2, half], across))
    wait_all(slot_loads)
    block_rows = width // 4

    def away(slot, lefts, rights, block, target):
        columns = pl.ds(pl.multiple_of(block * block_rows, block_rows), block_rows)
        total = outer_sum(lefts[0][:, columns], rights[0][...]) + outer_sum(
            lefts[1][:, columns], rights[1][...]
        )
        place_rows = w_down.at[pl.ds(slot * block_rows, block_rows), pl.ds(0, units // 2)]
        place_rows[...] = total.astype(jnp.bfloat16)
        return load(place_rows, target)

    down_sides = ((cotangent, cotangent_slot), (hidden.at[along_x], hidden_slot))
    up_sides = ((normed, normed_slot), (grad_up.at[along_y], up_slot))
    for index in range(2):
        outs.append(
            away(index, *down_sides, 2 * (1 - along_y) + index, down_away.at[index])
        )
        outs.append(
            away(2 + index, *up_sides, 2 * index + 1 - along_x, up_away.at[index])
        )
    wait_all(back_copies)
    wait_all(late)
    wait_all(outs[1:])


def forward(ends, x, gains, cotangent, tables, weights):
    rows, width = x.shape
    w_query, w_key, w_value, w_out, w_gate, w_up, w_down = weights
    units = w_gate.shape[1]
    total = 4 * rows
    f32 = jnp.float32
    wide, message = shape_of(rows, width), shape_of(rows, 2 * HD)
    by_half, by_quarter = shape_of(2, rows, units // 2), shape_of(4, rows, units // 4)
    block = shape_of(2, width // 4, units // 2)
    vmem_outs = (shape_of(2, total, dtype=f32), shape_of(1, width, dtype=f32))
    far_outs = (
        shape_of(2, total, PAD),
        shape_of(total, PAD),
        shape_of(total, PAD),
        shape_of(2, total, PAD, dtype=f32),
        wide,
        wide,
        shape_of(3, rows, width),
        wide,
        wide,
        wide,
        by_half,
        by_quarter,
        by_half,
        shape_of(rows, units // 2),
        shape_of(rows, units // 2),
        shape_of(rows, w_out.shape[0]),
        wide,
        shape_of(rows, width, dtype=f32),
        block,
        block,
        *(message,) * 4,
        wide,
    )

    def low(*dims):
        return pltpu.VMEM(dims, jnp.bfloat16)

    scratch = [
        low(*w_out.shape),
        low(*w_gate.shape),
        low(*w_up.shape),
        low(*w_down.shape),
        low(rows, width),
        low(rows, width),
        pltpu.VMEM((rows, PAD), f32),
        pltpu.VMEM((rows, PAD), f32),
        low(rows, width),
        low(4, rows, 4 * HD),
        low(3, rows, 4 * HD),
        low(2, total, PAD),
        low(total, PAD),
        low(total, PAD),
        pltpu.VMEM((2, 2, rows, PAD), f32),
        low(4, rows, 2 * HD),
        low(4, rows, 2 * HD),
        low(rows, w_out.shape[0]),
        low(rows, width),
        low(rows, width),
        low(rows, width),
        low(*by_half.shape),
        low(*by_quarter.shape),
        low(*by_half.shape),
        low(rows, width),
        low(rows, width),
        pltpu.VMEM((ROW_TILE, width), f32),
        pltpu.SemaphoreType.REGULAR,
        pltpu.SemaphoreType.DMA((40,)),
        pltpu.SemaphoreType.DMA((44,)),
        pltpu.SemaphoreType.DMA((44,)),
    ]
    return pl.pallas_call(
        forward_kernel,
        out_shape=vmem_outs + far_outs,
        in_specs=[pl.BlockSpec(memory_space=pltpu.SMEM), IN_ANY]
        + [IN_VMEM] * 2
        + [IN_ANY] * 10,
        out_specs=(IN_VMEM,) * len(vmem_outs) + (IN_ANY,) * len(far_outs),
        scratch_shapes=scratch,
        compiler_params=pltpu.CompilerParams(
            collective_id=0, has_side_effects=True, vmem_limit_bytes=63 * MEBI
        ),
        cost_estimate=pl.CostEstimate(
            flops=16 * rows * width * units, bytes_accessed=64 * MEBI, transcendentals=0
        ),
        name="forward",
    )(ends, x, *gains, cotangent, *tables, *weights)


def tail_kernel(
    back_0,
    back_1,
    back_2,
    back_3,
    merged,
    grad_low,
    gain,
    mlp_gain_sum,
    cotangent,
    cotangent_x,
    normed,
    normed_x,
    normed_y,
    hidden,
    hidden_x,
    grad_up,
    up_y,
    grad_gate,
    down_in,
    up_in,
    normed_one,
    shards,
    w_query,
    w_key,
    w_value,
    x_far,
    grad_middle_far,
    grad_input,
    grad_down,
    grad_gate_x,
    grad_gate_y,
    grad_up_rows,
    grad_out,
    grad_query,
    grad_key,
    grad_value,
    gains,
    cotangents,
    normeds,
    hiddens,
    ups,
    gate_xs,
    gate_ys,
    inputs,
    grad_middle,
    arrived,
    heads,
    query,
    key,
    value,
    part,
    other,
    gate_x_away,
    gate_y_away,
    out_away,
    head_away,
    down_1,
    up_1,
    gate_x_1,
    gate_y_1,
    out_1,
    head_1,
    down_2,
    up_2,
    gate_x_2,
    gate_y_2,
    out_2,
    head_2,
    down_3,
    up_3,
    gate_x_3,
    gate_y_3,
    out_3,
    head_3,
    down_4,
    up_4,
    gate_x_4,
    gate_y_4,
    out_4,
    head_rows,
    gain_0,
    gain_1,
    gain_2,
    gain_3,
    gain_4,
    load_sem,
    send_sem,
    recv_sem,
):
    dp_index, place, core = (lax.axis_index(name) for name in ("dp", "seq", "tensor"))
    along_x, along_y = dp_index % 2, dp_index // 2
    near, far = place % 2, place // 2
    rows, width = x_far.shape
    block_rows = width // 4
    peers = [{"seq": partner(place, d)} for d in (1, 2, 3)]
    over_x, over_y = {"dp": partner(dp_index, 1)}, {"dp": partner(dp_index, 2)}
    across = {"tensor": 1 - core}
    greet([*peers, over_x, over_y, across])

    copies = Copies(load_sem, send_sem, recv_sem)
    send, load = copies.send, copies.load

    gate_copies = [
        send(grad_gate.at[1 - along_x], gate_xs.at[1], over_x),
        send(grad_gate.at[3 - along_y], gate_ys.at[1], over_y),
    ]
    back_copies = [
        send(source, arrived.at[d], peers[d]) for d, source in enumerate((back_1, back_2, back_3))
    ]
    first, second, third = (pl.ds(index * rows, rows) for index in range(3))
    for_gates = [
        load(normed, normeds.at[first]),
        load(normed_x, normeds.at[second]),
        load(normed_y, normeds.at[third]),
        load(grad_gate.at[along_x], gate_xs.at[0]),
        load(grad_gate.at[2 + along_y], gate_ys.at[0]),
    ]
    for_down = [
        load(cotangent, cotangents.at[first]),
        load(cotangent_x, cotangents.at[second]),
        load(hidden.at[along_x], hiddens.at[0]),
        load(hidden_x, hiddens.at[1]),
        load(down_in, down_1),
    ]
    for_up = [
        load(grad_up.at[along_y], ups.at[0]),
        load(up_y, ups.at[1]),
        load(up_in, up_1),
    ]
    for_head = [load(normed_one, inputs.at[0])] + [
        load(shards.at[d], inputs.at[d + 1]) for d in range(3)
    ]
    late_loads = [load(grad_middle_far, grad_middle)]

    def outer(pairs, block):
        columns = pl.ds(pl.multiple_of(block * block_rows, block_rows), block_rows)
        total = None
        for left, right in pairs:
            term = outer_sum(left[:, columns], right)
            total = term if total is None else total + term
        return total

    down_pairs = [
        (cotangents.at[first], lambda: hiddens[0]),
        (cotangents.at[second], lambda: hiddens[1]),
    ]
    up_pairs = [(normeds.at[first], lambda: ups[0]), (normeds.at[third], lambda: ups[1])]
    gate_x_pairs = [
        (normeds.at[first], lambda: gate_xs[0]),
        (normeds.at[second], lambda: gate_xs[1]),
    ]
    gate_y_pairs = [
        (normeds.at[first], lambda: gate_ys[0]),
        (normeds.at[third], lambda: gate_ys[1]),
    ]
    out_pairs = [(grad_low, lambda: merged[...])]
    head_pairs = [
        (inputs.at[d], lambda back=back: back[...])
        for d, back in enumerate((back_0, back_1, back_2, back_3))
    ]

    def block_along_y(side, index):
        return 2 * side + index

    def block_along_x(side, index):
        return 2 * index + side

    def fill(target, pairs, block_of, side):
        for index in range(2):
            target[index] = outer(
                [(left, right()) for left, right in pairs], block_of(side, index)
            ).astype(jnp.bfloat16)

    def add_outer(landed, pairs, block_of, side):
        for index in range(2):
            landed[index] = (
                landed[index].astype(jnp.float32)
                + outer([(left, right()) for left, right in pairs], block_of(side, index))
            ).astype(jnp.bfloat16)

    def quarters(ref):
        return ref.reshape(2, 2, 2, width // 16, ref.shape[-1])

    def send_near(ref, target):
        return send(quarters(ref).at[:, :, 1 - near], target, peers[0])

    def add_near(ref, target):
        kept = quarters(ref)
        for index in range(2):
            for side in range(2):
                target[index, side] = (
                    target[index, side].astype(jnp.float32)
                    + kept[index, side, near].astype(jnp.float32)
                ).astype(jnp.bfloat16)

    def send_far(ref, target):
        return send(ref.at[:, 1 - far], target, peers[1])

    def add_far(ref, target):
        for index in range(2):
            target[index] = (
                target[index].astype(jnp.float32) + ref[index, far].astype(jnp.float32)
            ).astype(jnp.bfloat16)

    wait_all(for_down)
    add_outer(down_1, down_pairs, block_along_y, along_y)
    down_copy = send_near(down_1, down_2)
    wait_all(for_up)
    wait_all(for_gates)
    add_outer(up_1, up_pairs, block_along_x, along_x)
    up_copy = send_near(up_1, up_2)
    wait_all(gate_copies)
    fill(gate_x_away, gate_x_pairs, block_along_y, 1 - along_y)
    gate_x_copy = send(gate_x_away, gate_x_1, over_y)
    fill(gate_y_away, gate_y_pairs, block_along_x, 1 - along_x)
    gate_y_copy = send(gate_y_away, gate_y_1, over_x)
    fill(out_away, out_pairs, block_along_x, 1 - along_x)
    out_copy = send(out_away, out_1, over_x)
    wait_all(for_head)
    fill(head_away, head_pairs, block_along_x, 1 - along_x)
    head_copy = send(head_away, head_1, over_x)
    gate_x_copy.wait()
    add_outer(gate_x_1, gate_x_pairs, block_along_y, along_y)
    gate_x_copy = send_near(gate_x_1, gate_x_2)
    gate_y_copy.wait()
    add_outer(gate_y_1, gate_y_pairs, block_along_x, along_x)
    gate_y_copy = send_near(gate_y_1, gate_y_2)

    weights = normeds
    columns = [w.shape[1] for w in (w_query, w_key, w_value)]
    starts = [0, columns[0], columns[0] + columns[1]]
    weight_loads = [
        load(w, weights.at[:, pl.ds(start, size)])
        for w, start, size in zip((w_query, w_key, w_value), starts, columns, strict=True)
    ]
    heads[place] = back_0[...]
    for d, copy in enumerate(back_copies):
        copy.wait()
        heads[partner(place, d + 1)] = arrived[d]
    for head in range(4):
        query[:, 2 * head * HD : 2 * (head + 1) * HD] = heads[head, :, : 2 * HD]
        key[:, head * HD : (head + 1) * HD] = heads[head, :, 2 * HD : 3 * HD]
        value[:, head * HD : (head + 1) * HD] = heads[head, :, 3 * HD :]
    wait_all(weight_loads)
    tiles = [pl.ds(block * ROW_TILE, ROW_TILE) for block in range(rows // ROW_TILE)]
    part_copies = []
    for tile in tiles:
        total = None
        for ref, start, size in zip((query, key, value), starts, columns, strict=True):
            term = times_transpose(ref[tile, :], weights[:, start : start + size])
            total = term if total is None else total + term
        part[tile, :] = total.astype(jnp.bfloat16)
        part_copies.append(send(part.at[tile], other.at[tile], across))

    out_copy.wait()
    add_outer(out_1, out_pairs, block_along_x, along_x)
    out_copy = send(out_1.at[1 - along_y], out_2, over_y)
    head_copy.wait()
    add_outer(head_1, head_pairs, block_along_x, along_x)
    head_copy = send(head_1.at[1 - along_y], head_2, over_y)

    input_load = load(x_far, inputs.at[0])
    wait_all([input_load, *late_loads])
    for block, (tile, copy) in enumerate(zip(tiles, part_copies, strict=True)):
        copy.wait()
        values = inputs[0, tile, :].astype(jnp.float32)
        inverse = norm_scale(values)
        unit_rows = values * inverse
        grad_normed = part[tile, :].astype(jnp.float32) + other[tile, :].astype(jnp.float32)
        term = jnp.sum(grad_normed * unit_rows, axis=0, keepdims=True)
        gain_sum = term if block == 0 else gain_sum + term
        scaled = grad_normed * gain[...]
        grad_input[tile, :] = (
            grad_middle[tile, :]
            + inverse * (scaled - unit_rows * jnp.mean(scaled * unit_rows, axis=-1, keepdims=True))
        ).astype(jnp.bfloat16)
    width_each = width // 16
    gain_0[...] = jnp.zeros_like(gain_0)
    for index in range(16):
        lanes = slice(index * width_each, (index + 1) * width_each)
        slot = (index // 8, (index // 4) % 2, (index // 2) % 2, index % 2)
        gain_0[(*slot, slice(0, 1), slice(0, width_each))] = gain_sum[:, lanes]
        gain_0[(*slot, slice(1, 2), slice(0, width_each))] = mlp_gain_sum[:, lanes]
    gain_copy = send(gain_0.at[1 - along_y], gain_1, over_y)

    down_copy.wait()
    add_near(down_1, down_2)
    down_copy = send_far(down_2, down_3)
    gain_copy.wait()
    gain_1[...] += gain_0[along_y]
    gain_copy = send(gain_1.at[1 - along_x], gain_2, over_x)
    up_copy.wait()
    add_near(up_1, up_2)
    up_copy = send_far(up_2, up_3)
    out_copy.wait()
    out_2[...] = (
        out_2[...].astype(jnp.float32) + out_1[along_y].astype(jnp.float32)
    ).astype(jnp.bfloat16)
    out_copy = send(
        out_2.reshape(2, 2, width_each, out_2.shape[-1]).at[:, 1 - near], out_3, peers[0]
    )
    head_copy.wait()
    head_2[...] = (
        head_2[...].astype(jnp.float32) + head_1[along_y].astype(jnp.float32)
    ).astype(jnp.bfloat16)
    head_slots = head_2.reshape(4, width_each, head_2.shape[-1])
    head_copies = [
        send(head_slots.at[partner(place, d + 1)], head_3.at[d], peers[d]) for d in range(3)
    ]
    gain_copy.wait()
    gain_2[...] += gain_1[along_x]
    gain_copy = send(gain_2.at[1 - far], gain_3, peers[1])
    gate_x_copy.wait()
    add_near(gate_x_1, gate_x_2)
    gate_x_copy = send_far(gate_x_2, gate_x_3)
    gate_y_copy.wait()
    add_near(gate_y_1, gate_y_2)
    gate_y_copy = send_far(gate_y_2, gate_y_3)
    gain_copy.wait()
    gain_3[...] += gain_2[far]
    gain_copy = send(gain_3.at[1 - near], gain_4, peers[0])

    down_copy.wait()
    add_far(down_2, down_3)
    down_copy = send(down_3.at[1 - along_x], down_4, over_x)
    up_copy.wait()
    add_far(up_2, up_3)
    up_copy = send(up_3.at[1 - along_y], up_4, over_y)
    out_copy.wait()
    out_kept = out_2.reshape(2, 2, width_each, out_2.shape[-1])
    for side in range(2):
        out_3[side] = (
            out_3[side].astype(jnp.float32) + out_kept[side, near].astype(jnp.float32)
        ).astype(jnp.bfloat16)
    out_copy = send(out_3.at[1 - far], out_4, peers[1])
    gain_copy.wait()
    gains[...] = gain_4[...] + gain_3[near]
    gate_x_copy.wait()
    add_far(gate_x_2, gate_x_3)
    gate_x_copy = send(gate_x_3.at[1 - along_x], gate_x_4, over_x)
    gate_y_copy.wait()
    add_far(gate_y_2, gate_y_3)
    gate_y_copy = send(gate_y_3.at[1 - along_y], gate_y_4, over_y)

    head_rows[place] = head_slots[place]
    for d, copy in enumerate(head_copies):
        copy.wait()
        head_rows[partner(place, d + 1)] = head_3[d]
    for head in range(4):
        mine = head_rows[head].astype(jnp.float32)
        grad_query[:, 2 * head * HD : 2 * (head + 1) * HD] = mine[:, : 2 * HD]
        grad_key[:, head * HD : (head + 1) * HD] = mine[:, 2 * HD : 3 * HD]
        grad_value[:, head * HD : (head + 1) * HD] = mine[:, 3 * HD :]

    def both_sides(ref, landed, here, target):
        target[here] = ref[here].astype(jnp.float32)
        target[1 - here] = landed[...].astype(jnp.float32)

    out_copy.wait()
    grad_out[...] = out_4[...].astype(jnp.float32) + out_3[far].astype(jnp.float32)
    down_copy.wait()
    both_sides(down_3, down_4, along_x, grad_down)
    up_copy.wait()
    both_sides(up_3, up_4, along_y, grad_up_rows)
    gate_x_copy.wait()
    both_sides(gate_x_3, gate_x_4, along_x, grad_gate_x)
    gate_y_copy.wait()
    both_sides(gate_y_3, gate_y_4, along_y, grad_gate_y)


def tail(backs, merged, grad_low, gain, mlp_gain_sum, far):
    rows, width = grad_low.shape
    operands = list(far.values())
    query, key = far["w_query"].shape[1], far["w_key"].shape[1]
    each, block_rows = width // 16, width // 4
    half, quarter = far["hidden"].shape[2], far["grad_gate"].shape[2]
    f32 = jnp.float32
    outs = (
        shape_of(rows, width),
        shape_of(2, each, half, dtype=f32),
        shape_of(2, each, quarter, dtype=f32),
        shape_of(2, each, quarter, dtype=f32),
        shape_of(2, each, half, dtype=f32),
        shape_of(each, merged.shape[1], dtype=f32),
        shape_of(each, query, dtype=f32),
        shape_of(each, key, dtype=f32),
        shape_of(each, key, dtype=f32),
        shape_of(8, PAD, dtype=f32),
    )

    def low(*dims):
        return pltpu.VMEM(dims, jnp.bfloat16)

    head, merged_width = 4 * HD, merged.shape[1]
    sizes = (half, half, quarter, quarter)
    scratch = [
        low(2 * rows, width),
        low(3 * rows, width),
        low(2, rows, half),
        low(2, rows, half),
        low(2, rows, quarter),
        low(2, rows, quarter),
        low(4, rows, width),
        pltpu.VMEM((rows, width), f32),
        low(3, rows, head),
        low(4, rows, head),
        low(rows, query),
        low(rows, key),
        low(rows, key),
        low(rows, width),
        low(rows, width),
        low(2, block_rows, quarter),
        low(2, block_rows, quarter),
        low(2, block_rows, merged_width),
        low(2, block_rows, head),
        *(low(2, block_rows, size) for size in (*sizes, merged_width, head)),
        *(low(2, 2, each, size) for size in sizes),
        low(block_rows, merged_width),
        low(block_rows, head),
        *(low(2, each, size) for size in (*sizes, merged_width)),
        low(3, each, head),
        *(low(each, size) for size in (*sizes, merged_width)),
        low(4, each, head),
        pltpu.VMEM((2, 2, 2, 2, 8, PAD), f32),
        pltpu.VMEM((2, 2, 2, 8, PAD), f32),
        pltpu.VMEM((2, 2, 8, PAD), f32),
        pltpu.VMEM((2, 8, PAD), f32),
        pltpu.VMEM((8, PAD), f32),
        pltpu.SemaphoreType.DMA((24,)),
        pltpu.SemaphoreType.DMA((44,)),
        pltpu.SemaphoreType.DMA((44,)),
    ]
    return pl.pallas_call(
        tail_kernel,
        out_shape=outs,
        in_specs=[IN_VMEM] * 8 + [IN_ANY] * len(operands),
        out_specs=(IN_VMEM,) * len(outs),
        scratch_shapes=scratch,
        compiler_params=pltpu.CompilerParams(
            collective_id=2, has_side_effects=True, vmem_limit_bytes=63 * MEBI
        ),
        cost_estimate=pl.CostEstimate(
            flops=6 * rows * width * 4 * half, bytes_accessed=32 * MEBI, transcendentals=0
        ),
        name="tail",
    )(*backs, merged, grad_low, gain, mlp_gain_sum, *operands)


def attention_backward_kernel(
    info,
    grad_0,
    grad_1,
    grad_2,
    grad_3,
    heads,
    keys,
    values,
    exact,
    lse,
    cosine,
    sine,
    first_wait,
    second_wait,
    back_0,
    back_1,
    back_2,
    back_3,
    grad_heads,
    grad_query,
    grad_key,
    grad_value,
):
    grads, backs = (grad_0, grad_1, grad_2, grad_3), (back_0, back_1, back_2, back_3)
    rows_each = grad_0.shape[0]
    total = rows_each * len(grads)
    ends = [info[index] for index in range(4)]
    place = info[4]
    grad_heads[...] = jnp.zeros_like(grad_heads)
    grad_key[...] = jnp.zeros_like(grad_key)
    grad_value[...] = jnp.zeros_like(grad_value)
    for step, grad in enumerate(grads):
        rows = pl.ds(pl.multiple_of((place ^ step) * rows_each, rows_each), rows_each)
        grad_heads[0, rows, :HD] = grad[:, :HD]
        grad_heads[1, rows, :HD] = grad[:, HD:]
    scale = HD ** (-0.5) * LOG2E

    def query_step(index, nothing):
        first = pl.multiple_of(index * QUERY_TILE, QUERY_TILE)
        tile = pl.ds(first, QUERY_TILE)
        queries = jnp.concatenate([heads[0, tile, :], heads[1, tile, :]], axis=0)
        grad_rows = jnp.concatenate([grad_heads[0, tile, :], grad_heads[1, tile, :]], axis=0)
        exact_rows = jnp.concatenate([exact[0, tile, :], exact[1, tile, :]], axis=0)
        delta = jnp.sum(
            jnp.transpose(grad_rows.astype(jnp.float32) * exact_rows), axis=0, keepdims=True
        )
        log_row = jnp.concatenate([lse[0:1, tile], lse[1:2, tile]], axis=1)
        row_ids = lax.broadcasted_iota(jnp.int32, (1, 2 * QUERY_TILE), 1) % QUERY_TILE + first
        starts = doc_start(ends, row_ids)
        low_tile = doc_start(ends, first) // KEY_TILE
        high_tile = (first + QUERY_TILE - 1) // KEY_TILE + 1

        def key_step(key_index, summed):
            first_key = pl.multiple_of(key_index * KEY_TILE, KEY_TILE)
            key_rows = pl.ds(first_key, KEY_TILE)
            key_part, value_part = keys[key_rows, :], values[key_rows, :]
            scores = scale * times_transpose(key_part, queries)
            columns = lax.broadcasted_iota(jnp.int32, (KEY_TILE, 1), 0) + first_key
            probs = jnp.where(
                (columns >= starts) & (columns <= row_ids), jnp.exp2(scores - log_row), 0.0
            )
            grad_scores = (probs * (times_transpose(value_part, grad_rows) - delta)).astype(
                jnp.bfloat16
            )
            grad_value[key_rows, :] += jnp.dot(
                probs.astype(jnp.bfloat16), grad_rows, preferred_element_type=jnp.float32
            )
            grad_key[key_rows, :] += jnp.dot(
                grad_scores, queries, preferred_element_type=jnp.float32
            )
            return summed + outer_sum(grad_scores, key_part)

        summed = lax.fori_loop(
            low_tile, high_tile, key_step, jnp.zeros((2 * QUERY_TILE, PAD), jnp.float32)
        )
        grad_query[0, tile, :] = summed[:QUERY_TILE]
        grad_query[1, tile, :] = summed[QUERY_TILE:]
        return nothing

    lax.fori_loop(0, total // QUERY_TILE, query_step, 0)
    for step, back in enumerate(backs):
        rows = pl.ds(pl.multiple_of((place ^ step) * rows_each, rows_each), rows_each)
        cos_part, sin_part = cosine[rows, :], sine[rows, :]

        def turned_back(part):
            lanes = lax.broadcasted_iota(jnp.int32, part.shape, 1)
            swapped = jnp.where(
                lanes < HD // 2, pltpu.roll(part, PAD - HD // 2, 1), pltpu.roll(part, HD // 2, 1)
            )
            turned = (part * cos_part - swapped * sin_part) * HD ** (-0.5)
            return turned[:, :HD].astype(jnp.bfloat16)

        back[:, :HD] = turned_back(grad_query[0, rows, :])
        back[:, HD : 2 * HD] = turned_back(grad_query[1, rows, :])
        back[:, 2 * HD : 3 * HD] = turned_back(grad_key[rows, :])
        back[:, 3 * HD :] = grad_value[rows, :HD].astype(jnp.bfloat16)


def attention_backward(info, grads, kept, waits):
    rows_each = grads[0].shape[0]
    total = rows_each * len(grads)
    return pl.pallas_call(
        attention_backward_kernel,
        out_shape=tuple(jax.ShapeDtypeStruct((rows_each, 4 * HD), jnp.bfloat16) for _ in grads),
        in_specs=[pl.BlockSpec(memory_space=pltpu.SMEM)]
        + [pl.BlockSpec(memory_space=pltpu.VMEM)] * (len(grads) + len(kept))
        + [IN_ANY] * len(waits),
        out_specs=(pl.BlockSpec(memory_space=pltpu.VMEM),) * len(grads),
        scratch_shapes=[
            pltpu.VMEM((2, total, PAD), jnp.bfloat16),
            pltpu.VMEM((2, total, PAD), jnp.float32),
            pltpu.VMEM((total, PAD), jnp.float32),
            pltpu.VMEM((total, PAD), jnp.float32),
        ],
        compiler_params=pltpu.CompilerParams(vmem_limit_bytes=48 * MEBI),
        cost_estimate=pl.CostEstimate(
            flops=10 * 2 * total * total * PAD // 2, bytes_accessed=8 * MEBI, transcendentals=total * total
        ),
        name="attention_backward",
    )(info, *grads, *kept, *waits)


def swap(array, axis, bit):
    return lax.ppermute(array, axis, [(i, i ^ bit) for i in range(lax.axis_size(axis))])


def local_paired(
    hidden_in,
    lengths,
    attn_gain,
    w_query,
    w_key,
    w_value,
    w_out,
    mlp_gain,
    w_gate,
    w_up,
    w_down,
    out_grad,
):
    rows, width = hidden_in.shape[1], hidden_in.shape[2]
    dp_index, place, core = (lax.axis_index(name) for name in ("dp", "seq", "tensor"))
    along_x, along_y = dp_index % 2, dp_index // 2
    total_rows = 4 * rows
    x, cotangent = hidden_in[0], out_grad[0]
    gain_one, gain_two = attn_gain[None], mlp_gain[None]
    info = jnp.concatenate(
        [jnp.cumsum(lengths[0]), jnp.stack([place, along_x, along_y, core])]
    ).astype(jnp.int32)

    def over_x(array):
        return swap(array, "dp", 1)

    def over_y(array):
        return swap(array, "dp", 2)

    _, _, offsets, _ = doc_layout(lengths[0], 0, total_rows)
    cosine, sine = rope_tables(offsets)
    cosine, sine = cosine[:, 0], sine[:, 0]
    spare = PAD - HD
    cosine = jnp.pad(jnp.concatenate([cosine, cosine], axis=1), ((0, 0), (0, spare)))
    sine = jnp.pad(jnp.concatenate([-sine, sine], axis=1), ((0, 0), (0, spare)))

    (
        lse,
        mlp_gain_part,
        heads,
        keys,
        values,
        exact,
        cotangent_x,
        attn_input,
        input_shards,
        mlp_input,
        mlp_x,
        mlp_y,
        hidden,
        grad_gate,
        grad_up,
        hidden_x,
        up_y,
        attn_heads,
        grad_low,
        grad_middle,
        down_away,
        up_away,
        *grad_dealt,
        result,
    ) = forward(
        info,
        x,
        (gain_one, gain_two),
        cotangent,
        (cosine, sine),
        (w_query, w_key, w_value, w_out, w_gate, w_up, w_down),
    )
    kept = (heads, keys, values, exact, lse)
    down_in, up_in = over_y(down_away), over_x(up_away)
    backs = attention_backward(info, grad_dealt, kept + (cosine, sine), (down_away, up_away))
    (
        grad_inputs,
        grad_down,
        grad_gate_x,
        grad_gate_y,
        grad_up_rows,
        grad_out,
        grad_w_query,
        grad_w_key,
        grad_w_value,
        gains,
    ) = tail(
        backs,
        attn_heads,
        grad_low,
        gain_one,
        mlp_gain_part,
        dict(
            cotangent=cotangent,
            cotangent_x=cotangent_x,
            normed=mlp_input,
            normed_x=mlp_x,
            normed_y=mlp_y,
            hidden=hidden,
            hidden_x=hidden_x,
            grad_up=grad_up,
            up_y=up_y,
            grad_gate=grad_gate,
            down_in=down_in,
            up_in=up_in,
            normed_one=attn_input,
            shards=input_shards,
            w_query=w_query,
            w_key=w_key,
            w_value=w_value,
            x=x,
            grad_middle=grad_middle,
        ),
    )
    grad_w_gate = jnp.concatenate(
        [grad_gate_x[0], grad_gate_x[1], grad_gate_y[0], grad_gate_y[1]], axis=1
    )
    grad_w_up = jnp.concatenate([grad_up_rows[0], grad_up_rows[1]], axis=1)
    grad_w_down = jnp.swapaxes(grad_down, 1, 2).reshape(-1, width // 16)
    return (
        result[None],
        grad_inputs[None],
        gains[0, : width // 16],
        grad_w_query,
        grad_w_key,
        grad_w_value,
        grad_out.T,
        gains[1, : width // 16],
        grad_w_gate,
        grad_w_up,
        grad_w_down,
    )


def solution(mesh):
    in_specs = (
        P("dp", "seq", None),
        P("dp", None),
        P(),
        P(None, "tensor"),
        P(None, "tensor"),
        P(None, "tensor"),
        P("tensor", None),
        P(),
        P(None, "tensor"),
        P(None, "tensor"),
        P("tensor", None),
        P("dp", "seq", None),
    )
    out_specs = (
        P("dp", "seq", None),
        P("dp", "seq", None),
        P(("dp", "seq")),
        P(("dp", "seq"), "tensor"),
        P(("dp", "seq"), "tensor"),
        P(("dp", "seq"), "tensor"),
        P("tensor", ("dp", "seq")),
        P(("dp", "seq")),
        P(("dp", "seq"), "tensor"),
        P(("dp", "seq"), "tensor"),
        P("tensor", ("dp", "seq")),
    )
    body = local_paired if tuple(mesh.shape[name] for name in ("dp", "seq", "tensor")) == (4, 4, 2) else local
    return jax.shard_map(body, mesh=mesh, in_specs=in_specs, out_specs=out_specs, check_vma=False)
```

```python
import jax
import jax.numpy as jnp
from jax import lax
from jax.experimental import pallas as pl
from jax.experimental.pallas import tpu as pltpu
from jax.sharding import PartitionSpec as P

HQ = 16
KV = 8
HD = 96


epsilon = 1e-05
rope_theta = 100000.0
masked_score = -1e30


def doc_layout(length_row, first_row, row_count):
    positions = first_row + jnp.arange(row_count, dtype=jnp.int32)
    doc_ends = jnp.cumsum(length_row)
    passed = (positions[:, None] >= doc_ends[None, :]).astype(jnp.int32)
    segment = jnp.sum(passed, axis=1)
    doc_start = jnp.sum(passed * length_row[None, :], axis=1)
    return (positions, segment, positions - doc_start, segment < length_row.shape[0])


def rope_tables(offsets):
    half_size = HD // 2
    inverse = rope_theta ** (-2.0 * jnp.arange(half_size, dtype=jnp.float32) / HD)
    angles = offsets.astype(jnp.float32)[:, None] * inverse[None, :]
    return (jnp.cos(angles)[:, None, :], jnp.sin(angles)[:, None, :])


def rotate(values, cosine, sine_table):
    half_size = values.shape[-1] // 2
    first_half = values[..., :half_size]
    second_half = values[..., half_size:]
    return jnp.concatenate(
        [
            first_half * cosine - second_half * sine_table,
            second_half * cosine + first_half * sine_table,
        ],
        axis=-1,
    )


def rotate_back(gradient, cosine, sine_table):
    half_size = gradient.shape[-1] // 2
    first_half = gradient[..., :half_size]
    second_half = gradient[..., half_size:]
    return jnp.concatenate(
        [
            first_half * cosine + second_half * sine_table,
            second_half * cosine - first_half * sine_table,
        ],
        axis=-1,
    )


def outer_sum(left, right):
    return lax.dot_general(
        left, right, (((0,), (0,)), ((), ())), preferred_element_type=jnp.float32
    )


def times_transpose(left, right):
    return lax.dot_general(
        left, right, (((1,), (1,)), ((), ())), preferred_element_type=jnp.float32
    )


def allowed_pairs(query_rows, query_seg, key_rows, key_seg, key_valid):
    same_doc = (
        (query_seg[:, None] == key_seg[None, :])
        & (key_rows[None, :] <= query_rows[:, None])
        & key_valid[None, :]
    )
    return same_doc | (key_rows[None, :] == query_rows[:, None])


def score_block(queries, key_part, allowed_mask):
    raw_scores = jnp.einsum("qkgd,jkd->kgqj", queries, key_part, preferred_element_type=jnp.float32)
    return jnp.where(allowed_mask[None, None], raw_scores * HD ** (-0.5), masked_score)


def backward_terms(queries, grad_heads, log_total, delta, key_part, value_part, allowed_mask):
    probs = jnp.exp(score_block(queries, key_part, allowed_mask) - log_total[..., None])
    grad_probs = jnp.einsum(
        "qkgd,jkd->kgqj", grad_heads, value_part, preferred_element_type=jnp.float32
    )
    grad_scores = (probs * (grad_probs - delta[..., None])).astype(jnp.bfloat16)
    return (probs.astype(jnp.bfloat16), grad_scores)


def block_loader(keys_all, values_all, query_info, key_info, block_rows):
    query_rows, query_seg = query_info

    def load_block(block_index):
        first_key = block_index * block_rows
        key_part = lax.dynamic_slice_in_dim(keys_all, first_key, block_rows, 0)
        value_part = lax.dynamic_slice_in_dim(values_all, first_key, block_rows, 0)
        key_rows, key_seg, key_valid = tuple(
            (lax.dynamic_slice_in_dim(member, first_key, block_rows, 0) for member in key_info)
        )
        return (
            key_part,
            value_part,
            allowed_pairs(query_rows, query_seg, key_rows, key_seg, key_valid),
        )

    return load_block


def attend_forward(queries, keys_all, values_all, query_info, key_info, block_rows):
    last_row = query_info[0][-1]
    block_count = keys_all.shape[0] // block_rows
    stat_shape = (queries.shape[1], queries.shape[2], queries.shape[0])
    load_block = block_loader(keys_all, values_all, query_info, key_info, block_rows)

    def stats_step(block_index, running):

        def stats_compute(state_in):
            row_max, row_sum = state_in
            key_part, value_part, allowed_mask = load_block(block_index)
            scores = score_block(queries, key_part, allowed_mask)
            new_max = jnp.maximum(row_max, jnp.max(scores, axis=-1))
            new_sum = row_sum * jnp.exp(row_max - new_max) + jnp.sum(
                jnp.exp(scores - new_max[..., None]), axis=-1
            )
            return (new_max, new_sum)

        return lax.cond(
            block_index * block_rows <= last_row, stats_compute, lambda state_in: state_in, running
        )

    start_stats = (
        jnp.full(stat_shape, masked_score, jnp.float32),
        jnp.zeros(stat_shape, jnp.float32),
    )
    row_max, row_sum = lax.fori_loop(0, block_count, stats_step, start_stats)
    log_total = row_max + jnp.log(row_sum)

    def output_step(block_index, running):

        def output_compute(state_in):
            kept_sum, rest_sum = state_in
            key_part, value_part, allowed_mask = load_block(block_index)
            probs = jnp.exp(score_block(queries, key_part, allowed_mask) - log_total[..., None])
            probs_low = probs.astype(jnp.bfloat16)
            rest_low = (probs - probs_low.astype(jnp.float32)).astype(jnp.bfloat16)
            kept_sum = kept_sum + jnp.einsum(
                "kgqj,jkd->qkgd", probs_low, value_part, preferred_element_type=jnp.float32
            )
            rest_sum = rest_sum + jnp.einsum(
                "kgqj,jkd->qkgd", rest_low, value_part, preferred_element_type=jnp.float32
            )
            return (kept_sum, rest_sum)

        return lax.cond(
            block_index * block_rows <= last_row, output_compute, lambda state_in: state_in, running
        )

    zero_out = jnp.zeros(queries.shape, jnp.float32)
    kept_sum, rest_sum = lax.fori_loop(0, block_count, output_step, (zero_out, zero_out))
    return (log_total, kept_sum, kept_sum + rest_sum)


def attend_backward(
    queries, grad_heads, log_total, delta, keys_all, values_all, query_info, key_info, block_rows
):
    last_row = query_info[0][-1]
    block_count = keys_all.shape[0] // block_rows
    key_width = keys_all.shape[1] * keys_all.shape[2]
    load_block = block_loader(keys_all, values_all, query_info, key_info, block_rows)

    def grad_step(running, block_index):

        def grad_compute(state_in):
            key_part, value_part, allowed_mask = load_block(block_index)
            probs_low, grad_scores = backward_terms(
                queries, grad_heads, log_total, delta, key_part, value_part, allowed_mask
            )
            grad_query = state_in + jnp.einsum(
                "kgqj,jkd->qkgd", grad_scores, key_part, preferred_element_type=jnp.float32
            )
            key_terms = ()
            grad_key = jnp.einsum(
                "kgqj,qkgd->jkd", grad_scores, queries, preferred_element_type=jnp.float32
            )
            grad_value = jnp.einsum(
                "kgqj,qkgd->jkd", probs_low, grad_heads, preferred_element_type=jnp.float32
            )
            key_terms = (
                grad_key.reshape(block_rows, key_width),
                grad_value.reshape(block_rows, key_width),
            )
            return (grad_query, key_terms)

        def skipped(state_in):
            key_terms = ()
            zero_block = jnp.zeros((block_rows, key_width), jnp.float32)
            key_terms = (zero_block, zero_block)
            return (state_in, key_terms)

        return lax.cond(block_index * block_rows <= last_row, grad_compute, skipped, running)

    grad_query, key_terms = lax.scan(
        grad_step, jnp.zeros(queries.shape, jnp.float32), jnp.arange(block_count, dtype=jnp.int32)
    )
    key_terms = tuple((member.reshape(block_count * block_rows, key_width) for member in key_terms))
    return (grad_query, key_terms)


def local(
    hidden_in,
    lengths,
    attn_gain,
    w_query,
    w_key,
    w_value,
    w_out,
    mlp_gain,
    w_gate,
    w_up,
    w_down,
    out_grad,
):
    seq_count = hidden_in.shape[0]
    tok_rows = hidden_in.shape[1]
    width = hidden_in.shape[2]
    row_total = seq_count * tok_rows
    seq_total = tok_rows * lax.axis_size("seq")
    first_row = lax.axis_index("seq") * tok_rows
    half_rows = row_total // lax.axis_size("tensor")
    half_start = lax.axis_index("tensor") * half_rows
    block_rows = min(512, seq_total)
    kv_local = w_key.shape[1] // HD
    group_size = HQ // KV
    heads_local = kv_local * group_size

    def own_half(array_in):
        return lax.dynamic_slice_in_dim(array_in, half_start, half_rows, 0)

    inputs = hidden_in.reshape(row_total, width).astype(jnp.float32)
    query_rows, query_seg, query_offsets, query_valid = jax.vmap(
        lambda length_row: doc_layout(length_row, first_row, tok_rows)
    )(lengths)
    key_layout = jax.vmap(lambda length_row: doc_layout(length_row, 0, seq_total))(lengths)
    cosine, sine_table = rope_tables(query_offsets.reshape(row_total))
    valid_rows = query_valid.reshape(row_total).astype(jnp.float32)[:, None]
    inverse_one = lax.rsqrt(jnp.mean(inputs * inputs, axis=-1, keepdims=True) + epsilon)
    normed_one = inputs * inverse_one
    attn_input = (normed_one * attn_gain).astype(jnp.bfloat16)
    query_raw = jnp.dot(attn_input, w_query, preferred_element_type=jnp.float32).reshape(
        row_total, heads_local, HD
    )
    key_raw = jnp.dot(attn_input, w_key, preferred_element_type=jnp.float32).reshape(
        row_total, kv_local, HD
    )
    values_own = (
        jnp.dot(attn_input, w_value, preferred_element_type=jnp.float32)
        .astype(jnp.bfloat16)
        .reshape(seq_count, tok_rows, kv_local * HD)
    )
    queries = (
        rotate(query_raw, cosine, sine_table)
        .astype(jnp.bfloat16)
        .reshape(seq_count, tok_rows, kv_local, group_size, HD)
    )
    keys_own = (
        rotate(key_raw, cosine, sine_table)
        .astype(jnp.bfloat16)
        .reshape(seq_count, tok_rows, kv_local * HD)
    )
    keys_all, values_all = (
        lax.all_gather(keys_own, "seq", axis=1, tiled=True),
        lax.all_gather(values_own, "seq", axis=1, tiled=True),
    )
    key_shape = (seq_count, seq_total, kv_local, HD)

    def forward_one(items):
        query_s, key_s, value_s, rows_s, seg_s, key_rows, key_seg, key_valid = items
        return attend_forward(
            query_s, key_s, value_s, (rows_s, seg_s), (key_rows, key_seg, key_valid), block_rows
        )

    log_total, kept_sum, exact_sum = lax.map(
        forward_one,
        (
            queries,
            keys_all.reshape(key_shape),
            values_all.reshape(key_shape),
            query_rows,
            query_seg,
            key_layout[0],
            key_layout[1],
            key_layout[3],
        ),
    )
    attn_heads = (kept_sum.reshape(row_total, heads_local * HD) * valid_rows).astype(jnp.bfloat16)
    attn_part = jnp.dot(attn_heads, w_out, preferred_element_type=jnp.float32)
    middle = own_half(inputs) + lax.psum_scatter(
        attn_part, "tensor", scatter_dimension=0, tiled=True
    )
    inverse_two = lax.rsqrt(jnp.mean(middle * middle, axis=-1, keepdims=True) + epsilon)
    normed_two = middle * inverse_two
    mlp_half = (normed_two * mlp_gain).astype(jnp.bfloat16)
    mlp_input = lax.all_gather(mlp_half, "tensor", axis=0, tiled=True)
    gate = jnp.dot(mlp_input, w_gate, preferred_element_type=jnp.float32)
    upward = jnp.dot(mlp_input, w_up, preferred_element_type=jnp.float32)
    hidden = (jax.nn.silu(gate) * upward).astype(jnp.bfloat16)
    mlp_part = jnp.dot(hidden, w_down, preferred_element_type=jnp.float32)
    result = middle + lax.psum_scatter(
        mlp_part.astype(jnp.bfloat16), "tensor", scatter_dimension=0, tiled=True
    ).astype(jnp.float32)
    cotangent = out_grad.reshape(row_total, width)
    grad_hidden = times_transpose(cotangent, w_down)
    sigmoid_gate = jax.nn.sigmoid(gate)
    grad_gate = (grad_hidden * upward * sigmoid_gate * (1.0 + gate * (1.0 - sigmoid_gate))).astype(
        jnp.bfloat16
    )
    grad_upward = (grad_hidden * gate * sigmoid_gate).astype(jnp.bfloat16)
    grad_w_down = outer_sum(hidden, cotangent)
    grad_w_gate = outer_sum(mlp_input, grad_gate)
    grad_w_up = outer_sum(mlp_input, grad_upward)
    grad_mlp_in = lax.psum_scatter(
        times_transpose(grad_gate, w_gate) + times_transpose(grad_upward, w_up),
        "tensor",
        scatter_dimension=0,
        tiled=True,
    )
    mlp_gain_part = jnp.sum(grad_mlp_in * normed_two, axis=0)
    scaled_two = grad_mlp_in * mlp_gain
    grad_middle = own_half(cotangent).astype(jnp.float32) + inverse_two * (
        scaled_two - normed_two * jnp.mean(scaled_two * normed_two, axis=-1, keepdims=True)
    )
    grad_middle_low = lax.all_gather(grad_middle.astype(jnp.bfloat16), "tensor", axis=0, tiled=True)
    grad_w_out = outer_sum(attn_heads, grad_middle_low)
    grad_heads = (
        times_transpose(grad_middle_low, w_out).astype(jnp.bfloat16)
        * valid_rows.astype(jnp.bfloat16)
    ).reshape(seq_count, tok_rows, kv_local, group_size, HD)
    delta = jnp.einsum(
        "sqkgd,sqkgd->skgq", grad_heads, exact_sum, preferred_element_type=jnp.float32
    )
    keys_back, values_back = (
        lax.all_gather(keys_own, "seq", axis=1, tiled=True),
        lax.all_gather(values_own, "seq", axis=1, tiled=True),
    )
    keys_back = keys_back.reshape(key_shape)
    values_back = values_back.reshape(key_shape)

    def backward_one():

        def run(items):
            (
                query_s,
                grad_s,
                log_s,
                delta_s,
                key_s,
                value_s,
                rows_s,
                seg_s,
                key_rows,
                key_seg,
                key_valid,
            ) = items
            return attend_backward(
                query_s,
                grad_s,
                log_s,
                delta_s,
                key_s,
                value_s,
                (rows_s, seg_s),
                (key_rows, key_seg, key_valid),
                block_rows,
            )

        return run

    backward_items = (
        queries,
        grad_heads,
        log_total,
        delta,
        keys_back,
        values_back,
        query_rows,
        query_seg,
        key_layout[0],
        key_layout[1],
        key_layout[3],
    )
    grad_query, key_terms = lax.map(backward_one(), backward_items)
    grad_key_sum, grad_value_sum = (
        lax.psum_scatter(
            key_terms[0].astype(jnp.bfloat16), "seq", scatter_dimension=1, tiled=True
        ).astype(jnp.float32),
        lax.psum_scatter(
            key_terms[1].astype(jnp.bfloat16), "seq", scatter_dimension=1, tiled=True
        ).astype(jnp.float32),
    )
    grad_key_rot = grad_key_sum.reshape(row_total, kv_local, HD) * HD ** (-0.5)
    grad_key_low = (
        rotate_back(grad_key_rot, cosine, sine_table)
        .astype(jnp.bfloat16)
        .reshape(row_total, kv_local * HD)
    )
    grad_value_low = grad_value_sum.reshape(row_total, kv_local * HD).astype(jnp.bfloat16)
    grad_query_rot = (grad_query * HD ** (-0.5)).reshape(row_total, heads_local, HD)
    grad_query_low = (
        rotate_back(grad_query_rot, cosine, sine_table)
        .astype(jnp.bfloat16)
        .reshape(row_total, heads_local * HD)
    )
    grad_w_query = outer_sum(attn_input, grad_query_low)
    grad_w_key = outer_sum(attn_input, grad_key_low)
    grad_w_value = outer_sum(attn_input, grad_value_low)
    attn_back_part = (
        times_transpose(grad_query_low, w_query)
        + times_transpose(grad_key_low, w_key)
        + times_transpose(grad_value_low, w_value)
    )
    grad_attn_in = lax.psum_scatter(
        attn_back_part.astype(jnp.bfloat16), "tensor", scatter_dimension=0, tiled=True
    ).astype(jnp.float32)
    normed_half = own_half(normed_one)
    attn_gain_part = jnp.sum(grad_attn_in * normed_half, axis=0)
    scaled_one = grad_attn_in * attn_gain
    grad_inputs = grad_middle + own_half(inverse_one) * (
        scaled_one - normed_half * jnp.mean(scaled_one * normed_half, axis=-1, keepdims=True)
    )
    grad_attn_gain, grad_mlp_gain = lax.psum((attn_gain_part, mlp_gain_part), "tensor")
    reduced = tuple(
        (
            lax.psum_scatter(grad_attn_gain, ("dp", "seq"), scatter_dimension=0, tiled=True),
            lax.psum_scatter(grad_w_query, ("dp", "seq"), scatter_dimension=0, tiled=True),
            lax.psum_scatter(grad_w_key, ("dp", "seq"), scatter_dimension=0, tiled=True),
            lax.psum_scatter(grad_w_value, ("dp", "seq"), scatter_dimension=0, tiled=True),
            lax.psum_scatter(grad_w_out, ("dp", "seq"), scatter_dimension=1, tiled=True),
            lax.psum_scatter(grad_mlp_gain, ("dp", "seq"), scatter_dimension=0, tiled=True),
            lax.psum_scatter(grad_w_gate, ("dp", "seq"), scatter_dimension=0, tiled=True),
            lax.psum_scatter(grad_w_up, ("dp", "seq"), scatter_dimension=0, tiled=True),
            lax.psum_scatter(grad_w_down, ("dp", "seq"), scatter_dimension=1, tiled=True),
        )
    )
    result_all, grad_all = (
        lax.all_gather(result.astype(jnp.bfloat16), "tensor", axis=0, tiled=True),
        lax.all_gather(grad_inputs.astype(jnp.bfloat16), "tensor", axis=0, tiled=True),
    )
    out_shape = (seq_count, tok_rows, width)
    return (
        result_all.reshape(out_shape),
        grad_all.reshape(out_shape),
        reduced[0],
        reduced[1],
        reduced[2],
        reduced[3],
        reduced[4],
        reduced[5],
        reduced[6],
        reduced[7],
        reduced[8],
    )


LOG2E = 1.4426950408889634
QUERY_TILE = 256
KEY_TILE = 512
PAD = 128
ROW_TILE = 256
MEBI = 1024 * 1024
VMEM_LIMIT = 56 * MEBI
IN_VMEM = pl.BlockSpec(memory_space=pltpu.VMEM)
IN_ANY = pl.BlockSpec(memory_space=pl.ANY)


def doc_start(ends, rows):
    start = jnp.zeros_like(rows)
    for end in ends:
        start = jnp.where(rows >= end, end, start)
    return jnp.where(rows >= ends[-1], rows, start)


def dot_plain(left, right):
    return jnp.dot(left, right, preferred_element_type=jnp.float32)


def shape_of(*dims, dtype=jnp.bfloat16):
    return jax.ShapeDtypeStruct(dims, dtype)


def norm_scale(values):
    return lax.rsqrt(jnp.mean(values * values, axis=-1, keepdims=True) + epsilon)


def partner(position, step):
    if step == 0:
        return position
    if step == 1:
        return position + 1 - 2 * (position % 2)
    if step == 2:
        return position + 2 - 4 * (position // 2)
    return 3 - position


def greet(places):
    barrier = pltpu.get_barrier_semaphore()
    for device in places:
        pl.semaphore_signal(barrier, inc=1, device_id=device, device_id_type=pl.DeviceIdType.MESH)
    pl.semaphore_wait(barrier, len(places))


class Load:
    def __init__(self, source, target, sems, free):
        self.index, self.free = free.pop(0), free
        self.copy = pltpu.make_async_copy(source, target, sems.at[self.index])
        self.copy.start()

    def wait(self):
        self.copy.wait()
        self.free.append(self.index)


class Copies:
    def __init__(self, load_sem, send_sem, recv_sem):
        self.sems = (load_sem, send_sem, recv_sem)
        self.free, self.sends = list(range(load_sem.shape[0])), 0

    def load(self, source, target):
        return Load(source, target, self.sems[0], self.free)

    def send(self, source, target, device):
        copy = pltpu.make_async_remote_copy(
            src_ref=source,
            dst_ref=target,
            send_sem=self.sems[1].at[self.sends],
            recv_sem=self.sems[2].at[self.sends],
            device_id=device,
            device_id_type=pl.DeviceIdType.MESH,
        )
        copy.start()
        self.sends += 1
        return copy


def wait_all(copies):
    for copy in copies:
        copy.wait()


def forward_kernel(
    ends_ref,
    x_far,
    gain_one,
    gain_two,
    cotangent_far,
    cosine_far,
    sine_far,
    w_query,
    w_key,
    w_value,
    w_out_far,
    w_gate_far,
    w_up_far,
    w_down_far,
    lse,
    gain_sum,
    heads_out,
    keys_out,
    values_out,
    exact_out,
    cotangent_x,
    normed_one_out,
    shards,
    normed_out,
    normed_x,
    normed_y,
    hidden_out,
    grad_gate_out,
    grad_up_out,
    hidden_x,
    up_y,
    merged_out,
    grad_low_out,
    grad_middle_out,
    down_away,
    up_away,
    back_0,
    back_1,
    back_2,
    back_3,
    result,
    w_out,
    w_gate,
    w_up,
    w_down,
    x,
    cotangent,
    cosine,
    sine,
    normed_one,
    packed,
    packed_in,
    heads,
    keys,
    values,
    exact,
    low,
    low_in,
    merged,
    part,
    other,
    normed,
    hidden,
    grad_gate,
    grad_up,
    grad_part,
    grad_other,
    grad_middle,
    free_sem,
    load_sem,
    send_sem,
    recv_sem,
):
    dp_index, place, core = (lax.axis_index(name) for name in ("dp", "seq", "tensor"))
    along_x, along_y = dp_index % 2, dp_index // 2
    rows, width = x.shape
    units = w_up.shape[1]
    half_rows, quarter_rows = rows // 2, rows // 4
    half = pl.ds(pl.multiple_of(core * half_rows, half_rows), half_rows)
    first_quarter = pl.ds(pl.multiple_of(core * half_rows, quarter_rows), quarter_rows)
    second_quarter = pl.ds(
        pl.multiple_of(core * half_rows + quarter_rows, quarter_rows), quarter_rows
    )
    peers = [{"seq": partner(place, d)} for d in (1, 2, 3)]
    over_x, over_y = {"dp": partner(dp_index, 1)}, {"dp": partner(dp_index, 2)}
    across = {"tensor": 1 - core}
    tiles = [pl.ds(block * ROW_TILE, ROW_TILE) for block in range(rows // ROW_TILE)]
    copies = Copies(load_sem, send_sem, recv_sem)
    send, load = copies.send, copies.load
    late = []

    columns = [w.shape[1] for w in (w_query, w_key, w_value)]
    starts = [0, columns[0], columns[0] + columns[1]]
    weight_parts = [
        w_gate.at[:, pl.ds(start, size)] for start, size in zip(starts, columns, strict=True)
    ]
    own_rows = pl.ds(pl.multiple_of(place * rows, rows), rows)
    x_load = load(x_far, x)
    table_loads = [load(cosine_far.at[own_rows], cosine), load(sine_far.at[own_rows], sine)]
    head_loads = [
        load(w, target)
        for w, target in zip((w_value, w_key, w_query), reversed(weight_parts), strict=True)
    ]
    greet([*peers, over_x, over_y, across])
    beside_copy = send(cotangent_far.at[half], cotangent_x.at[half], over_x)
    other_loads = [load(w_out_far, w_out), load(w_up_far, w_up), load(w_down_far, w_down)]
    cotangent_load = load(cotangent_far, cotangent)

    heads[...] = jnp.zeros_like(heads)
    keys[...] = jnp.zeros_like(keys)
    values[...] = jnp.zeros_like(values)
    x_load.wait()
    packed_copies = []
    for block, tile in enumerate(tiles):
        inputs = x[tile, :].astype(jnp.float32)
        rows_low = (inputs * norm_scale(inputs) * gain_one[...]).astype(jnp.bfloat16)
        normed_one[tile, :] = rows_low
        if block == 0:
            wait_all(head_loads)
            wait_all(table_loads)
        cos_part, sin_part = cosine[tile, :HD], sine[tile, :HD]

        def turned(value, cos_part=cos_part, sin_part=sin_part):
            swapped = jnp.concatenate([value[:, HD // 2 :], value[:, : HD // 2]], axis=1)
            return (value * cos_part + swapped * sin_part).astype(jnp.bfloat16)

        value = dot_plain(rows_low, weight_parts[2][...])
        for head in range(4):
            packed[head, tile, 3 * HD :] = value[:, head * HD : (head + 1) * HD].astype(jnp.bfloat16)
        key = dot_plain(rows_low, weight_parts[1][...])
        for head in range(4):
            packed[head, tile, 2 * HD : 3 * HD] = turned(key[:, head * HD : (head + 1) * HD])
        query = dot_plain(rows_low, weight_parts[0][...])
        for head in range(4):
            first = 2 * head * HD
            packed[head, tile, :HD] = turned(query[:, first : first + HD])
            packed[head, tile, HD : 2 * HD] = turned(query[:, first + HD : first + 2 * HD])
        for d in (1, 2, 3):
            packed_copies.append(
                (
                    d,
                    tile,
                    send(packed.at[partner(place, d), tile], packed_in.at[d - 1, tile], peers[d - 1]),
                )
            )
    gate_load = load(w_gate_far, w_gate)
    outs = [load(normed_one, normed_one_out)]

    def unpack(source, block):
        here = pl.ds(pl.multiple_of(block * rows, rows), rows)
        heads[0, here, :HD] = source[:, :HD]
        heads[1, here, :HD] = source[:, HD : 2 * HD]
        keys[here, :HD] = source[:, 2 * HD : 3 * HD]
        values[here, :HD] = source[:, 3 * HD :]

    unpack(packed.at[place], place)
    beside_copy.wait()
    cotangent_copy = send(cotangent_x.at[half], cotangent_x.at[half], across)
    for d, tile, copy in packed_copies:
        copy.wait()
    for d in (1, 2, 3):
        unpack(packed_in.at[d - 1], partner(place, d))
    outs += [load(heads, heads_out), load(keys, keys_out), load(values, values_out)]

    shard_near = send(normed_one.at[half], shards.at[0, half], peers[0])
    shard_far = [send(normed_one.at[first_quarter], shards.at[1, first_quarter], peers[1])]

    ends = [ends_ref[index] for index in range(4)]
    scale = HD ** (-0.5) * LOG2E

    def attend(first, key_tiles):
        tile = pl.ds(first, QUERY_TILE)
        queries = jnp.concatenate([heads[0, tile, :], heads[1, tile, :]], axis=0)
        row_ids = lax.broadcasted_iota(jnp.int32, (2 * QUERY_TILE, 1), 0) % QUERY_TILE + first
        doc_starts = doc_start(ends, row_ids)

        def key_step(key_index, state):
            row_max, row_sum, summed = state
            first_key = pl.multiple_of(key_index * KEY_TILE, KEY_TILE)
            key_rows = pl.ds(first_key, KEY_TILE)
            scores = scale * times_transpose(queries, keys[key_rows, :])
            key_ids = lax.broadcasted_iota(jnp.int32, (1, KEY_TILE), 1) + first_key
            scores = jnp.where((key_ids >= doc_starts) & (key_ids <= row_ids), scores, masked_score)
            new_max = jnp.maximum(row_max, jnp.max(scores, axis=1, keepdims=True))
            probs = jnp.exp2(scores - new_max)
            shrink = jnp.exp2(row_max - new_max)
            row_sum = row_sum * shrink + jnp.sum(probs, axis=1, keepdims=True)
            summed = summed * shrink + dot_plain(probs.astype(jnp.bfloat16), values[key_rows, :])
            return (new_max, row_sum, summed)

        row_max, row_sum, summed = lax.fori_loop(
            0,
            key_tiles,
            key_step,
            (
                jnp.full((2 * QUERY_TILE, 1), masked_score, jnp.float32),
                jnp.zeros((2 * QUERY_TILE, 1), jnp.float32),
                jnp.zeros((2 * QUERY_TILE, PAD), jnp.float32),
            ),
        )
        attended = jnp.where(row_ids < ends[-1], summed / row_sum, 0.0)
        total_log = row_max + jnp.log(row_sum) * LOG2E
        total_row = jnp.transpose(jnp.broadcast_to(total_log, (2 * QUERY_TILE, PAD)))[:1, :]
        return attended, total_row

    def attend_block(step, nothing):
        distance = 3 - step
        one, two = distance % 2, distance // 2
        flipped = place + one * (1 - 2 * (place % 2))
        block = flipped + two * (2 - 4 * (flipped // 2))

        slot = step % 2

        def attend_tile(index, nothing):
            first = pl.multiple_of(block * rows + index * QUERY_TILE, QUERY_TILE)
            attended, total_row = attend(first, block + 1)
            tile = pl.ds(first, QUERY_TILE)
            inner = pl.ds(pl.multiple_of(index * QUERY_TILE, QUERY_TILE), QUERY_TILE)
            for head in range(2):
                mine = attended[head * QUERY_TILE : (head + 1) * QUERY_TILE]
                exact[slot, head, inner, :] = mine
                low[distance, inner, head * HD : (head + 1) * HD] = mine[:, :HD].astype(
                    jnp.bfloat16
                )
                lse[head : head + 1, tile] = total_row[
                    :, head * QUERY_TILE : (head + 1) * QUERY_TILE
                ]
            return nothing

        lax.fori_loop(0, rows // QUERY_TILE, attend_tile, nothing)
        return block

    low_copies, exact_copies = {}, []
    for step in range(4):
        if step > 1:
            exact_copies[step - 2].wait()
        block = attend_block(step, 0)
        exact_rows = pl.ds(pl.multiple_of(block * rows, rows), rows)
        exact_copies.append(load(exact.at[step % 2], exact_out.at[:, exact_rows]))
        distance = 3 - step
        if distance:
            low_copies[distance] = send(
                low.at[distance], low_in.at[place], peers[distance - 1]
            )
    outs += exact_copies[2:]
    low_in[place] = low[0]
    for distance in (3, 2, 1):
        low_copies[distance].wait()
    shard_far.append(send(normed_one.at[second_quarter], shards.at[1, second_quarter], peers[1]))
    shard_far[0].wait()
    shard_both = [send(shards.at[1, first_quarter], shards.at[2, first_quarter], peers[0])]
    shard_near.wait()
    late.append(send(shards.at[0, half], shards.at[0, half], across))

    for head in range(4):
        merged[:, 2 * head * HD : 2 * (head + 1) * HD] = low_in[head]
    wait_all(other_loads)
    part_copies = []
    for tile in tiles:
        part[tile, :] = dot_plain(merged[tile, :], w_out[...]).astype(jnp.bfloat16)
        part_copies.append(send(part.at[tile], other.at[tile], across))

    def middle_rows(tile):
        return x[tile, :].astype(jnp.float32) + (
            part[tile, :].astype(jnp.float32) + other[tile, :].astype(jnp.float32)
        )

    for tile, copy in zip(tiles, part_copies, strict=True):
        copy.wait()
        middle = middle_rows(tile)
        normed[tile, :] = (middle * norm_scale(middle) * gain_two[...]).astype(jnp.bfloat16)
    normed_copies = [
        send(normed.at[half], normed_x.at[half], over_x),
        send(normed.at[half], normed_y.at[half], over_y),
    ]
    outs += [load(normed, normed_out), load(merged, merged_out)]
    cotangent_load.wait()
    gate_load.wait()

    unit_tile = units // 4

    def unit_step(index, nothing):
        columns = pl.ds(pl.multiple_of(index * unit_tile, unit_tile), unit_tile)
        inner = pl.ds(pl.multiple_of((index % 2) * unit_tile, unit_tile), unit_tile)
        rows_low = normed[...]
        gate, up = dot_plain(rows_low, w_gate[:, columns]), dot_plain(rows_low, w_up[:, columns])
        back = times_transpose(cotangent[...], w_down[columns, :])
        sigma = jax.nn.sigmoid(gate)
        swish = gate * sigma
        hidden[index // 2, :, inner] = (swish * up).astype(jnp.bfloat16)
        grad_gate[index] = (back * up * sigma * (1.0 + gate * (1.0 - sigma))).astype(jnp.bfloat16)
        grad_up[index // 2, :, inner] = (back * swish).astype(jnp.bfloat16)
        return nothing

    lax.fori_loop(0, 4, unit_step, 0)
    unit_copies = [
        send(hidden.at[1 - along_x], hidden_x, over_x),
        send(grad_up.at[1 - along_y], up_y, over_y),
    ]
    outs += [load(hidden, hidden_out), load(grad_gate, grad_gate_out), load(grad_up, grad_up_out)]

    width_tile = width // 3
    grad_copies = []
    for index in range(3):
        columns = pl.ds(index * width_tile, width_tile)
        total = None
        for quarter in range(4):
            inner = pl.ds(quarter * unit_tile, unit_tile)
            term = times_transpose(grad_gate[quarter], w_gate[columns, inner])
            total = term if total is None else total + term
        for side in range(2):
            inner = pl.ds(side * 2 * unit_tile, 2 * unit_tile)
            total = total + times_transpose(grad_up[side], w_up[columns, inner])
        grad_part[:, columns] = total.astype(jnp.bfloat16)
        grad_copies.append(send(grad_part.at[:, columns], grad_other.at[:, columns], across))
    shard_far[1].wait()
    late.append(send(shards.at[1, half], shards.at[1, half], across))
    shard_both.append(send(shards.at[1, second_quarter], shards.at[2, second_quarter], peers[0]))
    wait_all(grad_copies)

    for block, tile in enumerate(tiles):
        middle = middle_rows(tile)
        inverse = norm_scale(middle)
        unit_rows = middle * inverse
        grad_normed = grad_part[tile, :].astype(jnp.float32) + grad_other[tile, :].astype(
            jnp.float32
        )
        gain_term = jnp.sum(grad_normed * unit_rows, axis=0, keepdims=True)
        gain_sum[...] = gain_term if block == 0 else gain_sum[...] + gain_term
        scaled = grad_normed * gain_two[...]
        total = cotangent[tile, :].astype(jnp.float32) + inverse * (
            scaled - unit_rows * jnp.mean(scaled * unit_rows, axis=-1, keepdims=True)
        )
        if block:
            outs.pop().wait()
        grad_middle[...] = total
        outs.append(load(grad_middle, grad_middle_out.at[tile]))
        rows_low = total.astype(jnp.bfloat16)
        grad_part[tile, :] = rows_low
        row_ids = lax.broadcasted_iota(jnp.int32, (ROW_TILE, 1), 0) + (
            place * rows + block * ROW_TILE
        )
        back = jnp.where(row_ids < ends[3], times_transpose(rows_low, w_out[...]), 0.0)
        for head in range(4):
            low[head, tile, :] = back[:, 2 * head * HD : 2 * (head + 1) * HD].astype(jnp.bfloat16)
    pl.semaphore_signal(free_sem, inc=1, device_id=across, device_id_type=pl.DeviceIdType.MESH)
    back_copies = [
        send(low.at[partner(place, d)], out, peers[d - 1])
        for d, out in ((1, back_1), (2, back_2), (3, back_3))
    ]
    outs += [
        load(low.at[place], back_0),
        load(grad_part, grad_low_out),
    ]

    outs[0].wait()
    down_copies = []
    for index in range(3):
        columns = pl.ds(index * width_tile, width_tile)
        total = dot_plain(hidden[0], w_down[: units // 2, columns]) + dot_plain(
            hidden[1], w_down[units // 2 :, columns]
        )
        normed_one[:, columns] = total.astype(jnp.bfloat16)
        if index == 0:
            pl.semaphore_wait(free_sem, 1)
        down_copies.append(send(normed_one.at[:, columns], grad_other.at[:, columns], across))

    wait_all(normed_copies)
    late.append(send(normed_x.at[half], normed_x.at[half], across))
    normed_copy = send(normed_y.at[half], normed_y.at[half], across)
    wait_all(unit_copies)
    cotangent_copy.wait()
    normed_copy.wait()
    cotangent_slot, normed_slot = w_gate.at[pl.ds(0, rows), pl.ds(0, width)], w_gate.at[
        pl.ds(rows, rows), pl.ds(0, width)
    ]
    hidden_slot, up_slot = w_up.at[pl.ds(0, rows), pl.ds(0, units // 2)], w_up.at[
        pl.ds(rows, rows), pl.ds(0, units // 2)
    ]
    slot_loads = [
        load(cotangent_x, cotangent_slot),
        load(hidden_x, hidden_slot),
        load(normed_y, normed_slot),
        load(up_y, up_slot),
    ]
    wait_all(down_copies)
    for tile in tiles:
        x[tile, :] = (
            middle_rows(tile)
            + (normed_one[tile, :].astype(jnp.float32) + grad_other[tile, :].astype(jnp.float32))
        ).astype(jnp.bfloat16)
    outs.append(load(x, result))
    wait_all(shard_both)
    late.append(send(shards.at[2, half], shards.at[2, half], across))
    wait_all(slot_loads)
    block_rows = width // 4

    def away(slot, lefts, rights, block, target):
        columns = pl.ds(pl.multiple_of(block * block_rows, block_rows), block_rows)
        total = outer_sum(lefts[0][:, columns], rights[0][...]) + outer_sum(
            lefts[1][:, columns], rights[1][...]
        )
        place_rows = w_down.at[pl.ds(slot * block_rows, block_rows), pl.ds(0, units // 2)]
        place_rows[...] = total.astype(jnp.bfloat16)
        return load(place_rows, target)

    down_sides = ((cotangent, cotangent_slot), (hidden.at[along_x], hidden_slot))
    up_sides = ((normed, normed_slot), (grad_up.at[along_y], up_slot))
    for index in range(2):
        outs.append(
            away(index, *down_sides, 2 * (1 - along_y) + index, down_away.at[index])
        )
        outs.append(
            away(2 + index, *up_sides, 2 * index + 1 - along_x, up_away.at[index])
        )
    wait_all(back_copies)
    wait_all(late)
    wait_all(outs[1:])


def forward(ends, x, gains, cotangent, tables, weights):
    rows, width = x.shape
    w_query, w_key, w_value, w_out, w_gate, w_up, w_down = weights
    units = w_gate.shape[1]
    total = 4 * rows
    f32 = jnp.float32
    wide, message = shape_of(rows, width), shape_of(rows, 2 * HD)
    by_half, by_quarter = shape_of(2, rows, units // 2), shape_of(4, rows, units // 4)
    block = shape_of(2, width // 4, units // 2)
    vmem_outs = (shape_of(2, total, dtype=f32), shape_of(1, width, dtype=f32))
    far_outs = (
        shape_of(2, total, PAD),
        shape_of(total, PAD),
        shape_of(total, PAD),
        shape_of(2, total, PAD, dtype=f32),
        wide,
        wide,
        shape_of(3, rows, width),
        wide,
        wide,
        wide,
        by_half,
        by_quarter,
        by_half,
        shape_of(rows, units // 2),
        shape_of(rows, units // 2),
        shape_of(rows, w_out.shape[0]),
        wide,
        shape_of(rows, width, dtype=f32),
        block,
        block,
        *(message,) * 4,
        wide,
    )

    def low(*dims):
        return pltpu.VMEM(dims, jnp.bfloat16)

    scratch = [
        low(*w_out.shape),
        low(*w_gate.shape),
        low(*w_up.shape),
        low(*w_down.shape),
        low(rows, width),
        low(rows, width),
        pltpu.VMEM((rows, PAD), f32),
        pltpu.VMEM((rows, PAD), f32),
        low(rows, width),
        low(4, rows, 4 * HD),
        low(3, rows, 4 * HD),
        low(2, total, PAD),
        low(total, PAD),
        low(total, PAD),
        pltpu.VMEM((2, 2, rows, PAD), f32),
        low(4, rows, 2 * HD),
        low(4, rows, 2 * HD),
        low(rows, w_out.shape[0]),
        low(rows, width),
        low(rows, width),
        low(rows, width),
        low(*by_half.shape),
        low(*by_quarter.shape),
        low(*by_half.shape),
        low(rows, width),
        low(rows, width),
        pltpu.VMEM((ROW_TILE, width), f32),
        pltpu.SemaphoreType.REGULAR,
        pltpu.SemaphoreType.DMA((40,)),
        pltpu.SemaphoreType.DMA((44,)),
        pltpu.SemaphoreType.DMA((44,)),
    ]
    return pl.pallas_call(
        forward_kernel,
        out_shape=vmem_outs + far_outs,
        in_specs=[pl.BlockSpec(memory_space=pltpu.SMEM), IN_ANY]
        + [IN_VMEM] * 2
        + [IN_ANY] * 10,
        out_specs=(IN_VMEM,) * len(vmem_outs) + (IN_ANY,) * len(far_outs),
        scratch_shapes=scratch,
        compiler_params=pltpu.CompilerParams(
            collective_id=0, has_side_effects=True, vmem_limit_bytes=63 * MEBI
        ),
        cost_estimate=pl.CostEstimate(
            flops=16 * rows * width * units, bytes_accessed=64 * MEBI, transcendentals=0
        ),
        name="forward",
    )(ends, x, *gains, cotangent, *tables, *weights)


def backward_kernel(
    ends_ref,
    lse,
    gain,
    mlp_gain_sum,
    grad_0,
    grad_1,
    grad_2,
    grad_3,
    heads_far,
    keys_far,
    values_far,
    exact_far,
    cosine_far,
    sine_far,
    merged_far,
    grad_low_far,
    cotangent,
    cotangent_x,
    normed,
    normed_x,
    normed_y,
    hidden,
    hidden_x,
    grad_up,
    up_y,
    grad_gate,
    down_away,
    up_away,
    normed_one,
    shards,
    w_query,
    w_key,
    w_value,
    x_far,
    grad_middle_far,
    grad_down,
    grad_gate_x,
    grad_gate_y,
    grad_up_rows,
    grad_out,
    grad_query,
    grad_key,
    grad_value,
    gains,
    grad_input,
    heads,
    keys,
    values,
    exact,
    cosine,
    sine,
    grad_heads,
    key_sum,
    value_sum,
    query_backs,
    value_backs,
    query_sorted,
    value_sorted,
    merged,
    grad_low,
    cotangents,
    normeds,
    hiddens,
    ups,
    gate_xs,
    gate_ys,
    inputs,
    grad_middle,
    key,
    value,
    other,
    out_away,
    out_stay,
    gate_x_away,
    gate_y_away,
    head_away,
    head_stay,
    down_1,
    up_1,
    gate_x_1,
    gate_y_1,
    out_1,
    head_1,
    down_2,
    up_2,
    gate_x_2,
    gate_y_2,
    out_2,
    head_2,
    down_3,
    up_3,
    gate_x_3,
    gate_y_3,
    out_3,
    head_3,
    down_4,
    up_4,
    gate_x_4,
    gate_y_4,
    out_4,
    head_rows,
    gain_0,
    gain_1,
    gain_2,
    gain_3,
    load_sem,
    send_sem,
    recv_sem,
):
    dp_index, place, core = (lax.axis_index(name) for name in ("dp", "seq", "tensor"))
    along_x, along_y = dp_index % 2, dp_index // 2
    rows, width = x_far.shape
    block_rows, width_each = width // 4, width // 16
    near, far = place % 2, place // 2
    peers = [{"seq": partner(place, d)} for d in (1, 2, 3)]
    over_x, over_y = {"dp": partner(dp_index, 1)}, {"dp": partner(dp_index, 2)}
    across = {"tensor": 1 - core}
    copies = Copies(load_sem, send_sem, recv_sem)
    send, load = copies.send, copies.load

    def rows_of(block):
        return pl.ds(pl.multiple_of(block * rows, rows), rows)

    greet([*peers, over_x, over_y, across])
    down_copy = send(down_away, down_1, over_y)
    up_copy = send(up_away, up_1, over_x)
    for_heads = [load(heads_far, heads), load(keys_far, keys), load(values_far, values)]
    for_heads += [load(exact_far, exact), load(cosine_far, cosine), load(sine_far, sine)]
    first, second, third = (pl.ds(index * rows, rows) for index in range(3))
    for_out = [load(merged_far, merged), load(grad_low_far, grad_low)]
    for_head = [load(normed_one, inputs.at[0])] + [
        load(shards.at[d], inputs.at[d + 1]) for d in range(3)
    ]
    kept_columns = pl.ds(pl.multiple_of(along_y * 2 * block_rows, block_rows), 2 * block_rows)
    for_down = [
        load(cotangent.at[:, kept_columns], cotangents.at[first]),
        load(cotangent_x.at[:, kept_columns], cotangents.at[second]),
        load(hidden.at[along_x], hiddens.at[0]),
        load(hidden_x, hiddens.at[1]),
    ]
    for_gates = [
        load(normed, normeds.at[first]),
        load(normed_x, normeds.at[second]),
        load(normed_y, normeds.at[third]),
        load(grad_gate.at[along_x], gate_xs.at[0]),
        load(grad_gate.at[2 + along_y], gate_ys.at[0]),
    ]
    for_up = [load(grad_up.at[along_y], ups.at[0]), load(up_y, ups.at[1])]

    def outer(pairs, block):
        columns = pl.ds(pl.multiple_of(block * block_rows, block_rows), block_rows)
        total = None
        for left, right in pairs:
            term = outer_sum(left[:, columns], right())
            total = term if total is None else total + term
        return total

    down_pairs = [
        (cotangents.at[first], lambda: hiddens[0]),
        (cotangents.at[second], lambda: hiddens[1]),
    ]
    up_pairs = [(normeds.at[first], lambda: ups[0]), (normeds.at[third], lambda: ups[1])]
    gate_x_pairs = [
        (normeds.at[first], lambda: gate_xs[0]),
        (normeds.at[second], lambda: gate_xs[1]),
    ]
    gate_y_pairs = [
        (normeds.at[first], lambda: gate_ys[0]),
        (normeds.at[third], lambda: gate_ys[1]),
    ]
    out_pairs = [(grad_low, lambda: merged[...])]
    query_pairs = [(inputs.at[d], lambda d=d: query_backs[d]) for d in range(4)]
    value_pairs = [(inputs.at[d], lambda d=d: value_backs[d]) for d in range(4)]

    def block_along_y(side, index):
        return 2 * side + index

    def block_along_x(side, index):
        return 2 * index + side

    def fill(target, pairs, block_of, side):
        for index in range(2):
            target[index] = outer(pairs, block_of(side, index)).astype(jnp.bfloat16)

    def add_outer(landed, pairs, block_of, side):
        for index in range(2):
            landed[index] = (
                landed[index].astype(jnp.float32) + outer(pairs, block_of(side, index))
            ).astype(jnp.bfloat16)

    def add(target, term):
        target[...] = (target[...].astype(jnp.float32) + term.astype(jnp.float32)).astype(
            jnp.bfloat16
        )

    def by_place(ref, blocks):
        return ref.reshape(blocks, 2, 2, width_each, ref.shape[-1])

    def start_near(slots, landed):
        return send(slots.at[:, :, 1 - near], landed, peers[0])

    def start_far(slots, landed, last, started):
        started.wait()
        for index in range(slots.shape[0]):
            for side in range(2):
                landed[index, side] = (
                    landed[index, side].astype(jnp.float32)
                    + slots[index, side, near].astype(jnp.float32)
                ).astype(jnp.bfloat16)
        return send(landed.at[:, 1 - far], last, peers[1])

    def add_far(landed, last, copy):
        copy.wait()
        for index in range(last.shape[0]):
            last[index] = (
                last[index].astype(jnp.float32) + landed[index, far].astype(jnp.float32)
            ).astype(jnp.bfloat16)

    ends = [ends_ref[index] for index in range(4)]
    scale = HD ** (-0.5) * LOG2E
    grad_heads[...] = jnp.zeros_like(grad_heads)
    key_sum[...] = jnp.zeros_like(key_sum)
    value_sum[...] = jnp.zeros_like(value_sum)
    for step, grad in enumerate((grad_0, grad_1, grad_2, grad_3)):
        here = rows_of(partner(place, step))
        grad_heads[0, here, :HD] = grad[:, :HD]
        grad_heads[1, here, :HD] = grad[:, HD:]
    wait_all(for_heads)

    def turned_back(value, cos_part, sin_part):
        swapped = jnp.concatenate([value[:, HD // 2 :], value[:, : HD // 2]], axis=1)
        return ((value * cos_part - swapped * sin_part) * HD ** (-0.5)).astype(jnp.bfloat16)

    def block_at(distance):
        one, two = distance % 2, distance // 2
        flipped = place + one * (1 - 2 * (place % 2))
        return flipped + two * (2 - 4 * (flipped // 2))

    def attend_block(distance):
        block = block_at(distance)

        def attend_tile(index, nothing):
            start = pl.multiple_of(block * rows + index * QUERY_TILE, QUERY_TILE)
            tile = pl.ds(start, QUERY_TILE)
            inner = pl.ds(pl.multiple_of(index * QUERY_TILE, QUERY_TILE), QUERY_TILE)
            queries = jnp.concatenate([heads[0, tile, :], heads[1, tile, :]], axis=0)
            grad_rows = jnp.concatenate([grad_heads[0, tile, :], grad_heads[1, tile, :]], axis=0)
            exact_rows = jnp.concatenate([exact[0, tile, :], exact[1, tile, :]], axis=0)
            delta = jnp.sum(
                jnp.transpose(grad_rows.astype(jnp.float32) * exact_rows), axis=0, keepdims=True
            )
            log_row = jnp.concatenate([lse[0:1, tile], lse[1:2, tile]], axis=1)
            row_ids = lax.broadcasted_iota(jnp.int32, (1, 2 * QUERY_TILE), 1) % QUERY_TILE + start
            doc_starts = doc_start(ends, row_ids)

            def key_step(key_index, summed):
                first_key = pl.multiple_of(key_index * KEY_TILE, KEY_TILE)
                key_rows = pl.ds(first_key, KEY_TILE)
                key_part, value_part = keys[key_rows, :], values[key_rows, :]
                scores = scale * times_transpose(key_part, queries)
                key_ids = lax.broadcasted_iota(jnp.int32, (KEY_TILE, 1), 0) + first_key
                probs = jnp.where(
                    (key_ids >= doc_starts) & (key_ids <= row_ids), jnp.exp2(scores - log_row), 0.0
                )
                grad_scores = (probs * (times_transpose(value_part, grad_rows) - delta)).astype(
                    jnp.bfloat16
                )
                value_sum[key_rows, :] += dot_plain(probs.astype(jnp.bfloat16), grad_rows)
                key_sum[key_rows, :] += dot_plain(grad_scores, queries)
                return summed + outer_sum(grad_scores, key_part)

            summed = lax.fori_loop(
                0, block + 1, key_step, jnp.zeros((2 * QUERY_TILE, PAD), jnp.float32)
            )
            table = cosine[tile, :HD], sine[tile, :HD]
            for head in range(2):
                mine = summed[head * QUERY_TILE : (head + 1) * QUERY_TILE, :HD]
                query_backs[distance, inner, head * HD : (head + 1) * HD] = turned_back(mine, *table)
            return nothing

        lax.fori_loop(0, rows // QUERY_TILE, attend_tile, 0)

    back_sends = copies.sends
    copies.sends += 6

    def back_copy(source, target, first, distance):
        index = back_sends + first + distance - 1
        return pltpu.make_async_remote_copy(
            src_ref=source.at[distance],
            dst_ref=target.at[place],
            send_sem=send_sem.at[index],
            recv_sem=recv_sem.at[index],
            device_id={"seq": block_at(distance)},
            device_id_type=pl.DeviceIdType.MESH,
        )

    def attend_and_send(step, nothing):
        attend_block(3 - step)
        back_copy(query_backs, query_sorted, 0, 3 - step).start()
        return nothing

    lax.fori_loop(0, 3, attend_and_send, 0)
    attend_block(0)

    def finish_keys(distance):
        here = rows_of(block_at(distance))
        value_backs[distance, :, :HD] = turned_back(
            key_sum[here, :HD], cosine[here, :HD], sine[here, :HD]
        )
        value_backs[distance, :, HD:] = value_sum[here, :HD].astype(jnp.bfloat16)

    def finish_and_send(step, nothing):
        finish_keys(3 - step)
        back_copy(value_backs, value_sorted, 3, 3 - step).start()
        return nothing

    lax.fori_loop(0, 3, finish_and_send, 0)
    finish_keys(0)
    gate_copies = [
        send(grad_gate.at[1 - along_x], gate_xs.at[1], over_x),
        send(grad_gate.at[3 - along_y], gate_ys.at[1], over_y),
    ]
    query_sorted[place] = query_backs[0]
    value_sorted[place] = value_backs[0]

    wait_all(for_head)
    for target, side in ((head_away, 1 - along_x), (head_stay, along_x)):
        for lanes, pairs in ((slice(0, 2 * HD), query_pairs), (slice(2 * HD, 4 * HD), value_pairs)):
            for index in range(2):
                target[index, :, lanes] = outer(pairs, block_along_x(side, index)).astype(
                    jnp.bfloat16
                )
    head_copy = send(head_away, head_1, over_x)
    wait_all(for_down)
    down_copy.wait()
    add_outer(down_1, down_pairs, block_along_y, 0)
    down_slots = by_place(down_1, 2)
    down_copies = start_near(down_slots, down_2)
    wait_all(for_up)
    wait_all(for_gates)
    up_copy.wait()
    add_outer(up_1, up_pairs, block_along_x, along_x)
    up_slots = by_place(up_1, 2)
    up_copies = start_near(up_slots, up_2)
    wait_all(gate_copies)
    fill(gate_x_away, gate_x_pairs, block_along_y, 1 - along_y)
    gate_x_copy = send(gate_x_away, gate_x_1, over_y)
    fill(gate_y_away, gate_y_pairs, block_along_x, 1 - along_x)
    gate_y_copy = send(gate_y_away, gate_y_1, over_x)
    wait_all(for_out)
    fill(out_away, out_pairs, block_along_y, 1 - along_y)
    out_copy = send(out_away, out_1, over_y)
    fill(out_stay, out_pairs, block_along_y, along_y)

    columns = [w.shape[1] for w in (w_query, w_key, w_value)]
    starts = [0, columns[0], columns[0] + columns[1]]
    weight_loads = [
        load(w.at[pl.ds(index * rows, rows)], inputs.at[index, :, pl.ds(start, size)])
        for w, start, size in zip((w_query, w_key, w_value), starts, columns, strict=True)
        for index in range(3)
    ]
    x = inputs.at[3]
    x_load = load(x_far, x)
    query, part = merged, grad_low
    for distance in (1, 2, 3):
        back_copy(query_backs, query_sorted, 0, distance).wait()
        back_copy(value_backs, value_sorted, 3, distance).wait()
    for head in range(4):
        query[:, 2 * head * HD : 2 * (head + 1) * HD] = query_sorted[head]
        key[:, head * HD : (head + 1) * HD] = value_sorted[head, :, :HD]
        value[:, head * HD : (head + 1) * HD] = value_sorted[head, :, HD:]
    wait_all(weight_loads)
    part_copies = []
    for third_index in range(3):
        total = None
        for ref, start, size in zip((query, key, value), starts, columns, strict=True):
            term = times_transpose(ref[...], inputs[third_index, :, start : start + size])
            total = term if total is None else total + term
        lanes = pl.ds(third_index * rows, rows)
        part[:, lanes] = total.astype(jnp.bfloat16)
        part_copies.append(send(part.at[:, lanes], other.at[:, lanes], across))

    gate_x_copy.wait()
    add_outer(gate_x_1, gate_x_pairs, block_along_y, along_y)
    gate_x_slots = by_place(gate_x_1, 2)
    gate_x_copies = start_near(gate_x_slots, gate_x_2)
    gate_y_copy.wait()
    add_outer(gate_y_1, gate_y_pairs, block_along_x, along_x)
    gate_y_slots = by_place(gate_y_1, 2)
    gate_y_copies = start_near(gate_y_slots, gate_y_2)
    head_copy.wait()
    for index in range(2):
        add(head_1.at[index], head_stay[index])
    head_copy = send(head_1.at[1 - along_y], head_2, over_y)

    x_load.wait()
    wait_all(part_copies)
    tiles = [pl.ds(block * (rows // 4), rows // 4) for block in range(4)]
    for block, tile in enumerate(tiles):
        load(grad_middle_far.at[tile], grad_middle).wait()
        tokens = x[tile, :].astype(jnp.float32)
        inverse = norm_scale(tokens)
        unit_rows = tokens * inverse
        grad_normed = part[tile, :].astype(jnp.float32) + other[tile, :].astype(jnp.float32)
        term = jnp.sum(grad_normed * unit_rows, axis=0, keepdims=True)
        gain_sum = term if block == 0 else gain_sum + term
        scaled = grad_normed * gain[...]
        x[tile, :] = (
            grad_middle[...]
            + inverse * (scaled - unit_rows * jnp.mean(scaled * unit_rows, axis=-1, keepdims=True))
        ).astype(jnp.bfloat16)
    input_copy = load(x, grad_input)
    gain_0[0:1, :] = gain_sum
    gain_0[1:2, :] = mlp_gain_sum[...]
    gain_copy = send(gain_0, gain_1, over_y)

    down_copy = start_far(down_slots, down_2, down_3, down_copies)
    up_copy = start_far(up_slots, up_2, up_3, up_copies)
    gain_copy.wait()
    gain_1[...] += gain_0[...]
    gain_copy = send(gain_1, gain_2, over_x)
    out_copy.wait()
    for index in range(2):
        add(out_1.at[index], out_stay[index])
    out_copy = send(out_1.at[1 - along_x], out_2, over_x)
    head_copy.wait()
    add(head_2, head_1[along_y])
    head_slots = head_2.reshape(4, width_each, head_2.shape[-1])
    head_copies = [
        send(head_slots.at[partner(place, d)], head_3.at[d - 1], peers[d - 1]) for d in (1, 2, 3)
    ]
    gate_x_copy = start_far(gate_x_slots, gate_x_2, gate_x_3, gate_x_copies)
    gate_y_copy = start_far(gate_y_slots, gate_y_2, gate_y_3, gate_y_copies)
    gain_copy.wait()
    gain_2[...] += gain_1[...]
    gain_copies = [send(gain_2, gain_3.at[d - 1], peers[d - 1]) for d in (1, 2, 3)]
    out_copy.wait()
    add(out_2, out_1[along_x])
    out_slots = by_place(out_2, 1)
    out_copies = start_near(out_slots, out_3)
    add_far(down_2, down_3, down_copy)
    down_copy = send(down_3.at[1 - along_x], down_4, over_x)
    add_far(up_2, up_3, up_copy)
    up_copy = send(up_3.at[1 - along_y], up_4, over_y)
    out_copy = start_far(out_slots, out_3, out_4, out_copies)
    wait_all(gain_copies)
    gains[...] = (gain_2[...] + gain_3[0]) + (gain_3[1] + gain_3[2])

    head_rows[place] = head_slots[place]
    for d, copy in enumerate(head_copies):
        copy.wait()
        head_rows[partner(place, d + 1)] = head_3[d]
    for head in range(4):
        mine = head_rows[head].astype(jnp.float32)
        grad_query[:, 2 * head * HD : 2 * (head + 1) * HD] = mine[:, : 2 * HD]
        grad_key[:, head * HD : (head + 1) * HD] = mine[:, 2 * HD : 3 * HD]
        grad_value[:, head * HD : (head + 1) * HD] = mine[:, 3 * HD :]

    def both_sides(ref, landed, here, target):
        target[here] = ref[here].astype(jnp.float32)
        target[1 - here] = landed[...].astype(jnp.float32)

    add_far(gate_x_2, gate_x_3, gate_x_copy)
    gate_x_copy = send(gate_x_3.at[1 - along_x], gate_x_4, over_x)
    add_far(gate_y_2, gate_y_3, gate_y_copy)
    gate_y_copy = send(gate_y_3.at[1 - along_y], gate_y_4, over_y)
    out_copy.wait()
    grad_out[...] = out_4[0].astype(jnp.float32) + out_3[0, far].astype(jnp.float32)
    down_copy.wait()
    both_sides(down_3, down_4, along_x, grad_down)
    up_copy.wait()
    both_sides(up_3, up_4, along_y, grad_up_rows)
    gate_x_copy.wait()
    both_sides(gate_x_3, gate_x_4, along_x, grad_gate_x)
    gate_y_copy.wait()
    both_sides(gate_y_3, gate_y_4, along_y, grad_gate_y)
    input_copy.wait()


def backward(ends, lse, gain, mlp_gain_sum, grads, far):
    rows = grads[0].shape[0]
    operands = list(far.values())
    width, query = far["w_query"].shape
    key, merged_width = far["w_key"].shape[1], far["merged"].shape[1]
    each, block_rows, total = width // 16, width // 4, 4 * rows
    half, quarter = far["hidden"].shape[2], far["grad_gate"].shape[2]
    f32 = jnp.float32
    outs = (
        shape_of(2, each, half, dtype=f32),
        shape_of(2, each, quarter, dtype=f32),
        shape_of(2, each, quarter, dtype=f32),
        shape_of(2, each, half, dtype=f32),
        shape_of(each, merged_width, dtype=f32),
        shape_of(each, query, dtype=f32),
        shape_of(each, key, dtype=f32),
        shape_of(each, key, dtype=f32),
        shape_of(2, width, dtype=f32),
        shape_of(rows, width),
    )

    def low(*dims):
        return pltpu.VMEM(dims, jnp.bfloat16)

    head = 4 * HD
    sizes = (half, half, quarter, quarter)
    scratch = [
        low(2, total, PAD),
        low(total, PAD),
        low(total, PAD),
        pltpu.VMEM((2, total, PAD), f32),
        pltpu.VMEM((total, PAD), f32),
        pltpu.VMEM((total, PAD), f32),
        low(2, total, PAD),
        pltpu.VMEM((total, PAD), f32),
        pltpu.VMEM((total, PAD), f32),
        *(low(4, rows, head // 2) for _ in range(4)),
        low(rows, merged_width),
        low(rows, width),
        low(2 * rows, width // 2),
        low(3 * rows, width),
        low(2, rows, half),
        low(2, rows, half),
        low(2, rows, quarter),
        low(2, rows, quarter),
        low(4, rows, width),
        pltpu.VMEM((rows // 4, width), f32),
        low(rows, key),
        low(rows, key),
        low(rows, width),
        low(2, block_rows, merged_width),
        low(2, block_rows, merged_width),
        low(2, block_rows, quarter),
        low(2, block_rows, quarter),
        low(2, block_rows, head),
        low(2, block_rows, head),
        *(low(2, block_rows, size) for size in (*sizes, merged_width, head)),
        *(low(2, 2, each, size) for size in sizes),
        low(block_rows, merged_width),
        low(block_rows, head),
        *(low(2, each, size) for size in sizes),
        low(1, 2, each, merged_width),
        low(3, each, head),
        *(low(each, size) for size in sizes),
        low(1, each, merged_width),
        low(4, each, head),
        *(pltpu.VMEM((2, width), f32) for _ in range(3)),
        pltpu.VMEM((3, 2, width), f32),
        pltpu.SemaphoreType.DMA((31,)),
        pltpu.SemaphoreType.DMA((41,)),
        pltpu.SemaphoreType.DMA((41,)),
    ]
    return pl.pallas_call(
        backward_kernel,
        out_shape=outs,
        in_specs=[pl.BlockSpec(memory_space=pltpu.SMEM)] + [IN_VMEM] * 7 + [IN_ANY] * len(operands),
        out_specs=(IN_VMEM,) * 9 + (IN_ANY,),
        scratch_shapes=scratch,
        compiler_params=pltpu.CompilerParams(
            collective_id=1, has_side_effects=True, vmem_limit_bytes=63 * MEBI
        ),
        cost_estimate=pl.CostEstimate(
            flops=8 * rows * width * 4 * half, bytes_accessed=64 * MEBI, transcendentals=0
        ),
        name="backward",
    )(ends, lse, gain, mlp_gain_sum, *grads, *operands)


def swap(array, axis, bit):
    return lax.ppermute(array, axis, [(i, i ^ bit) for i in range(lax.axis_size(axis))])


def local_paired(
    hidden_in,
    lengths,
    attn_gain,
    w_query,
    w_key,
    w_value,
    w_out,
    mlp_gain,
    w_gate,
    w_up,
    w_down,
    out_grad,
):
    rows, width = hidden_in.shape[1], hidden_in.shape[2]
    dp_index, place, core = (lax.axis_index(name) for name in ("dp", "seq", "tensor"))
    along_x, along_y = dp_index % 2, dp_index // 2
    total_rows = 4 * rows
    x, cotangent = hidden_in[0], out_grad[0]
    gain_one, gain_two = attn_gain[None], mlp_gain[None]
    info = jnp.concatenate(
        [jnp.cumsum(lengths[0]), jnp.stack([place, along_x, along_y, core])]
    ).astype(jnp.int32)

    def over_x(array):
        return swap(array, "dp", 1)

    def over_y(array):
        return swap(array, "dp", 2)

    _, _, offsets, _ = doc_layout(lengths[0], 0, total_rows)
    cosine, sine = rope_tables(offsets)
    cosine, sine = cosine[:, 0], sine[:, 0]
    spare = PAD - HD
    cosine = jnp.pad(jnp.concatenate([cosine, cosine], axis=1), ((0, 0), (0, spare)))
    sine = jnp.pad(jnp.concatenate([-sine, sine], axis=1), ((0, 0), (0, spare)))

    (
        lse,
        mlp_gain_part,
        heads,
        keys,
        values,
        exact,
        cotangent_x,
        attn_input,
        input_shards,
        mlp_input,
        mlp_x,
        mlp_y,
        hidden,
        grad_gate,
        grad_up,
        hidden_x,
        up_y,
        attn_heads,
        grad_low,
        grad_middle,
        down_away,
        up_away,
        *grad_dealt,
        result,
    ) = forward(
        info,
        x,
        (gain_one, gain_two),
        cotangent,
        (cosine, sine),
        (w_query, w_key, w_value, w_out, w_gate, w_up, w_down),
    )
    (
        grad_down,
        grad_gate_x,
        grad_gate_y,
        grad_up_rows,
        grad_out,
        grad_w_query,
        grad_w_key,
        grad_w_value,
        gains,
        grad_inputs,
    ) = backward(
        info,
        lse,
        gain_one,
        mlp_gain_part,
        grad_dealt,
        dict(
            heads=heads,
            keys=keys,
            values=values,
            exact=exact,
            cosine=cosine,
            sine=sine,
            merged=attn_heads,
            grad_low=grad_low,
            cotangent=cotangent,
            cotangent_x=cotangent_x,
            normed=mlp_input,
            normed_x=mlp_x,
            normed_y=mlp_y,
            hidden=hidden,
            hidden_x=hidden_x,
            grad_up=grad_up,
            up_y=up_y,
            grad_gate=grad_gate,
            down_away=down_away,
            up_away=up_away,
            normed_one=attn_input,
            shards=input_shards,
            w_query=w_query,
            w_key=w_key,
            w_value=w_value,
            x=x,
            grad_middle=grad_middle,
        ),
    )
    own_gains = lax.dynamic_slice_in_dim(
        gains, (4 * dp_index + place) * (width // 16), width // 16, 1
    )
    grad_w_gate = jnp.concatenate(
        [grad_gate_x[0], grad_gate_x[1], grad_gate_y[0], grad_gate_y[1]], axis=1
    )
    grad_w_up = jnp.concatenate([grad_up_rows[0], grad_up_rows[1]], axis=1)
    grad_w_down = jnp.swapaxes(grad_down, 1, 2).reshape(-1, width // 16)
    return (
        result[None],
        grad_inputs[None],
        own_gains[0],
        grad_w_query,
        grad_w_key,
        grad_w_value,
        grad_out.T,
        own_gains[1],
        grad_w_gate,
        grad_w_up,
        grad_w_down,
    )


def solution(mesh):
    in_specs = (
        P("dp", "seq", None),
        P("dp", None),
        P(),
        P(None, "tensor"),
        P(None, "tensor"),
        P(None, "tensor"),
        P("tensor", None),
        P(),
        P(None, "tensor"),
        P(None, "tensor"),
        P("tensor", None),
        P("dp", "seq", None),
    )
    out_specs = (
        P("dp", "seq", None),
        P("dp", "seq", None),
        P(("dp", "seq")),
        P(("dp", "seq"), "tensor"),
        P(("dp", "seq"), "tensor"),
        P(("dp", "seq"), "tensor"),
        P("tensor", ("dp", "seq")),
        P(("dp", "seq")),
        P(("dp", "seq"), "tensor"),
        P(("dp", "seq"), "tensor"),
        P("tensor", ("dp", "seq")),
    )
    body = local_paired if tuple(mesh.shape[name] for name in ("dp", "seq", "tensor")) == (4, 4, 2) else local
    return jax.shard_map(body, mesh=mesh, in_specs=in_specs, out_specs=out_specs, check_vma=False)
```

```python
import jax
import jax.numpy as jnp
from jax import lax
from jax.experimental import pallas as pl
from jax.experimental.pallas import tpu as pltpu
from jax.sharding import PartitionSpec as P

HQ = 16
KV = 8
HD = 96


epsilon = 1e-05
rope_theta = 100000.0
masked_score = -1e30


def doc_layout(length_row, first_row, row_count):
    positions = first_row + jnp.arange(row_count, dtype=jnp.int32)
    doc_ends = jnp.cumsum(length_row)
    passed = (positions[:, None] >= doc_ends[None, :]).astype(jnp.int32)
    segment = jnp.sum(passed, axis=1)
    doc_start = jnp.sum(passed * length_row[None, :], axis=1)
    return (positions, segment, positions - doc_start, segment < length_row.shape[0])


def rope_tables(offsets):
    half_size = HD // 2
    inverse = rope_theta ** (-2.0 * jnp.arange(half_size, dtype=jnp.float32) / HD)
    angles = offsets.astype(jnp.float32)[:, None] * inverse[None, :]
    return (jnp.cos(angles)[:, None, :], jnp.sin(angles)[:, None, :])


def rotate(values, cosine, sine_table):
    half_size = values.shape[-1] // 2
    first_half = values[..., :half_size]
    second_half = values[..., half_size:]
    return jnp.concatenate(
        [
            first_half * cosine - second_half * sine_table,
            second_half * cosine + first_half * sine_table,
        ],
        axis=-1,
    )


def rotate_back(gradient, cosine, sine_table):
    half_size = gradient.shape[-1] // 2
    first_half = gradient[..., :half_size]
    second_half = gradient[..., half_size:]
    return jnp.concatenate(
        [
            first_half * cosine + second_half * sine_table,
            second_half * cosine - first_half * sine_table,
        ],
        axis=-1,
    )


def outer_sum(left, right):
    return lax.dot_general(
        left, right, (((0,), (0,)), ((), ())), preferred_element_type=jnp.float32
    )


def times_transpose(left, right):
    return lax.dot_general(
        left, right, (((1,), (1,)), ((), ())), preferred_element_type=jnp.float32
    )


def allowed_pairs(query_rows, query_seg, key_rows, key_seg, key_valid):
    same_doc = (
        (query_seg[:, None] == key_seg[None, :])
        & (key_rows[None, :] <= query_rows[:, None])
        & key_valid[None, :]
    )
    return same_doc | (key_rows[None, :] == query_rows[:, None])


def score_block(queries, key_part, allowed_mask):
    raw_scores = jnp.einsum("qkgd,jkd->kgqj", queries, key_part, preferred_element_type=jnp.float32)
    return jnp.where(allowed_mask[None, None], raw_scores * HD ** (-0.5), masked_score)


def backward_terms(queries, grad_heads, log_total, delta, key_part, value_part, allowed_mask):
    probs = jnp.exp(score_block(queries, key_part, allowed_mask) - log_total[..., None])
    grad_probs = jnp.einsum(
        "qkgd,jkd->kgqj", grad_heads, value_part, preferred_element_type=jnp.float32
    )
    grad_scores = (probs * (grad_probs - delta[..., None])).astype(jnp.bfloat16)
    return (probs.astype(jnp.bfloat16), grad_scores)


def block_loader(keys_all, values_all, query_info, key_info, block_rows):
    query_rows, query_seg = query_info

    def load_block(block_index):
        first_key = block_index * block_rows
        key_part = lax.dynamic_slice_in_dim(keys_all, first_key, block_rows, 0)
        value_part = lax.dynamic_slice_in_dim(values_all, first_key, block_rows, 0)
        key_rows, key_seg, key_valid = tuple(
            (lax.dynamic_slice_in_dim(member, first_key, block_rows, 0) for member in key_info)
        )
        return (
            key_part,
            value_part,
            allowed_pairs(query_rows, query_seg, key_rows, key_seg, key_valid),
        )

    return load_block


def attend_forward(queries, keys_all, values_all, query_info, key_info, block_rows):
    last_row = query_info[0][-1]
    block_count = keys_all.shape[0] // block_rows
    stat_shape = (queries.shape[1], queries.shape[2], queries.shape[0])
    load_block = block_loader(keys_all, values_all, query_info, key_info, block_rows)

    def stats_step(block_index, running):

        def stats_compute(state_in):
            row_max, row_sum = state_in
            key_part, value_part, allowed_mask = load_block(block_index)
            scores = score_block(queries, key_part, allowed_mask)
            new_max = jnp.maximum(row_max, jnp.max(scores, axis=-1))
            new_sum = row_sum * jnp.exp(row_max - new_max) + jnp.sum(
                jnp.exp(scores - new_max[..., None]), axis=-1
            )
            return (new_max, new_sum)

        return lax.cond(
            block_index * block_rows <= last_row, stats_compute, lambda state_in: state_in, running
        )

    start_stats = (
        jnp.full(stat_shape, masked_score, jnp.float32),
        jnp.zeros(stat_shape, jnp.float32),
    )
    row_max, row_sum = lax.fori_loop(0, block_count, stats_step, start_stats)
    log_total = row_max + jnp.log(row_sum)

    def output_step(block_index, running):

        def output_compute(state_in):
            kept_sum, rest_sum = state_in
            key_part, value_part, allowed_mask = load_block(block_index)
            probs = jnp.exp(score_block(queries, key_part, allowed_mask) - log_total[..., None])
            probs_low = probs.astype(jnp.bfloat16)
            rest_low = (probs - probs_low.astype(jnp.float32)).astype(jnp.bfloat16)
            kept_sum = kept_sum + jnp.einsum(
                "kgqj,jkd->qkgd", probs_low, value_part, preferred_element_type=jnp.float32
            )
            rest_sum = rest_sum + jnp.einsum(
                "kgqj,jkd->qkgd", rest_low, value_part, preferred_element_type=jnp.float32
            )
            return (kept_sum, rest_sum)

        return lax.cond(
            block_index * block_rows <= last_row, output_compute, lambda state_in: state_in, running
        )

    zero_out = jnp.zeros(queries.shape, jnp.float32)
    kept_sum, rest_sum = lax.fori_loop(0, block_count, output_step, (zero_out, zero_out))
    return (log_total, kept_sum, kept_sum + rest_sum)


def attend_backward(
    queries, grad_heads, log_total, delta, keys_all, values_all, query_info, key_info, block_rows
):
    last_row = query_info[0][-1]
    block_count = keys_all.shape[0] // block_rows
    key_width = keys_all.shape[1] * keys_all.shape[2]
    load_block = block_loader(keys_all, values_all, query_info, key_info, block_rows)

    def grad_step(running, block_index):

        def grad_compute(state_in):
            key_part, value_part, allowed_mask = load_block(block_index)
            probs_low, grad_scores = backward_terms(
                queries, grad_heads, log_total, delta, key_part, value_part, allowed_mask
            )
            grad_query = state_in + jnp.einsum(
                "kgqj,jkd->qkgd", grad_scores, key_part, preferred_element_type=jnp.float32
            )
            key_terms = ()
            grad_key = jnp.einsum(
                "kgqj,qkgd->jkd", grad_scores, queries, preferred_element_type=jnp.float32
            )
            grad_value = jnp.einsum(
                "kgqj,qkgd->jkd", probs_low, grad_heads, preferred_element_type=jnp.float32
            )
            key_terms = (
                grad_key.reshape(block_rows, key_width),
                grad_value.reshape(block_rows, key_width),
            )
            return (grad_query, key_terms)

        def skipped(state_in):
            key_terms = ()
            zero_block = jnp.zeros((block_rows, key_width), jnp.float32)
            key_terms = (zero_block, zero_block)
            return (state_in, key_terms)

        return lax.cond(block_index * block_rows <= last_row, grad_compute, skipped, running)

    grad_query, key_terms = lax.scan(
        grad_step, jnp.zeros(queries.shape, jnp.float32), jnp.arange(block_count, dtype=jnp.int32)
    )
    key_terms = tuple((member.reshape(block_count * block_rows, key_width) for member in key_terms))
    return (grad_query, key_terms)


def local(
    hidden_in,
    lengths,
    attn_gain,
    w_query,
    w_key,
    w_value,
    w_out,
    mlp_gain,
    w_gate,
    w_up,
    w_down,
    out_grad,
):
    seq_count = hidden_in.shape[0]
    tok_rows = hidden_in.shape[1]
    width = hidden_in.shape[2]
    row_total = seq_count * tok_rows
    seq_total = tok_rows * lax.axis_size("seq")
    first_row = lax.axis_index("seq") * tok_rows
    half_rows = row_total // lax.axis_size("tensor")
    half_start = lax.axis_index("tensor") * half_rows
    block_rows = min(512, seq_total)
    kv_local = w_key.shape[1] // HD
    group_size = HQ // KV
    heads_local = kv_local * group_size

    def own_half(array_in):
        return lax.dynamic_slice_in_dim(array_in, half_start, half_rows, 0)

    inputs = hidden_in.reshape(row_total, width).astype(jnp.float32)
    query_rows, query_seg, query_offsets, query_valid = jax.vmap(
        lambda length_row: doc_layout(length_row, first_row, tok_rows)
    )(lengths)
    key_layout = jax.vmap(lambda length_row: doc_layout(length_row, 0, seq_total))(lengths)
    cosine, sine_table = rope_tables(query_offsets.reshape(row_total))
    valid_rows = query_valid.reshape(row_total).astype(jnp.float32)[:, None]
    inverse_one = lax.rsqrt(jnp.mean(inputs * inputs, axis=-1, keepdims=True) + epsilon)
    normed_one = inputs * inverse_one
    attn_input = (normed_one * attn_gain).astype(jnp.bfloat16)
    query_raw = jnp.dot(attn_input, w_query, preferred_element_type=jnp.float32).reshape(
        row_total, heads_local, HD
    )
    key_raw = jnp.dot(attn_input, w_key, preferred_element_type=jnp.float32).reshape(
        row_total, kv_local, HD
    )
    values_own = (
        jnp.dot(attn_input, w_value, preferred_element_type=jnp.float32)
        .astype(jnp.bfloat16)
        .reshape(seq_count, tok_rows, kv_local * HD)
    )
    queries = (
        rotate(query_raw, cosine, sine_table)
        .astype(jnp.bfloat16)
        .reshape(seq_count, tok_rows, kv_local, group_size, HD)
    )
    keys_own = (
        rotate(key_raw, cosine, sine_table)
        .astype(jnp.bfloat16)
        .reshape(seq_count, tok_rows, kv_local * HD)
    )
    keys_all, values_all = (
        lax.all_gather(keys_own, "seq", axis=1, tiled=True),
        lax.all_gather(values_own, "seq", axis=1, tiled=True),
    )
    key_shape = (seq_count, seq_total, kv_local, HD)

    def forward_one(items):
        query_s, key_s, value_s, rows_s, seg_s, key_rows, key_seg, key_valid = items
        return attend_forward(
            query_s, key_s, value_s, (rows_s, seg_s), (key_rows, key_seg, key_valid), block_rows
        )

    log_total, kept_sum, exact_sum = lax.map(
        forward_one,
        (
            queries,
            keys_all.reshape(key_shape),
            values_all.reshape(key_shape),
            query_rows,
            query_seg,
            key_layout[0],
            key_layout[1],
            key_layout[3],
        ),
    )
    attn_heads = (kept_sum.reshape(row_total, heads_local * HD) * valid_rows).astype(jnp.bfloat16)
    attn_part = jnp.dot(attn_heads, w_out, preferred_element_type=jnp.float32)
    middle = own_half(inputs) + lax.psum_scatter(
        attn_part, "tensor", scatter_dimension=0, tiled=True
    )
    inverse_two = lax.rsqrt(jnp.mean(middle * middle, axis=-1, keepdims=True) + epsilon)
    normed_two = middle * inverse_two
    mlp_half = (normed_two * mlp_gain).astype(jnp.bfloat16)
    mlp_input = lax.all_gather(mlp_half, "tensor", axis=0, tiled=True)
    gate = jnp.dot(mlp_input, w_gate, preferred_element_type=jnp.float32)
    upward = jnp.dot(mlp_input, w_up, preferred_element_type=jnp.float32)
    hidden = (jax.nn.silu(gate) * upward).astype(jnp.bfloat16)
    mlp_part = jnp.dot(hidden, w_down, preferred_element_type=jnp.float32)
    result = middle + lax.psum_scatter(
        mlp_part.astype(jnp.bfloat16), "tensor", scatter_dimension=0, tiled=True
    ).astype(jnp.float32)
    cotangent = out_grad.reshape(row_total, width)
    grad_hidden = times_transpose(cotangent, w_down)
    sigmoid_gate = jax.nn.sigmoid(gate)
    grad_gate = (grad_hidden * upward * sigmoid_gate * (1.0 + gate * (1.0 - sigmoid_gate))).astype(
        jnp.bfloat16
    )
    grad_upward = (grad_hidden * gate * sigmoid_gate).astype(jnp.bfloat16)
    grad_w_down = outer_sum(hidden, cotangent)
    grad_w_gate = outer_sum(mlp_input, grad_gate)
    grad_w_up = outer_sum(mlp_input, grad_upward)
    grad_mlp_in = lax.psum_scatter(
        times_transpose(grad_gate, w_gate) + times_transpose(grad_upward, w_up),
        "tensor",
        scatter_dimension=0,
        tiled=True,
    )
    mlp_gain_part = jnp.sum(grad_mlp_in * normed_two, axis=0)
    scaled_two = grad_mlp_in * mlp_gain
    grad_middle = own_half(cotangent).astype(jnp.float32) + inverse_two * (
        scaled_two - normed_two * jnp.mean(scaled_two * normed_two, axis=-1, keepdims=True)
    )
    grad_middle_low = lax.all_gather(grad_middle.astype(jnp.bfloat16), "tensor", axis=0, tiled=True)
    grad_w_out = outer_sum(attn_heads, grad_middle_low)
    grad_heads = (
        times_transpose(grad_middle_low, w_out).astype(jnp.bfloat16)
        * valid_rows.astype(jnp.bfloat16)
    ).reshape(seq_count, tok_rows, kv_local, group_size, HD)
    delta = jnp.einsum(
        "sqkgd,sqkgd->skgq", grad_heads, exact_sum, preferred_element_type=jnp.float32
    )
    keys_back, values_back = (
        lax.all_gather(keys_own, "seq", axis=1, tiled=True),
        lax.all_gather(values_own, "seq", axis=1, tiled=True),
    )
    keys_back = keys_back.reshape(key_shape)
    values_back = values_back.reshape(key_shape)

    def backward_one():

        def run(items):
            (
                query_s,
                grad_s,
                log_s,
                delta_s,
                key_s,
                value_s,
                rows_s,
                seg_s,
                key_rows,
                key_seg,
                key_valid,
            ) = items
            return attend_backward(
                query_s,
                grad_s,
                log_s,
                delta_s,
                key_s,
                value_s,
                (rows_s, seg_s),
                (key_rows, key_seg, key_valid),
                block_rows,
            )

        return run

    backward_items = (
        queries,
        grad_heads,
        log_total,
        delta,
        keys_back,
        values_back,
        query_rows,
        query_seg,
        key_layout[0],
        key_layout[1],
        key_layout[3],
    )
    grad_query, key_terms = lax.map(backward_one(), backward_items)
    grad_key_sum, grad_value_sum = (
        lax.psum_scatter(
            key_terms[0].astype(jnp.bfloat16), "seq", scatter_dimension=1, tiled=True
        ).astype(jnp.float32),
        lax.psum_scatter(
            key_terms[1].astype(jnp.bfloat16), "seq", scatter_dimension=1, tiled=True
        ).astype(jnp.float32),
    )
    grad_key_rot = grad_key_sum.reshape(row_total, kv_local, HD) * HD ** (-0.5)
    grad_key_low = (
        rotate_back(grad_key_rot, cosine, sine_table)
        .astype(jnp.bfloat16)
        .reshape(row_total, kv_local * HD)
    )
    grad_value_low = grad_value_sum.reshape(row_total, kv_local * HD).astype(jnp.bfloat16)
    grad_query_rot = (grad_query * HD ** (-0.5)).reshape(row_total, heads_local, HD)
    grad_query_low = (
        rotate_back(grad_query_rot, cosine, sine_table)
        .astype(jnp.bfloat16)
        .reshape(row_total, heads_local * HD)
    )
    grad_w_query = outer_sum(attn_input, grad_query_low)
    grad_w_key = outer_sum(attn_input, grad_key_low)
    grad_w_value = outer_sum(attn_input, grad_value_low)
    attn_back_part = (
        times_transpose(grad_query_low, w_query)
        + times_transpose(grad_key_low, w_key)
        + times_transpose(grad_value_low, w_value)
    )
    grad_attn_in = lax.psum_scatter(
        attn_back_part.astype(jnp.bfloat16), "tensor", scatter_dimension=0, tiled=True
    ).astype(jnp.float32)
    normed_half = own_half(normed_one)
    attn_gain_part = jnp.sum(grad_attn_in * normed_half, axis=0)
    scaled_one = grad_attn_in * attn_gain
    grad_inputs = grad_middle + own_half(inverse_one) * (
        scaled_one - normed_half * jnp.mean(scaled_one * normed_half, axis=-1, keepdims=True)
    )
    grad_attn_gain, grad_mlp_gain = lax.psum((attn_gain_part, mlp_gain_part), "tensor")
    reduced = tuple(
        (
            lax.psum_scatter(grad_attn_gain, ("dp", "seq"), scatter_dimension=0, tiled=True),
            lax.psum_scatter(grad_w_query, ("dp", "seq"), scatter_dimension=0, tiled=True),
            lax.psum_scatter(grad_w_key, ("dp", "seq"), scatter_dimension=0, tiled=True),
            lax.psum_scatter(grad_w_value, ("dp", "seq"), scatter_dimension=0, tiled=True),
            lax.psum_scatter(grad_w_out, ("dp", "seq"), scatter_dimension=1, tiled=True),
            lax.psum_scatter(grad_mlp_gain, ("dp", "seq"), scatter_dimension=0, tiled=True),
            lax.psum_scatter(grad_w_gate, ("dp", "seq"), scatter_dimension=0, tiled=True),
            lax.psum_scatter(grad_w_up, ("dp", "seq"), scatter_dimension=0, tiled=True),
            lax.psum_scatter(grad_w_down, ("dp", "seq"), scatter_dimension=1, tiled=True),
        )
    )
    result_all, grad_all = (
        lax.all_gather(result.astype(jnp.bfloat16), "tensor", axis=0, tiled=True),
        lax.all_gather(grad_inputs.astype(jnp.bfloat16), "tensor", axis=0, tiled=True),
    )
    out_shape = (seq_count, tok_rows, width)
    return (
        result_all.reshape(out_shape),
        grad_all.reshape(out_shape),
        reduced[0],
        reduced[1],
        reduced[2],
        reduced[3],
        reduced[4],
        reduced[5],
        reduced[6],
        reduced[7],
        reduced[8],
    )


LOG2E = 1.4426950408889634
QUERY_TILE = 256
KEY_TILE = 512
PAD = 128
ROW_TILE = 256
MEBI = 1024 * 1024
VMEM_LIMIT = 56 * MEBI
IN_VMEM = pl.BlockSpec(memory_space=pltpu.VMEM)
IN_ANY = pl.BlockSpec(memory_space=pl.ANY)


def doc_start(ends, rows):
    start = jnp.zeros_like(rows)
    for end in ends:
        start = jnp.where(rows >= end, end, start)
    return jnp.where(rows >= ends[-1], rows, start)


def dot_plain(left, right):
    return jnp.dot(left, right, preferred_element_type=jnp.float32)


def shape_of(*dims, dtype=jnp.bfloat16):
    return jax.ShapeDtypeStruct(dims, dtype)


def norm_scale(values):
    return lax.rsqrt(jnp.mean(values * values, axis=-1, keepdims=True) + epsilon)


def partner(position, step):
    if step == 0:
        return position
    if step == 1:
        return position + 1 - 2 * (position % 2)
    if step == 2:
        return position + 2 - 4 * (position // 2)
    return 3 - position


def greet(places):
    barrier = pltpu.get_barrier_semaphore()
    for device in places:
        pl.semaphore_signal(barrier, inc=1, device_id=device, device_id_type=pl.DeviceIdType.MESH)
    pl.semaphore_wait(barrier, len(places))


class Load:
    def __init__(self, source, target, sems, free):
        self.index, self.free = free.pop(0), free
        self.copy = pltpu.make_async_copy(source, target, sems.at[self.index])
        self.copy.start()

    def wait(self):
        self.copy.wait()
        self.free.append(self.index)


class Copies:
    def __init__(self, load_sem, send_sem, recv_sem):
        self.sems = (load_sem, send_sem, recv_sem)
        self.free, self.sends = list(range(load_sem.shape[0])), 0

    def load(self, source, target):
        return Load(source, target, self.sems[0], self.free)

    def send(self, source, target, device):
        copy = pltpu.make_async_remote_copy(
            src_ref=source,
            dst_ref=target,
            send_sem=self.sems[1].at[self.sends],
            recv_sem=self.sems[2].at[self.sends],
            device_id=device,
            device_id_type=pl.DeviceIdType.MESH,
        )
        copy.start()
        self.sends += 1
        return copy


def wait_all(copies):
    for copy in copies:
        copy.wait()


def forward_kernel(
    ends_ref,
    x_far,
    gain_one,
    gain_two,
    cotangent_far,
    cosine_far,
    sine_far,
    w_query,
    w_key,
    w_value,
    w_out_far,
    w_gate_far,
    w_up_far,
    w_down_far,
    lse,
    gain_sum,
    heads_out,
    keys_out,
    values_out,
    exact_out,
    cotangent_x,
    normed_one_out,
    shards,
    normed_out,
    normed_x,
    normed_y,
    hidden_out,
    grad_gate_out,
    grad_up_out,
    hidden_x,
    up_y,
    merged_out,
    grad_low_out,
    grad_middle_out,
    down_away,
    up_away,
    back_0,
    back_1,
    back_2,
    back_3,
    result,
    w_out,
    w_gate,
    w_up,
    w_down,
    x,
    cotangent,
    cosine,
    sine,
    normed_one,
    packed,
    packed_in,
    heads,
    keys,
    values,
    exact,
    low,
    low_in,
    merged,
    part,
    other,
    normed,
    hidden,
    grad_gate,
    grad_up,
    grad_part,
    grad_other,
    grad_middle,
    free_sem,
    load_sem,
    send_sem,
    recv_sem,
):
    dp_index, place, core = (lax.axis_index(name) for name in ("dp", "seq", "tensor"))
    along_x, along_y = dp_index % 2, dp_index // 2
    rows, width = x.shape
    units = w_up.shape[1]
    half_rows, quarter_rows = rows // 2, rows // 4
    half = pl.ds(pl.multiple_of(core * half_rows, half_rows), half_rows)
    first_quarter = pl.ds(pl.multiple_of(core * half_rows, quarter_rows), quarter_rows)
    second_quarter = pl.ds(
        pl.multiple_of(core * half_rows + quarter_rows, quarter_rows), quarter_rows
    )
    peers = [{"seq": partner(place, d)} for d in (1, 2, 3)]
    over_x, over_y = {"dp": partner(dp_index, 1)}, {"dp": partner(dp_index, 2)}
    across = {"tensor": 1 - core}
    tiles = [pl.ds(block * ROW_TILE, ROW_TILE) for block in range(rows // ROW_TILE)]
    copies = Copies(load_sem, send_sem, recv_sem)
    send, load = copies.send, copies.load
    late = []

    columns = [w.shape[1] for w in (w_query, w_key, w_value)]
    starts = [0, columns[0], columns[0] + columns[1]]
    weight_parts = [
        w_gate.at[:, pl.ds(start, size)] for start, size in zip(starts, columns, strict=True)
    ]
    own_rows = pl.ds(pl.multiple_of(place * rows, rows), rows)
    x_load = load(x_far, x)
    table_loads = [load(cosine_far.at[own_rows], cosine), load(sine_far.at[own_rows], sine)]
    head_loads = [
        load(w, target)
        for w, target in zip((w_value, w_key, w_query), reversed(weight_parts), strict=True)
    ]
    greet([*peers, over_x, over_y, across])
    beside_copy = send(cotangent_far.at[half], cotangent_x.at[half], over_x)
    other_loads = [load(w_out_far, w_out), load(w_up_far, w_up), load(w_down_far, w_down)]
    cotangent_load = load(cotangent_far, cotangent)

    heads[...] = jnp.zeros_like(heads)
    keys[...] = jnp.zeros_like(keys)
    values[...] = jnp.zeros_like(values)
    x_load.wait()
    packed_copies = []
    for block, tile in enumerate(tiles):
        inputs = x[tile, :].astype(jnp.float32)
        rows_low = (inputs * norm_scale(inputs) * gain_one[...]).astype(jnp.bfloat16)
        normed_one[tile, :] = rows_low
        if block == 0:
            wait_all(head_loads)
            wait_all(table_loads)
        cos_part, sin_part = cosine[tile, :HD], sine[tile, :HD]

        def turned(value, cos_part=cos_part, sin_part=sin_part):
            swapped = jnp.concatenate([value[:, HD // 2 :], value[:, : HD // 2]], axis=1)
            return (value * cos_part + swapped * sin_part).astype(jnp.bfloat16)

        value = dot_plain(rows_low, weight_parts[2][...])
        for head in range(4):
            packed[head, tile, 3 * HD :] = value[:, head * HD : (head + 1) * HD].astype(jnp.bfloat16)
        key = dot_plain(rows_low, weight_parts[1][...])
        for head in range(4):
            packed[head, tile, 2 * HD : 3 * HD] = turned(key[:, head * HD : (head + 1) * HD])
        query = dot_plain(rows_low, weight_parts[0][...])
        for head in range(4):
            first = 2 * head * HD
            packed[head, tile, :HD] = turned(query[:, first : first + HD])
            packed[head, tile, HD : 2 * HD] = turned(query[:, first + HD : first + 2 * HD])
        for d in (1, 2, 3):
            packed_copies.append(
                (
                    d,
                    tile,
                    send(packed.at[partner(place, d), tile], packed_in.at[d - 1, tile], peers[d - 1]),
                )
            )
    gate_load = load(w_gate_far, w_gate)
    outs = [load(normed_one, normed_one_out)]

    def unpack(source, block):
        here = pl.ds(pl.multiple_of(block * rows, rows), rows)
        heads[0, here, :HD] = source[:, :HD]
        heads[1, here, :HD] = source[:, HD : 2 * HD]
        keys[here, :HD] = source[:, 2 * HD : 3 * HD]
        values[here, :HD] = source[:, 3 * HD :]

    unpack(packed.at[place], place)
    beside_copy.wait()
    cotangent_copy = send(cotangent_x.at[half], cotangent_x.at[half], across)
    for d, tile, copy in packed_copies:
        copy.wait()
    for d in (1, 2, 3):
        unpack(packed_in.at[d - 1], partner(place, d))
    outs += [load(heads, heads_out), load(keys, keys_out), load(values, values_out)]

    shard_near = send(normed_one.at[half], shards.at[0, half], peers[0])
    shard_far = [send(normed_one.at[first_quarter], shards.at[1, first_quarter], peers[1])]

    ends = [ends_ref[index] for index in range(4)]
    scale = HD ** (-0.5) * LOG2E

    def attend(first, key_tiles):
        tile = pl.ds(first, QUERY_TILE)
        queries = jnp.concatenate([heads[0, tile, :], heads[1, tile, :]], axis=0)
        row_ids = lax.broadcasted_iota(jnp.int32, (2 * QUERY_TILE, 1), 0) % QUERY_TILE + first
        doc_starts = doc_start(ends, row_ids)

        def key_step(key_index, state):
            row_max, row_sum, summed = state
            first_key = pl.multiple_of(key_index * KEY_TILE, KEY_TILE)
            key_rows = pl.ds(first_key, KEY_TILE)
            scores = scale * times_transpose(queries, keys[key_rows, :])
            key_ids = lax.broadcasted_iota(jnp.int32, (1, KEY_TILE), 1) + first_key
            scores = jnp.where((key_ids >= doc_starts) & (key_ids <= row_ids), scores, masked_score)
            new_max = jnp.maximum(row_max, jnp.max(scores, axis=1, keepdims=True))
            probs = jnp.exp2(scores - new_max)
            shrink = jnp.exp2(row_max - new_max)
            row_sum = row_sum * shrink + jnp.sum(probs, axis=1, keepdims=True)
            summed = summed * shrink + dot_plain(probs.astype(jnp.bfloat16), values[key_rows, :])
            return (new_max, row_sum, summed)

        row_max, row_sum, summed = lax.fori_loop(
            0,
            key_tiles,
            key_step,
            (
                jnp.full((2 * QUERY_TILE, 1), masked_score, jnp.float32),
                jnp.zeros((2 * QUERY_TILE, 1), jnp.float32),
                jnp.zeros((2 * QUERY_TILE, PAD), jnp.float32),
            ),
        )
        attended = jnp.where(row_ids < ends[-1], summed / row_sum, 0.0)
        total_log = row_max + jnp.log(row_sum) * LOG2E
        total_row = jnp.transpose(jnp.broadcast_to(total_log, (2 * QUERY_TILE, PAD)))[:1, :]
        return attended, total_row

    def attend_block(step, nothing):
        distance = 3 - step
        one, two = distance % 2, distance // 2
        flipped = place + one * (1 - 2 * (place % 2))
        block = flipped + two * (2 - 4 * (flipped // 2))

        slot = step % 2

        def attend_tile(index, nothing):
            first = pl.multiple_of(block * rows + index * QUERY_TILE, QUERY_TILE)
            attended, total_row = attend(first, block + 1)
            tile = pl.ds(first, QUERY_TILE)
            inner = pl.ds(pl.multiple_of(index * QUERY_TILE, QUERY_TILE), QUERY_TILE)
            for head in range(2):
                mine = attended[head * QUERY_TILE : (head + 1) * QUERY_TILE]
                exact[slot, head, inner, :] = mine
                low[distance, inner, head * HD : (head + 1) * HD] = mine[:, :HD].astype(
                    jnp.bfloat16
                )
                lse[head : head + 1, tile] = total_row[
                    :, head * QUERY_TILE : (head + 1) * QUERY_TILE
                ]
            return nothing

        lax.fori_loop(0, rows // QUERY_TILE, attend_tile, nothing)
        return block

    low_copies, exact_copies = {}, []
    for step in range(4):
        if step > 1:
            exact_copies[step - 2].wait()
        block = attend_block(step, 0)
        exact_rows = pl.ds(pl.multiple_of(block * rows, rows), rows)
        exact_copies.append(load(exact.at[step % 2], exact_out.at[:, exact_rows]))
        distance = 3 - step
        if distance:
            low_copies[distance] = send(
                low.at[distance], low_in.at[place], peers[distance - 1]
            )
    outs += exact_copies[2:]
    low_in[place] = low[0]
    for distance in (3, 2, 1):
        low_copies[distance].wait()
    shard_far.append(send(normed_one.at[second_quarter], shards.at[1, second_quarter], peers[1]))
    shard_far[0].wait()
    shard_both = [send(shards.at[1, first_quarter], shards.at[2, first_quarter], peers[0])]
    shard_near.wait()
    late.append(send(shards.at[0, half], shards.at[0, half], across))

    for head in range(4):
        merged[:, 2 * head * HD : 2 * (head + 1) * HD] = low_in[head]
    wait_all(other_loads)
    part_copies = []
    for tile in tiles:
        part[tile, :] = dot_plain(merged[tile, :], w_out[...]).astype(jnp.bfloat16)
        part_copies.append(send(part.at[tile], other.at[tile], across))

    def middle_rows(tile):
        return x[tile, :].astype(jnp.float32) + (
            part[tile, :].astype(jnp.float32) + other[tile, :].astype(jnp.float32)
        )

    for tile, copy in zip(tiles, part_copies, strict=True):
        copy.wait()
        middle = middle_rows(tile)
        normed[tile, :] = (middle * norm_scale(middle) * gain_two[...]).astype(jnp.bfloat16)
    normed_copies = [
        send(normed.at[half], normed_x.at[half], over_x),
        send(normed.at[half], normed_y.at[half], over_y),
    ]
    outs += [load(normed, normed_out), load(merged, merged_out)]
    cotangent_load.wait()
    gate_load.wait()

    unit_tile = units // 4

    def unit_step(index, nothing):
        columns = pl.ds(pl.multiple_of(index * unit_tile, unit_tile), unit_tile)
        inner = pl.ds(pl.multiple_of((index % 2) * unit_tile, unit_tile), unit_tile)
        rows_low = normed[...]
        gate, up = dot_plain(rows_low, w_gate[:, columns]), dot_plain(rows_low, w_up[:, columns])
        back = times_transpose(cotangent[...], w_down[columns, :])
        sigma = jax.nn.sigmoid(gate)
        swish = gate * sigma
        hidden[index // 2, :, inner] = (swish * up).astype(jnp.bfloat16)
        grad_gate[index] = (back * up * sigma * (1.0 + gate * (1.0 - sigma))).astype(jnp.bfloat16)
        grad_up[index // 2, :, inner] = (back * swish).astype(jnp.bfloat16)
        return nothing

    lax.fori_loop(0, 4, unit_step, 0)
    unit_copies = [
        send(hidden.at[1 - along_x], hidden_x, over_x),
        send(grad_up.at[1 - along_y], up_y, over_y),
    ]
    outs += [load(hidden, hidden_out), load(grad_gate, grad_gate_out), load(grad_up, grad_up_out)]

    width_tile = width // 3
    grad_copies = []
    for index in range(3):
        columns = pl.ds(index * width_tile, width_tile)
        total = None
        for quarter in range(4):
            inner = pl.ds(quarter * unit_tile, unit_tile)
            term = times_transpose(grad_gate[quarter], w_gate[columns, inner])
            total = term if total is None else total + term
        for side in range(2):
            inner = pl.ds(side * 2 * unit_tile, 2 * unit_tile)
            total = total + times_transpose(grad_up[side], w_up[columns, inner])
        grad_part[:, columns] = total.astype(jnp.bfloat16)
        grad_copies.append(send(grad_part.at[:, columns], grad_other.at[:, columns], across))
    shard_far[1].wait()
    late.append(send(shards.at[1, half], shards.at[1, half], across))
    shard_both.append(send(shards.at[1, second_quarter], shards.at[2, second_quarter], peers[0]))
    wait_all(grad_copies)

    for block, tile in enumerate(tiles):
        middle = middle_rows(tile)
        inverse = norm_scale(middle)
        unit_rows = middle * inverse
        grad_normed = grad_part[tile, :].astype(jnp.float32) + grad_other[tile, :].astype(
            jnp.float32
        )
        gain_term = jnp.sum(grad_normed * unit_rows, axis=0, keepdims=True)
        gain_sum[...] = gain_term if block == 0 else gain_sum[...] + gain_term
        scaled = grad_normed * gain_two[...]
        total = cotangent[tile, :].astype(jnp.float32) + inverse * (
            scaled - unit_rows * jnp.mean(scaled * unit_rows, axis=-1, keepdims=True)
        )
        if block:
            outs.pop().wait()
        grad_middle[...] = total
        outs.append(load(grad_middle, grad_middle_out.at[tile]))
        rows_low = total.astype(jnp.bfloat16)
        grad_part[tile, :] = rows_low
        row_ids = lax.broadcasted_iota(jnp.int32, (ROW_TILE, 1), 0) + (
            place * rows + block * ROW_TILE
        )
        back = jnp.where(row_ids < ends[3], times_transpose(rows_low, w_out[...]), 0.0)
        for head in range(4):
            low[head, tile, :] = back[:, 2 * head * HD : 2 * (head + 1) * HD].astype(jnp.bfloat16)
    pl.semaphore_signal(free_sem, inc=1, device_id=across, device_id_type=pl.DeviceIdType.MESH)
    back_copies = [
        send(low.at[partner(place, d)], out, peers[d - 1])
        for d, out in ((1, back_1), (2, back_2), (3, back_3))
    ]
    outs += [
        load(low.at[place], back_0),
        load(grad_part, grad_low_out),
    ]

    outs[0].wait()
    down_copies = []
    for index in range(3):
        columns = pl.ds(index * width_tile, width_tile)
        total = dot_plain(hidden[0], w_down[: units // 2, columns]) + dot_plain(
            hidden[1], w_down[units // 2 :, columns]
        )
        normed_one[:, columns] = total.astype(jnp.bfloat16)
        if index == 0:
            pl.semaphore_wait(free_sem, 1)
        down_copies.append(send(normed_one.at[:, columns], grad_other.at[:, columns], across))

    wait_all(normed_copies)
    late.append(send(normed_x.at[half], normed_x.at[half], across))
    normed_copy = send(normed_y.at[half], normed_y.at[half], across)
    wait_all(unit_copies)
    cotangent_copy.wait()
    normed_copy.wait()
    cotangent_slot, normed_slot = w_gate.at[pl.ds(0, rows), pl.ds(0, width)], w_gate.at[
        pl.ds(rows, rows), pl.ds(0, width)
    ]
    hidden_slot, up_slot = w_up.at[pl.ds(0, rows), pl.ds(0, units // 2)], w_up.at[
        pl.ds(rows, rows), pl.ds(0, units // 2)
    ]
    slot_loads = [
        load(cotangent_x, cotangent_slot),
        load(hidden_x, hidden_slot),
        load(normed_y, normed_slot),
        load(up_y, up_slot),
    ]
    wait_all(down_copies)
    for tile in tiles:
        x[tile, :] = (
            middle_rows(tile)
            + (normed_one[tile, :].astype(jnp.float32) + grad_other[tile, :].astype(jnp.float32))
        ).astype(jnp.bfloat16)
    outs.append(load(x, result))
    wait_all(shard_both)
    late.append(send(shards.at[2, half], shards.at[2, half], across))
    wait_all(slot_loads)
    block_rows = width // 4

    def away(slot, lefts, rights, block, target):
        columns = pl.ds(pl.multiple_of(block * block_rows, block_rows), block_rows)
        total = outer_sum(lefts[0][:, columns], rights[0][...]) + outer_sum(
            lefts[1][:, columns], rights[1][...]
        )
        place_rows = w_down.at[pl.ds(slot * block_rows, block_rows), pl.ds(0, units // 2)]
        place_rows[...] = total.astype(jnp.bfloat16)
        return load(place_rows, target)

    down_sides = ((cotangent, cotangent_slot), (hidden.at[along_x], hidden_slot))
    up_sides = ((normed, normed_slot), (grad_up.at[along_y], up_slot))
    for index in range(2):
        outs.append(
            away(index, *down_sides, 2 * (1 - along_y) + index, down_away.at[index])
        )
        outs.append(
            away(2 + index, *up_sides, 2 * index + 1 - along_x, up_away.at[index])
        )
    wait_all(back_copies)
    wait_all(late)
    wait_all(outs[1:])


def forward(ends, x, gains, cotangent, tables, weights):
    rows, width = x.shape
    w_query, w_key, w_value, w_out, w_gate, w_up, w_down = weights
    units = w_gate.shape[1]
    total = 4 * rows
    f32 = jnp.float32
    wide, message = shape_of(rows, width), shape_of(rows, 2 * HD)
    by_half, by_quarter = shape_of(2, rows, units // 2), shape_of(4, rows, units // 4)
    block = shape_of(2, width // 4, units // 2)
    vmem_outs = (shape_of(2, total, dtype=f32), shape_of(1, width, dtype=f32))
    far_outs = (
        shape_of(2, total, PAD),
        shape_of(total, PAD),
        shape_of(total, PAD),
        shape_of(2, total, PAD, dtype=f32),
        wide,
        wide,
        shape_of(3, rows, width),
        wide,
        wide,
        wide,
        by_half,
        by_quarter,
        by_half,
        shape_of(rows, units // 2),
        shape_of(rows, units // 2),
        shape_of(rows, w_out.shape[0]),
        wide,
        shape_of(rows, width, dtype=f32),
        block,
        block,
        *(message,) * 4,
        wide,
    )

    def low(*dims):
        return pltpu.VMEM(dims, jnp.bfloat16)

    scratch = [
        low(*w_out.shape),
        low(*w_gate.shape),
        low(*w_up.shape),
        low(*w_down.shape),
        low(rows, width),
        low(rows, width),
        pltpu.VMEM((rows, PAD), f32),
        pltpu.VMEM((rows, PAD), f32),
        low(rows, width),
        low(4, rows, 4 * HD),
        low(3, rows, 4 * HD),
        low(2, total, PAD),
        low(total, PAD),
        low(total, PAD),
        pltpu.VMEM((2, 2, rows, PAD), f32),
        low(4, rows, 2 * HD),
        low(4, rows, 2 * HD),
        low(rows, w_out.shape[0]),
        low(rows, width),
        low(rows, width),
        low(rows, width),
        low(*by_half.shape),
        low(*by_quarter.shape),
        low(*by_half.shape),
        low(rows, width),
        low(rows, width),
        pltpu.VMEM((ROW_TILE, width), f32),
        pltpu.SemaphoreType.REGULAR,
        pltpu.SemaphoreType.DMA((40,)),
        pltpu.SemaphoreType.DMA((44,)),
        pltpu.SemaphoreType.DMA((44,)),
    ]
    return pl.pallas_call(
        forward_kernel,
        out_shape=vmem_outs + far_outs,
        in_specs=[pl.BlockSpec(memory_space=pltpu.SMEM), IN_ANY]
        + [IN_VMEM] * 2
        + [IN_ANY] * 10,
        out_specs=(IN_VMEM,) * len(vmem_outs) + (IN_ANY,) * len(far_outs),
        scratch_shapes=scratch,
        compiler_params=pltpu.CompilerParams(
            collective_id=0, has_side_effects=True, vmem_limit_bytes=63 * MEBI
        ),
        cost_estimate=pl.CostEstimate(
            flops=16 * rows * width * units, bytes_accessed=64 * MEBI, transcendentals=0
        ),
        name="forward",
    )(ends, x, *gains, cotangent, *tables, *weights)


def backward_kernel(
    ends_ref,
    lse,
    gain,
    mlp_gain_sum,
    grad_0,
    grad_1,
    grad_2,
    grad_3,
    heads_far,
    keys_far,
    values_far,
    exact_far,
    cosine_far,
    sine_far,
    merged_far,
    grad_low_far,
    cotangent,
    cotangent_x,
    normed,
    normed_x,
    normed_y,
    hidden,
    hidden_x,
    grad_up,
    up_y,
    grad_gate,
    down_away,
    up_away,
    normed_one,
    shards,
    w_query,
    w_key,
    w_value,
    x_far,
    grad_middle_far,
    grad_down,
    grad_gate_x,
    grad_gate_y,
    grad_up_rows,
    grad_out,
    grad_query,
    grad_key,
    grad_value,
    gains,
    grad_input,
    heads,
    keys,
    values,
    exact,
    cosine,
    sine,
    grad_heads,
    key_sum,
    value_sum,
    query_backs,
    value_backs,
    query_sorted,
    value_sorted,
    merged,
    grad_low,
    cotangents,
    normeds,
    hiddens,
    ups,
    gate_xs,
    gate_ys,
    inputs,
    grad_middle,
    key,
    value,
    other,
    out_away,
    out_stay,
    gate_x_away,
    gate_y_away,
    head_away,
    head_stay,
    down_1,
    up_1,
    gate_x_1,
    gate_y_1,
    out_1,
    head_1,
    down_2,
    up_2,
    gate_x_2,
    gate_y_2,
    out_2,
    head_2,
    down_3,
    up_3,
    gate_x_3,
    gate_y_3,
    out_3,
    head_3,
    down_4,
    up_4,
    gate_x_4,
    gate_y_4,
    out_4,
    head_rows,
    gain_0,
    gain_1,
    gain_2,
    gain_3,
    load_sem,
    send_sem,
    recv_sem,
):
    dp_index, place, core = (lax.axis_index(name) for name in ("dp", "seq", "tensor"))
    along_x, along_y = dp_index % 2, dp_index // 2
    rows, width = x_far.shape
    block_rows, width_each = width // 4, width // 16
    near, far = place % 2, place // 2
    peers = [{"seq": partner(place, d)} for d in (1, 2, 3)]
    over_x, over_y = {"dp": partner(dp_index, 1)}, {"dp": partner(dp_index, 2)}
    across = {"tensor": 1 - core}
    copies = Copies(load_sem, send_sem, recv_sem)
    send, load = copies.send, copies.load

    def rows_of(block):
        return pl.ds(pl.multiple_of(block * rows, rows), rows)

    greet([*peers, over_x, over_y, across])
    down_copy = send(down_away, down_1, over_y)
    up_copy = send(up_away, up_1, over_x)
    for_heads = [load(heads_far, heads), load(keys_far, keys), load(values_far, values)]
    for_heads += [load(exact_far, exact), load(cosine_far, cosine), load(sine_far, sine)]
    first, second, third = (pl.ds(index * rows, rows) for index in range(3))
    for_out = [load(merged_far, merged), load(grad_low_far, grad_low)]
    for_head = [load(normed_one, inputs.at[0])] + [
        load(shards.at[d], inputs.at[d + 1]) for d in range(3)
    ]
    kept_columns = pl.ds(pl.multiple_of(along_y * 2 * block_rows, block_rows), 2 * block_rows)
    for_down = [
        load(cotangent.at[:, kept_columns], cotangents.at[first]),
        load(cotangent_x.at[:, kept_columns], cotangents.at[second]),
        load(hidden.at[along_x], hiddens.at[0]),
        load(hidden_x, hiddens.at[1]),
    ]
    for_gates = [
        load(normed, normeds.at[first]),
        load(normed_x, normeds.at[second]),
        load(normed_y, normeds.at[third]),
        load(grad_gate.at[along_x], gate_xs.at[0]),
        load(grad_gate.at[2 + along_y], gate_ys.at[0]),
    ]
    for_up = [load(grad_up.at[along_y], ups.at[0]), load(up_y, ups.at[1])]

    def outer(pairs, block):
        columns = pl.ds(pl.multiple_of(block * block_rows, block_rows), block_rows)
        total = None
        for left, right in pairs:
            term = outer_sum(left[:, columns], right())
            total = term if total is None else total + term
        return total

    down_pairs = [
        (cotangents.at[first], lambda: hiddens[0]),
        (cotangents.at[second], lambda: hiddens[1]),
    ]
    up_pairs = [(normeds.at[first], lambda: ups[0]), (normeds.at[third], lambda: ups[1])]
    gate_x_pairs = [
        (normeds.at[first], lambda: gate_xs[0]),
        (normeds.at[second], lambda: gate_xs[1]),
    ]
    gate_y_pairs = [
        (normeds.at[first], lambda: gate_ys[0]),
        (normeds.at[third], lambda: gate_ys[1]),
    ]
    out_pairs = [(grad_low, lambda: merged[...])]
    query_pairs = [(inputs.at[d], lambda d=d: query_backs[d]) for d in range(4)]
    value_pairs = [(inputs.at[d], lambda d=d: value_backs[d]) for d in range(4)]

    def block_along_y(side, index):
        return 2 * side + index

    def block_along_x(side, index):
        return 2 * index + side

    def fill(target, pairs, block_of, side):
        for index in range(2):
            target[index] = outer(pairs, block_of(side, index)).astype(jnp.bfloat16)

    def add_outer(landed, pairs, block_of, side):
        for index in range(2):
            landed[index] = (
                landed[index].astype(jnp.float32) + outer(pairs, block_of(side, index))
            ).astype(jnp.bfloat16)

    def add(target, term):
        target[...] = (target[...].astype(jnp.float32) + term.astype(jnp.float32)).astype(
            jnp.bfloat16
        )

    def by_place(ref, blocks):
        return ref.reshape(blocks, 2, 2, width_each, ref.shape[-1])

    def start_near(slots, landed):
        return send(slots.at[:, :, 1 - near], landed, peers[0])

    def start_far(slots, landed, last, started):
        started.wait()
        for index in range(slots.shape[0]):
            for side in range(2):
                landed[index, side] = (
                    landed[index, side].astype(jnp.float32)
                    + slots[index, side, near].astype(jnp.float32)
                ).astype(jnp.bfloat16)
        return send(landed.at[:, 1 - far], last, peers[1])

    def add_far(landed, last, copy):
        copy.wait()
        for index in range(last.shape[0]):
            last[index] = (
                last[index].astype(jnp.float32) + landed[index, far].astype(jnp.float32)
            ).astype(jnp.bfloat16)

    ends = [ends_ref[index] for index in range(4)]
    scale = HD ** (-0.5) * LOG2E
    grad_heads[...] = jnp.zeros_like(grad_heads)
    key_sum[...] = jnp.zeros_like(key_sum)
    value_sum[...] = jnp.zeros_like(value_sum)
    for step, grad in enumerate((grad_0, grad_1, grad_2, grad_3)):
        here = rows_of(partner(place, step))
        grad_heads[0, here, :HD] = grad[:, :HD]
        grad_heads[1, here, :HD] = grad[:, HD:]
    wait_all(for_heads)

    def turned_back(value, cos_part, sin_part):
        swapped = jnp.concatenate([value[:, HD // 2 :], value[:, : HD // 2]], axis=1)
        return ((value * cos_part - swapped * sin_part) * HD ** (-0.5)).astype(jnp.bfloat16)

    def block_at(distance):
        one, two = distance % 2, distance // 2
        flipped = place + one * (1 - 2 * (place % 2))
        return flipped + two * (2 - 4 * (flipped // 2))

    def attend_block(distance):
        block = block_at(distance)

        def attend_tile(index, nothing):
            start = pl.multiple_of(block * rows + index * QUERY_TILE, QUERY_TILE)
            tile = pl.ds(start, QUERY_TILE)
            inner = pl.ds(pl.multiple_of(index * QUERY_TILE, QUERY_TILE), QUERY_TILE)
            queries = jnp.concatenate([heads[0, tile, :], heads[1, tile, :]], axis=0)
            grad_rows = jnp.concatenate([grad_heads[0, tile, :], grad_heads[1, tile, :]], axis=0)
            exact_rows = jnp.concatenate([exact[0, tile, :], exact[1, tile, :]], axis=0)
            delta = jnp.sum(
                jnp.transpose(grad_rows.astype(jnp.float32) * exact_rows), axis=0, keepdims=True
            )
            log_row = jnp.concatenate([lse[0:1, tile], lse[1:2, tile]], axis=1)
            row_ids = lax.broadcasted_iota(jnp.int32, (1, 2 * QUERY_TILE), 1) % QUERY_TILE + start
            doc_starts = doc_start(ends, row_ids)

            def key_step(key_index, summed):
                first_key = pl.multiple_of(key_index * KEY_TILE, KEY_TILE)
                key_rows = pl.ds(first_key, KEY_TILE)
                key_part, value_part = keys[key_rows, :], values[key_rows, :]
                scores = scale * times_transpose(key_part, queries)
                key_ids = lax.broadcasted_iota(jnp.int32, (KEY_TILE, 1), 0) + first_key
                probs = jnp.where(
                    (key_ids >= doc_starts) & (key_ids <= row_ids), jnp.exp2(scores - log_row), 0.0
                )
                grad_scores = (probs * (times_transpose(value_part, grad_rows) - delta)).astype(
                    jnp.bfloat16
                )
                value_sum[key_rows, :] += dot_plain(probs.astype(jnp.bfloat16), grad_rows)
                key_sum[key_rows, :] += dot_plain(grad_scores, queries)
                return summed + outer_sum(grad_scores, key_part)

            summed = lax.fori_loop(
                0, block + 1, key_step, jnp.zeros((2 * QUERY_TILE, PAD), jnp.float32)
            )
            table = cosine[tile, :HD], sine[tile, :HD]
            for head in range(2):
                mine = summed[head * QUERY_TILE : (head + 1) * QUERY_TILE, :HD]
                query_backs[distance, inner, head * HD : (head + 1) * HD] = turned_back(mine, *table)
            return nothing

        lax.fori_loop(0, rows // QUERY_TILE, attend_tile, 0)

    back_sends = copies.sends
    copies.sends += 6

    def back_copy(source, target, first, distance):
        index = back_sends + first + distance - 1
        return pltpu.make_async_remote_copy(
            src_ref=source.at[distance],
            dst_ref=target.at[place],
            send_sem=send_sem.at[index],
            recv_sem=recv_sem.at[index],
            device_id={"seq": block_at(distance)},
            device_id_type=pl.DeviceIdType.MESH,
        )

    def attend_and_send(step, nothing):
        attend_block(3 - step)
        back_copy(query_backs, query_sorted, 0, 3 - step).start()
        return nothing

    lax.fori_loop(0, 3, attend_and_send, 0)
    attend_block(0)

    def finish_keys(distance):
        here = rows_of(block_at(distance))
        value_backs[distance, :, :HD] = turned_back(
            key_sum[here, :HD], cosine[here, :HD], sine[here, :HD]
        )
        value_backs[distance, :, HD:] = value_sum[here, :HD].astype(jnp.bfloat16)

    def finish_and_send(step, nothing):
        finish_keys(3 - step)
        back_copy(value_backs, value_sorted, 3, 3 - step).start()
        return nothing

    lax.fori_loop(0, 3, finish_and_send, 0)
    finish_keys(0)
    gate_copies = [
        send(grad_gate.at[1 - along_x], gate_xs.at[1], over_x),
        send(grad_gate.at[3 - along_y], gate_ys.at[1], over_y),
    ]
    query_sorted[place] = query_backs[0]
    value_sorted[place] = value_backs[0]

    wait_all(for_head)
    for target, side in ((head_away, 1 - along_x), (head_stay, along_x)):
        for lanes, pairs in ((slice(0, 2 * HD), query_pairs), (slice(2 * HD, 4 * HD), value_pairs)):
            for index in range(2):
                target[index, :, lanes] = outer(pairs, block_along_x(side, index)).astype(
                    jnp.bfloat16
                )
    wait_all(for_down)
    down_copy.wait()
    add_outer(down_1, down_pairs, block_along_y, 0)
    down_slots = by_place(down_1, 2)
    down_copies = start_near(down_slots, down_2)
    wait_all(for_up)
    wait_all(for_gates)
    up_copy.wait()
    add_outer(up_1, up_pairs, block_along_x, along_x)
    up_slots = by_place(up_1, 2)
    up_copies = start_near(up_slots, up_2)
    wait_all(gate_copies)
    fill(gate_x_away, gate_x_pairs, block_along_y, 1 - along_y)
    gate_x_copy = send(gate_x_away, gate_x_1, over_y)
    fill(gate_y_away, gate_y_pairs, block_along_x, 1 - along_x)
    gate_y_copy = send(gate_y_away, gate_y_1, over_x)
    wait_all(for_out)
    fill(out_away, out_pairs, block_along_y, 1 - along_y)
    fill(out_stay, out_pairs, block_along_y, along_y)

    columns = [w.shape[1] for w in (w_query, w_key, w_value)]
    starts = [0, columns[0], columns[0] + columns[1]]
    weight_loads = [
        load(w.at[pl.ds(index * rows, rows)], inputs.at[index, :, pl.ds(start, size)])
        for w, start, size in zip((w_query, w_key, w_value), starts, columns, strict=True)
        for index in range(3)
    ]
    x = inputs.at[3]
    x_load = load(x_far, x)
    query, part = merged, grad_low
    for distance in (1, 2, 3):
        back_copy(query_backs, query_sorted, 0, distance).wait()
        back_copy(value_backs, value_sorted, 3, distance).wait()
    for head in range(4):
        query[:, 2 * head * HD : 2 * (head + 1) * HD] = query_sorted[head]
        key[:, head * HD : (head + 1) * HD] = value_sorted[head, :, :HD]
        value[:, head * HD : (head + 1) * HD] = value_sorted[head, :, HD:]
    wait_all(weight_loads)
    part_copies = []
    for third_index in range(3):
        total = None
        for ref, start, size in zip((query, key, value), starts, columns, strict=True):
            term = times_transpose(ref[...], inputs[third_index, :, start : start + size])
            total = term if total is None else total + term
        lanes = pl.ds(third_index * rows, rows)
        part[:, lanes] = total.astype(jnp.bfloat16)
        part_copies.append(send(part.at[:, lanes], other.at[:, lanes], across))

    gate_x_copy.wait()
    add_outer(gate_x_1, gate_x_pairs, block_along_y, along_y)
    gate_x_slots = by_place(gate_x_1, 2)
    gate_x_copies = start_near(gate_x_slots, gate_x_2)
    gate_y_copy.wait()
    add_outer(gate_y_1, gate_y_pairs, block_along_x, along_x)
    gate_y_slots = by_place(gate_y_1, 2)
    gate_y_copies = start_near(gate_y_slots, gate_y_2)
    head_copy = send(head_away, head_1, over_x)
    out_copy = send(out_away, out_1, over_y)

    x_load.wait()
    wait_all(part_copies)
    tiles = [pl.ds(block * (rows // 4), rows // 4) for block in range(4)]
    for block, tile in enumerate(tiles):
        load(grad_middle_far.at[tile], grad_middle).wait()
        tokens = x[tile, :].astype(jnp.float32)
        inverse = norm_scale(tokens)
        unit_rows = tokens * inverse
        grad_normed = part[tile, :].astype(jnp.float32) + other[tile, :].astype(jnp.float32)
        term = jnp.sum(grad_normed * unit_rows, axis=0, keepdims=True)
        gain_sum = term if block == 0 else gain_sum + term
        scaled = grad_normed * gain[...]
        x[tile, :] = (
            grad_middle[...]
            + inverse * (scaled - unit_rows * jnp.mean(scaled * unit_rows, axis=-1, keepdims=True))
        ).astype(jnp.bfloat16)
    input_copy = load(x, grad_input)
    gain_0[0:1, :] = gain_sum
    gain_0[1:2, :] = mlp_gain_sum[...]
    gain_copy = send(gain_0, gain_1, over_y)

    down_copy = start_far(down_slots, down_2, down_3, down_copies)
    up_copy = start_far(up_slots, up_2, up_3, up_copies)
    gain_copy.wait()
    gain_1[...] += gain_0[...]
    gain_copy = send(gain_1, gain_2, over_x)
    head_copy.wait()
    for index in range(2):
        add(head_1.at[index], head_stay[index])
    head_copy = send(head_1.at[1 - along_y], head_2, over_y)
    out_copy.wait()
    for index in range(2):
        add(out_1.at[index], out_stay[index])
    out_copy = send(out_1.at[1 - along_x], out_2, over_x)
    head_copy.wait()
    add(head_2, head_1[along_y])
    head_slots = head_2.reshape(4, width_each, head_2.shape[-1])
    head_copies = [
        send(head_slots.at[partner(place, d)], head_3.at[d - 1], peers[d - 1]) for d in (1, 2, 3)
    ]
    gate_x_copy = start_far(gate_x_slots, gate_x_2, gate_x_3, gate_x_copies)
    gate_y_copy = start_far(gate_y_slots, gate_y_2, gate_y_3, gate_y_copies)
    gain_copy.wait()
    gain_2[...] += gain_1[...]
    gain_copies = [send(gain_2, gain_3.at[d - 1], peers[d - 1]) for d in (1, 2, 3)]
    out_copy.wait()
    add(out_2, out_1[along_x])
    out_slots = by_place(out_2, 1)
    out_copies = start_near(out_slots, out_3)
    add_far(down_2, down_3, down_copy)
    down_copy = send(down_3.at[1 - along_x], down_4, over_x)
    add_far(up_2, up_3, up_copy)
    up_copy = send(up_3.at[1 - along_y], up_4, over_y)
    out_copy = start_far(out_slots, out_3, out_4, out_copies)
    wait_all(gain_copies)
    gains[...] = (gain_2[...] + gain_3[0]) + (gain_3[1] + gain_3[2])

    head_rows[place] = head_slots[place]
    for d, copy in enumerate(head_copies):
        copy.wait()
        head_rows[partner(place, d + 1)] = head_3[d]
    for head in range(4):
        mine = head_rows[head].astype(jnp.float32)
        grad_query[:, 2 * head * HD : 2 * (head + 1) * HD] = mine[:, : 2 * HD]
        grad_key[:, head * HD : (head + 1) * HD] = mine[:, 2 * HD : 3 * HD]
        grad_value[:, head * HD : (head + 1) * HD] = mine[:, 3 * HD :]

    def both_sides(ref, landed, here, target):
        target[here] = ref[here].astype(jnp.float32)
        target[1 - here] = landed[...].astype(jnp.float32)

    add_far(gate_x_2, gate_x_3, gate_x_copy)
    gate_x_copy = send(gate_x_3.at[1 - along_x], gate_x_4, over_x)
    add_far(gate_y_2, gate_y_3, gate_y_copy)
    gate_y_copy = send(gate_y_3.at[1 - along_y], gate_y_4, over_y)
    out_copy.wait()
    grad_out[...] = out_4[0].astype(jnp.float32) + out_3[0, far].astype(jnp.float32)
    down_copy.wait()
    both_sides(down_3, down_4, along_x, grad_down)
    up_copy.wait()
    both_sides(up_3, up_4, along_y, grad_up_rows)
    gate_x_copy.wait()
    both_sides(gate_x_3, gate_x_4, along_x, grad_gate_x)
    gate_y_copy.wait()
    both_sides(gate_y_3, gate_y_4, along_y, grad_gate_y)
    input_copy.wait()


def backward(ends, lse, gain, mlp_gain_sum, grads, far):
    rows = grads[0].shape[0]
    operands = list(far.values())
    width, query = far["w_query"].shape
    key, merged_width = far["w_key"].shape[1], far["merged"].shape[1]
    each, block_rows, total = width // 16, width // 4, 4 * rows
    half, quarter = far["hidden"].shape[2], far["grad_gate"].shape[2]
    f32 = jnp.float32
    outs = (
        shape_of(2, each, half, dtype=f32),
        shape_of(2, each, quarter, dtype=f32),
        shape_of(2, each, quarter, dtype=f32),
        shape_of(2, each, half, dtype=f32),
        shape_of(each, merged_width, dtype=f32),
        shape_of(each, query, dtype=f32),
        shape_of(each, key, dtype=f32),
        shape_of(each, key, dtype=f32),
        shape_of(2, width, dtype=f32),
        shape_of(rows, width),
    )

    def low(*dims):
        return pltpu.VMEM(dims, jnp.bfloat16)

    head = 4 * HD
    sizes = (half, half, quarter, quarter)
    scratch = [
        low(2, total, PAD),
        low(total, PAD),
        low(total, PAD),
        pltpu.VMEM((2, total, PAD), f32),
        pltpu.VMEM((total, PAD), f32),
        pltpu.VMEM((total, PAD), f32),
        low(2, total, PAD),
        pltpu.VMEM((total, PAD), f32),
        pltpu.VMEM((total, PAD), f32),
        *(low(4, rows, head // 2) for _ in range(4)),
        low(rows, merged_width),
        low(rows, width),
        low(2 * rows, width // 2),
        low(3 * rows, width),
        low(2, rows, half),
        low(2, rows, half),
        low(2, rows, quarter),
        low(2, rows, quarter),
        low(4, rows, width),
        pltpu.VMEM((rows // 4, width), f32),
        low(rows, key),
        low(rows, key),
        low(rows, width),
        low(2, block_rows, merged_width),
        low(2, block_rows, merged_width),
        low(2, block_rows, quarter),
        low(2, block_rows, quarter),
        low(2, block_rows, head),
        low(2, block_rows, head),
        *(low(2, block_rows, size) for size in (*sizes, merged_width, head)),
        *(low(2, 2, each, size) for size in sizes),
        low(block_rows, merged_width),
        low(block_rows, head),
        *(low(2, each, size) for size in sizes),
        low(1, 2, each, merged_width),
        low(3, each, head),
        *(low(each, size) for size in sizes),
        low(1, each, merged_width),
        low(4, each, head),
        *(pltpu.VMEM((2, width), f32) for _ in range(3)),
        pltpu.VMEM((3, 2, width), f32),
        pltpu.SemaphoreType.DMA((31,)),
        pltpu.SemaphoreType.DMA((41,)),
        pltpu.SemaphoreType.DMA((41,)),
    ]
    return pl.pallas_call(
        backward_kernel,
        out_shape=outs,
        in_specs=[pl.BlockSpec(memory_space=pltpu.SMEM)] + [IN_VMEM] * 7 + [IN_ANY] * len(operands),
        out_specs=(IN_VMEM,) * 9 + (IN_ANY,),
        scratch_shapes=scratch,
        compiler_params=pltpu.CompilerParams(
            collective_id=1, has_side_effects=True, vmem_limit_bytes=63 * MEBI
        ),
        cost_estimate=pl.CostEstimate(
            flops=8 * rows * width * 4 * half, bytes_accessed=64 * MEBI, transcendentals=0
        ),
        name="backward",
    )(ends, lse, gain, mlp_gain_sum, *grads, *operands)


def swap(array, axis, bit):
    return lax.ppermute(array, axis, [(i, i ^ bit) for i in range(lax.axis_size(axis))])


def local_paired(
    hidden_in,
    lengths,
    attn_gain,
    w_query,
    w_key,
    w_value,
    w_out,
    mlp_gain,
    w_gate,
    w_up,
    w_down,
    out_grad,
):
    rows, width = hidden_in.shape[1], hidden_in.shape[2]
    dp_index, place, core = (lax.axis_index(name) for name in ("dp", "seq", "tensor"))
    along_x, along_y = dp_index % 2, dp_index // 2
    total_rows = 4 * rows
    x, cotangent = hidden_in[0], out_grad[0]
    gain_one, gain_two = attn_gain[None], mlp_gain[None]
    info = jnp.concatenate(
        [jnp.cumsum(lengths[0]), jnp.stack([place, along_x, along_y, core])]
    ).astype(jnp.int32)

    def over_x(array):
        return swap(array, "dp", 1)

    def over_y(array):
        return swap(array, "dp", 2)

    _, _, offsets, _ = doc_layout(lengths[0], 0, total_rows)
    cosine, sine = rope_tables(offsets)
    cosine, sine = cosine[:, 0], sine[:, 0]
    spare = PAD - HD
    cosine = jnp.pad(jnp.concatenate([cosine, cosine], axis=1), ((0, 0), (0, spare)))
    sine = jnp.pad(jnp.concatenate([-sine, sine], axis=1), ((0, 0), (0, spare)))

    (
        lse,
        mlp_gain_part,
        heads,
        keys,
        values,
        exact,
        cotangent_x,
        attn_input,
        input_shards,
        mlp_input,
        mlp_x,
        mlp_y,
        hidden,
        grad_gate,
        grad_up,
        hidden_x,
        up_y,
        attn_heads,
        grad_low,
        grad_middle,
        down_away,
        up_away,
        *grad_dealt,
        result,
    ) = forward(
        info,
        x,
        (gain_one, gain_two),
        cotangent,
        (cosine, sine),
        (w_query, w_key, w_value, w_out, w_gate, w_up, w_down),
    )
    (
        grad_down,
        grad_gate_x,
        grad_gate_y,
        grad_up_rows,
        grad_out,
        grad_w_query,
        grad_w_key,
        grad_w_value,
        gains,
        grad_inputs,
    ) = backward(
        info,
        lse,
        gain_one,
        mlp_gain_part,
        grad_dealt,
        dict(
            heads=heads,
            keys=keys,
            values=values,
            exact=exact,
            cosine=cosine,
            sine=sine,
            merged=attn_heads,
            grad_low=grad_low,
            cotangent=cotangent,
            cotangent_x=cotangent_x,
            normed=mlp_input,
            normed_x=mlp_x,
            normed_y=mlp_y,
            hidden=hidden,
            hidden_x=hidden_x,
            grad_up=grad_up,
            up_y=up_y,
            grad_gate=grad_gate,
            down_away=down_away,
            up_away=up_away,
            normed_one=attn_input,
            shards=input_shards,
            w_query=w_query,
            w_key=w_key,
            w_value=w_value,
            x=x,
            grad_middle=grad_middle,
        ),
    )
    own_gains = lax.dynamic_slice_in_dim(
        gains, (4 * dp_index + place) * (width // 16), width // 16, 1
    )
    grad_w_gate = jnp.concatenate(
        [grad_gate_x[0], grad_gate_x[1], grad_gate_y[0], grad_gate_y[1]], axis=1
    )
    grad_w_up = jnp.concatenate([grad_up_rows[0], grad_up_rows[1]], axis=1)
    grad_w_down = jnp.swapaxes(grad_down, 1, 2).reshape(-1, width // 16)
    return (
        result[None],
        grad_inputs[None],
        own_gains[0],
        grad_w_query,
        grad_w_key,
        grad_w_value,
        grad_out.T,
        own_gains[1],
        grad_w_gate,
        grad_w_up,
        grad_w_down,
    )


def solution(mesh):
    in_specs = (
        P("dp", "seq", None),
        P("dp", None),
        P(),
        P(None, "tensor"),
        P(None, "tensor"),
        P(None, "tensor"),
        P("tensor", None),
        P(),
        P(None, "tensor"),
        P(None, "tensor"),
        P("tensor", None),
        P("dp", "seq", None),
    )
    out_specs = (
        P("dp", "seq", None),
        P("dp", "seq", None),
        P(("dp", "seq")),
        P(("dp", "seq"), "tensor"),
        P(("dp", "seq"), "tensor"),
        P(("dp", "seq"), "tensor"),
        P("tensor", ("dp", "seq")),
        P(("dp", "seq")),
        P(("dp", "seq"), "tensor"),
        P(("dp", "seq"), "tensor"),
        P("tensor", ("dp", "seq")),
    )
    body = local_paired if tuple(mesh.shape[name] for name in ("dp", "seq", "tensor")) == (4, 4, 2) else local
    return jax.shard_map(body, mesh=mesh, in_specs=in_specs, out_specs=out_specs, check_vma=False)
```
